128 devices in a mesh: seq: 64 (over z, x, y), head: 2 (over core).
Axes of the slice: x: 4, y: 4, z: 4, core: 2. Of those that a mesh axis runs over, the one named last changes fastest.
Arguments:
- queries: float32 [32768, 4096], P('seq', 'head'), may hold values from -6 to 6
- keys: float32 [32768, 4096], P('seq', 'head'), may hold values from -6 to 6
- values: float32 [32768, 4096], P('seq', 'head'), may hold values from -6 to 6
- log_decay: float32 [32, 32768], P('head', 'seq'), may hold values from -1 to 0, as said below
- level_weights: float32 [32, 16, 32768], P('head', None, 'seq'), may hold values from 0.25 to 2.5
- norm_gain: float32 [4096], P('head'), may hold values from 0.1 to 1.9
- out_weight: float32 [4096, 2048], P('head', 'seq'), may hold values from -0.09375 to 0.09375
Outputs:
- mixed: float32 [32768, 2048], P('seq', 'head')
The draws below stay inside these ranges and needn't reach their ends.
Inputs may be any that keep to these rules, and one draw needn't show every extreme that they name: `log_decay`: every entry is non-positive.
All inputs are finite; a program needn't handle non-finite values.
Results may differ from the reference program's by a relative error of at most 0.0003.
Values sent between devices are 32-bit elements; how exact they have to be, the bound alone decides.
No kernel may reach another device: no remote copies, remote signals or barrier semaphores. Data moves between devices by JAX's collectives and lax.ppermute only.
A program may use at most 192 MiB of HBM per device.

```python
import math
import jax
import jax.numpy as jnp
from jax import lax

D = 2048
HEAD_TOTAL = 32
DH = 128
TOK_DEV = 512
HD = 4096
SEQUENCE_TOKENS = 32768
TOK_BITS = 9
SEQ_BITS = 6
LEVELS = 16
N_SEQ = 64


def draw_log_decay(key, part):
    every_key_row = jax.random.split(jax.random.fold_in(key, 7), 5)
    share = 0.5
    fast_heads = jax.random.uniform(every_key_row[0], (HEAD_TOTAL,)) < share
    fast_rate = jnp.log(10.0) / jax.random.uniform(every_key_row[1], (HEAD_TOTAL,), minval=30.0, maxval=50.0)
    slow_rate = jnp.full((HEAD_TOTAL,), 0.3 * jnp.log(10.0) / SEQUENCE_TOKENS, jnp.float32)
    rate_head = jnp.where(fast_heads, fast_rate, slow_rate)
    factor = jnp.exp(jax.random.uniform(every_key_row[2], (HEAD_TOTAL, SEQUENCE_TOKENS), minval=jnp.log(0.5), maxval=jnp.log(2.0)))
    base_offset = -rate_head[:, None] * factor
    group_position = jax.random.randint(every_key_row[3], (HEAD_TOTAL, 2), 0, SEQUENCE_TOKENS)
    group_depth = jax.random.uniform(every_key_row[4], (HEAD_TOTAL, 2), minval=0.22, maxval=0.69)
    match_count = (jnp.arange(SEQUENCE_TOKENS, dtype=jnp.int32)[None, None, :] == group_position[:, :, None]).astype(jnp.float32)
    token_group = -jnp.sum(match_count * group_depth[:, :, None], axis=1)
    return jnp.clip(base_offset + token_group, -1.0, 0.0).astype(jnp.float32)


def block_scale(rng, dims, cuts, smallest, high):
    gain, own = 1.0, jax.random.fold_in(rng, 6)
    for position, blocks in cuts:
        heights = jnp.exp(jax.random.uniform(jax.random.fold_in(own, position), (blocks,), jnp.float32, smallest / len(cuts), high / len(cuts)))
        gain = gain * jnp.repeat(heights, dims[position] // blocks).reshape([-1 if axis == position else 1 for axis in range(len(dims))])
    return gain


def gaussian(key, shape, spread, bound, pieces=(), kind=jnp.bfloat16):
    drawn = jax.random.normal(key, shape, jnp.float32) * spread
    if len(pieces) > 0:
        drawn = block_scale(key, shape, pieces, -0.22, 0.18) * drawn
    return jnp.clip(drawn, min=-bound, max=bound).astype(kind)


def setup_inputs(seed: int = 0) -> dict:
    key_of = jax.random.split(jax.random.key(seed), 8)
    queries = gaussian(key_of[0], (SEQUENCE_TOKENS, HD), 1.0, 6.0, ((0, 64), (1, 2)), jnp.float32)
    keys = gaussian(key_of[1], (SEQUENCE_TOKENS, HD), 1.0, 6.0, ((0, 64), (1, 2)), jnp.float32)
    values = gaussian(key_of[2], (SEQUENCE_TOKENS, HD), 1.0, 6.0, ((0, 64), (1, 2)), jnp.float32)
    log_decay = draw_log_decay(jax.random.fold_in(key_of[7], 71), 0)
    level_weights = jnp.clip(jnp.exp(math.log(2.5) - 2.3025851 * jax.random.uniform(key_of[4], (HEAD_TOTAL, LEVELS, SEQUENCE_TOKENS), jnp.float32) ** block_scale(key_of[4], (HEAD_TOTAL, LEVELS, SEQUENCE_TOKENS), ((0, 2), (2, 64)), -0.2, 0.2)), 0.25, 2.5)
    norm_gain = jnp.clip(1.0 + 0.18 * jax.random.normal(key_of[5], (HD,), jnp.float32), 0.1, 1.9)
    out_weight = gaussian(key_of[6], (HD, D), HD ** -0.5, 0.09375, ((0, 2), (1, 64)), jnp.float32)
    return dict(queries=queries, keys=keys, values=values, log_decay=log_decay, level_weights=level_weights, norm_gain=norm_gain, out_weight=out_weight)


HIGH = lax.Precision.HIGHEST

def level_table(count, bits):
    positions = jnp.arange(count, dtype=jnp.int32)
    mixed_bits = positions[:, None] ^ positions[None, :]
    level_ids = jnp.zeros((count, count), jnp.int32)
    for level_bit in range(bits):
        level_ids = level_ids + (mixed_bits >> level_bit > 0).astype(jnp.int32)
    return level_ids

def reference(queries, keys, values, log_decay, level_weights, norm_gain, out_weight):
    spans = N_SEQ
    tok_count = TOK_DEV
    head_count = HEAD_TOTAL
    head_size = DH
    query_heads = queries.reshape(spans, tok_count, head_count, head_size) * head_size ** (-0.5)
    key_heads = keys.reshape(spans, tok_count, head_count, head_size)
    value_heads = values.reshape(spans, tok_count, head_count, head_size)
    decay_sum = jnp.cumsum(log_decay.reshape(head_count, spans, tok_count), axis=2)
    span_decay = decay_sum[:, :, -1]
    start_decay = jnp.concatenate([jnp.zeros((head_count, 1), jnp.float32), jnp.cumsum(span_decay, axis=1)[:, :-1]], axis=1)
    end_decay = start_decay + span_decay
    fade_weight = jnp.exp(span_decay[:, :, None] - decay_sum)
    span_states = jnp.einsum('cjhd,hcj,cjhe->chde', key_heads, fade_weight, value_heads, precision=HIGH)
    span_ids = jnp.arange(spans, dtype=jnp.int32)
    weight_list = []
    for level_bit in range(SEQ_BITS):
        upper_side = span_ids >> level_bit & 1 == 1
        sibling = span_ids[None, :] >> level_bit == (span_ids[:, None] >> level_bit) - 1
        chosen = upper_side[:, None] & sibling
        gap = jnp.where(chosen[None], start_decay[:, :, None] - end_decay[:, None, :], -jnp.inf)
        weight_list.append(jnp.exp(gap))
    far_mix = jnp.stack(weight_list, axis=0).transpose(2, 0, 1, 3)
    lam_all = level_weights.reshape(head_count, LEVELS, spans, tok_count).transpose(2, 0, 1, 3)
    decay_spans = decay_sum.transpose(1, 0, 2)
    onehot = (level_table(tok_count, TOK_BITS)[None] == jnp.arange(TOK_BITS + 1, dtype=jnp.int32)[:, None, None]).astype(jnp.float32)
    positions = jnp.arange(tok_count, dtype=jnp.int32)
    causal = positions[:, None] >= positions[None, :]

    def one_span(inputs):
        query_c, key_c, value_c, decay_c, lam_c, mix_c = inputs
        near = jnp.einsum('hli,lij->hij', lam_c[:, :TOK_BITS + 1, :], onehot, precision=HIGH)
        gap = jnp.where(causal[None], decay_c[:, :, None] - decay_c[:, None, :], -jnp.inf)
        scores = jnp.einsum('ihd,jhd->hij', query_c, key_c, precision=HIGH) * near * jnp.exp(gap)
        local_out = jnp.einsum('hij,jhd->ihd', scores, value_c, precision=HIGH)
        level_states = jnp.einsum('lhe,ehdf->hldf', mix_c, span_states, precision=HIGH)
        far_weight = lam_c[:, TOK_BITS + 1:, :] * jnp.exp(decay_c)[:, None, :]
        weighted = query_c[:, :, None, :] * far_weight.transpose(2, 0, 1)[:, :, :, None]
        far_out = jnp.einsum('ihld,hlde->ihe', weighted, level_states, precision=HIGH)
        total_out = local_out + far_out
        root_mean = jnp.sqrt(lax.optimization_barrier(jnp.mean(total_out * total_out, axis=-1, keepdims=True)) + 1e-06)
        return (total_out / root_mean).reshape(tok_count, head_count * head_size) * norm_gain
    normed = lax.map(one_span, (query_heads, key_heads, value_heads, decay_spans, lam_all, far_mix))
    normed = normed.reshape(spans * tok_count, head_count * head_size)
    return jnp.dot(normed, out_weight, precision=HIGH, preferred_element_type=jnp.float32)
```

```python
import functools

import jax
import jax.numpy as jnp
from jax import lax
from jax.experimental import pallas as pl
from jax.experimental.pallas import tpu as pltpu
from jax.sharding import PartitionSpec as P

HIGH = lax.Precision.HIGHEST
DH = 128
CHUNK = 128
ROWS = DH + 8
F32 = jnp.float32
BF16 = jnp.bfloat16
NT = (((1,), (1,)), ((), ()))
TN = (((0,), (0,)), ((), ()))
NN = (((1,), (0,)), ((), ()))
VMEM = pl.BlockSpec(memory_space=pltpu.VMEM)
SMEM = pl.BlockSpec(memory_space=pltpu.SMEM)


def params(mib=40):
    return pltpu.CompilerParams(vmem_limit_bytes=mib * 2**20)


def cost(flops, bytes_accessed):
    return pl.CostEstimate(flops=int(flops), bytes_accessed=int(bytes_accessed), transcendentals=0)


def split(x):
    hi = x.astype(BF16)
    return hi, (x - hi.astype(F32)).astype(BF16)


def mm(a, b, dims):
    return lax.dot_general(a, b, dims, preferred_element_type=F32)


def mm3(a, b, dims):
    a_hi, a_lo = split(a)
    b_hi, b_lo = split(b)
    return mm(a_hi, b_hi, dims) + (mm(a_hi, b_lo, dims) + mm(a_lo, b_hi, dims))


def outer_sum(k, v):
    made = mm(jnp.concatenate(split(k), axis=1), jnp.concatenate(split(v), axis=1), TN)
    return made[:DH, :DH] + (made[:DH, DH:] + made[DH:, :DH])


def state_kernel(k_ref, v_ref, ld_ref, out_ref):
    heads, tok = ld_ref.shape
    ld = ld_ref[...]
    hi = ld.astype(BF16)
    rest = ld - hi.astype(F32)
    mid = rest.astype(BF16)
    low = (rest - mid.astype(F32)).astype(BF16)
    later = lax.broadcasted_iota(jnp.int32, (tok, tok), 1) > lax.broadcasted_iota(jnp.int32, (tok, tok), 0)
    later = jnp.where(later, 1.0, 0.0).astype(BF16)
    fade = jnp.exp(mm(later, hi, NT) + (mm(later, mid, NT) + mm(later, low, NT)))
    total = jnp.sum(ld, axis=1, keepdims=True)
    for h in range(heads):
        cols = pl.ds(h * DH, DH)
        out_ref[h, :DH, :] = outer_sum(k_ref[:, cols] * fade[:, h : h + 1], v_ref[:, cols])
        out_ref[h, DH:, :] = jnp.broadcast_to(total[h : h + 1, :], (ROWS - DH, DH))


def own_state(keys, values, log_decay):
    heads, tok = log_decay.shape
    width = heads * DH
    return pl.pallas_call(
        state_kernel,
        out_shape=jax.ShapeDtypeStruct((heads, ROWS, DH), F32),
        in_specs=[VMEM] * 3,
        out_specs=VMEM,
        compiler_params=params(),
        cost_estimate=cost(8 * tok * width * DH, 4 * (2 * tok * width)),
        name="own_state",
    )(keys, values, log_decay)


def merge_kernel(upper_ref, mine_ref, other_ref, out_ref):
    upper = upper_ref[0] == 1
    for h in range(mine_ref.shape[0]):
        mine, other = mine_ref[h], other_ref[h]
        low = jnp.where(upper, other, mine)
        high = jnp.where(upper, mine, other)
        faded = jnp.exp(high[DH : DH + 1, :])
        out_ref[h, :DH, :] = faded * low[:DH] + high[:DH]
        out_ref[h, DH:, :] = low[DH:] + high[DH:]


def merged(upper, mine, other):
    return pl.pallas_call(
        merge_kernel,
        out_shape=jax.ShapeDtypeStruct(mine.shape, F32),
        in_specs=[SMEM, VMEM, VMEM],
        out_specs=VMEM,
        compiler_params=params(16),
        cost_estimate=cost(3 * mine.size, 12 * mine.size),
        name="merge",
    )(upper, mine, other)


def near_kernel(q_ref, k_ref, v_ref, cum_ref, total_ref, w_ref, out_ref):
    heads, tok = cum_ref.shape[1:]
    chunks = tok // CHUNK
    tile_bits = CHUNK.bit_length() - 1
    row = lax.broadcasted_iota(jnp.int32, (CHUNK, CHUNK), 0)
    col = lax.broadcasted_iota(jnp.int32, (CHUNK, CHUNK), 1)
    apart = row ^ col
    causal = row >= col
    for h in range(heads):
        cols = pl.ds(h * DH, DH)
        cum = cum_ref[0, h : h + 1, :]
        weight_cols = jnp.transpose(w_ref[h])
        cum_cols = jnp.transpose(jnp.concatenate([cum] * 8, axis=0))
        states = []
        ends = []
        outs = []
        for m in range(chunks):
            rows = pl.ds(m * CHUNK, CHUNK)
            at = slice(m * CHUNK, (m + 1) * CHUNK)
            q = q_ref[rows, cols] * DH**-0.5
            k = k_ref[rows, cols]
            v = v_ref[rows, cols]
            w = weight_cols[at]
            c = cum_cols[at, 0:1]
            near = jnp.broadcast_to(w[:, 0:1], (CHUNK, CHUNK))
            for bit in range(tile_bits):
                near = jnp.where(apart >= 2**bit, w[:, bit + 1 : bit + 2], near)
            gap = jnp.where(causal, c - cum[:, at], -1e30)
            scores = mm3(q, k, NT) * (near * jnp.exp(gap))
            out = mm3(scores, v, NN)
            for bit in range(2):
                if m >> bit & 1:
                    first = (m >> bit) - 1 << bit
                    seen = states[first]
                    for n in range(first + 1, first + 2**bit):
                        seen = jnp.exp(ends[n]) * seen + states[n]
                    out = out + w[:, tile_bits + 1 + bit : tile_bits + 2 + bit] * mm3(q, seen, NN)
            outs.append(out)
            if m < chunks - 1:
                end = total_ref[h, m : m + 1, :]
                states.append(outer_sum(k * jnp.exp(end[:, 0:1] - c), v))
                ends.append(end)
        for m in range(chunks):
            out_ref[pl.ds(m * CHUNK, CHUNK), cols] = outs[m]


def near_part(queries, keys, values, cum, totals, weights, first, heads):
    tok = queries.shape[0]
    width = heads * DH
    chunks = totals.shape[1]
    wide = pl.BlockSpec((tok, width), lambda i: (0, first // heads))
    return pl.pallas_call(
        near_kernel,
        out_shape=jax.ShapeDtypeStruct((tok, width), F32),
        grid=(1,),
        in_specs=[
            wide,
            wide,
            wide,
            pl.BlockSpec((1, heads, tok), lambda i: (first // heads, 0, 0)),
            pl.BlockSpec((heads, chunks, DH), lambda i: (first // heads, 0, 0)),
            pl.BlockSpec((heads, weights.shape[1], tok), lambda i: (first // heads, 0, 0)),
        ],
        out_specs=pl.BlockSpec((tok, width), lambda i: (0, 0)),
        compiler_params=params(),
        cost_estimate=cost(60 * tok * width * DH, 16 * tok * width),
        name="near",
    )(queries, keys, values, cum.reshape(-1, heads, tok), totals, weights)


def far_kernel(upper_ref, q_ref, near_ref, w_ref, gain_ref, *refs):
    *state_refs, hi_ref, lo_ref = refs
    first = w_ref.shape[1] - len(state_refs)
    q_hi, q_lo = split(q_ref[...] * DH**-0.5)
    q_both = jnp.concatenate([q_hi, q_lo], axis=1)
    weight_cols = jnp.transpose(w_ref[0])
    out = near_ref[...]
    before = jnp.zeros((1, DH), F32)
    for level, ref in enumerate(state_refs):
        upper = upper_ref[level] == 1
        reach = jnp.where(upper, jnp.exp(before), 0.0)
        s_hi, s_lo = split(ref[0, :DH, :] * reach)
        before = before + jnp.where(upper, ref[0, DH : DH + 1, :], 0.0)
        made = mm(q_both, jnp.concatenate([s_hi, s_hi], axis=0), NN) + mm(q_hi, s_lo, NN)
        out = out + weight_cols[:, first + level : first + level + 1] * made
    mean = jnp.mean(out * out, axis=1, keepdims=True)
    out = out * (1.0 / jnp.sqrt(mean + 1e-06)) * gain_ref[...]
    hi, lo = split(out)
    hi_ref[...] = hi
    lo_ref[...] = lo


def far_and_norm(upper, queries, near, weights, gain, states, first):
    heads = states[0].shape[0]
    tok = queries.shape[0]
    levels = weights.shape[1]
    out = jax.ShapeDtypeStruct((tok, heads * DH), BF16)
    return pl.pallas_call(
        far_kernel,
        out_shape=(out, out),
        grid=(heads,),
        in_specs=[
            SMEM,
            pl.BlockSpec((tok, DH), lambda h: (0, first + h)),
            pl.BlockSpec((tok, DH), lambda h: (0, h)),
            pl.BlockSpec((1, levels, tok), lambda h: (first + h, 0, 0)),
            pl.BlockSpec((1, DH), lambda h: (0, first + h)),
        ]
        + [pl.BlockSpec((1, ROWS, DH), lambda h: (h, 0, 0))] * len(states),
        out_specs=[pl.BlockSpec((tok, DH), lambda h: (0, h))] * 2,
        compiler_params=params(),
        cost_estimate=cost(8 * len(states) * tok * heads * DH * DH, 16 * tok * heads * DH),
        name="far",
    )(upper, queries, near, weights, gain, *states)


def project_kernel(side_ref, hi_ref, lo_ref, w_ref, *refs):
    out_ref = refs[-1]
    w_hi, w_lo = split(w_ref[...])
    x_hi, x_lo = hi_ref[...], lo_ref[...]
    made = mm(x_hi, w_hi, NT) + (mm(x_hi, w_lo, NT) + mm(x_lo, w_hi, NT))
    if len(refs) == 2:
        made = made + refs[0][...]
    out_ref[...] = made


def project(side, x_hi, x_lo, weight, part, sides, so_far=None):
    tok, depth = x_hi.shape
    width = weight.shape[0] // sides
    tile = 256
    steps = width // tile
    whole = pl.BlockSpec((tok, depth), lambda i, side: (0, 0))
    moving = pl.BlockSpec((tok, tile), lambda i, side: (0, i))
    more = [] if so_far is None else [so_far]
    return pl.pallas_call(
        project_kernel,
        out_shape=jax.ShapeDtypeStruct((tok, width), F32),
        grid_spec=pltpu.PrefetchScalarGridSpec(
            num_scalar_prefetch=1,
            grid=(steps,),
            in_specs=[
                whole,
                whole,
                pl.BlockSpec((tile, depth), lambda i, side: (side[0] * steps + i, part)),
            ]
            + [moving] * len(more),
            out_specs=moving,
        ),
        compiler_params=params(),
        cost_estimate=cost(6 * tok * depth * width, 4 * (depth * width + 2 * tok * width)),
        name="project",
    )(side, x_hi, x_lo, weight, *more)


def local(queries, keys, values, log_decay, level_weights, norm_gain, out_weight):
    head_count, tok = log_decay.shape
    chunks = tok // CHUNK
    n_seq = lax.axis_size("seq")
    sides = lax.axis_size("head")
    seq_bits = n_seq.bit_length() - 1
    near_levels = tok.bit_length()
    seq_index = lax.axis_index("seq")
    groups = 2
    size = head_count // groups

    weight = lax.all_gather(out_weight.T, "seq", axis=0, tiled=True)

    upper = (seq_index >> jnp.arange(seq_bits, dtype=jnp.int32)) & 1
    blocks = []
    for g in range(groups):
        cols = slice(g * size * DH, (g + 1) * size * DH)
        blocks.append(own_state(keys[:, cols], values[:, cols], log_decay[g * size : (g + 1) * size]))

    upto = jnp.triu(jnp.ones((CHUNK, CHUNK), F32))
    cum = jnp.dot(log_decay.reshape(head_count * chunks, CHUNK), upto, precision=HIGH)
    cum = cum.reshape(head_count, chunks, CHUNK)
    ends = cum[:, :, -1:]
    totals = jnp.broadcast_to(ends, (head_count, chunks, DH))
    starts = [jnp.zeros_like(ends[:, :1])]
    for m in range(chunks - 1):
        starts.append(starts[-1] + ends[:, m : m + 1])
    start = jnp.concatenate(starts, axis=1)
    past = jnp.concatenate([jnp.zeros_like(ends[:, :3]), ends[:, 2:3]], axis=1)
    position = jnp.arange(chunks, dtype=jnp.int32)[None, :, None]
    odd = jnp.where(position % 2 == 1, jnp.exp(cum), 0.0).reshape(head_count, 1, tok)
    late = jnp.where(position >= 2, jnp.exp(cum + past), 0.0).reshape(head_count, 1, tok)
    far = jnp.exp(cum + start).reshape(head_count, 1, tok)
    weights = jnp.concatenate(
        [
            level_weights[:, : near_levels - 2],
            level_weights[:, near_levels - 2 : near_levels - 1] * odd,
            level_weights[:, near_levels - 1 : near_levels] * late,
            level_weights[:, near_levels:] * far,
        ],
        axis=1,
    )
    cum = cum.reshape(head_count, tok)

    near = []
    small = 4
    for g in range(groups):
        parts = [
            near_part(queries, keys, values, cum, totals, weights, first, small)
            for first in range(g * size, (g + 1) * size, small)
        ]
        near.append(jnp.concatenate(parts, axis=1))

    arrived = [[] for _ in range(groups)]
    for bit in range(seq_bits):
        last = bit == seq_bits - 1
        pairs = [(s, s ^ 2**bit) for s in range(n_seq) if not last or not s >> bit & 1]
        for g in range(groups):
            other = lax.ppermute(blocks[g], "seq", pairs)
            arrived[g].append(other)
            if not last:
                blocks[g] = merged(upper[bit : bit + 1], blocks[g], other)

    me = lax.axis_index("head").astype(jnp.int32)
    mine = me.reshape(1)
    theirs = (sides - 1 - me).reshape(1)
    gain = norm_gain.reshape(1, -1)
    to_send = to_keep = None
    for g in range(groups):
        x_hi, x_lo = far_and_norm(upper, queries, near[g], weights, gain, arrived[g], g * size)
        to_send = project(theirs, x_hi, x_lo, weight, g, sides, to_send)
        if g == groups - 1:
            came = lax.ppermute(to_send, "head", [(s, sides - 1 - s) for s in range(sides)])
        to_keep = project(mine, x_hi, x_lo, weight, g, sides, to_keep)
    return to_keep + came


def solution(mesh):
    return jax.shard_map(
        local,
        mesh=mesh,
        in_specs=(
            P("seq", "head"),
            P("seq", "head"),
            P("seq", "head"),
            P("head", "seq"),
            P("head", None, "seq"),
            P("head"),
            P("head", "seq"),
        ),
        out_specs=P("seq", "head"),
        check_vma=False,
    )
```

```python
import functools

import jax
import jax.numpy as jnp
from jax import lax
from jax.experimental import pallas as pl
from jax.experimental.pallas import tpu as pltpu
from jax.sharding import PartitionSpec as P

HIGH = lax.Precision.HIGHEST
DH = 128
CHUNK = 128
ROWS = DH + 8
F32 = jnp.float32
BF16 = jnp.bfloat16
NT = (((1,), (1,)), ((), ()))
TN = (((0,), (0,)), ((), ()))
NN = (((1,), (0,)), ((), ()))
ANY = pl.BlockSpec(memory_space=pl.ANY)
VMEM = pl.BlockSpec(memory_space=pltpu.VMEM)
SMEM = pl.BlockSpec(memory_space=pltpu.SMEM)


def params(mib=56):
    return pltpu.CompilerParams(vmem_limit_bytes=mib * 2**20)


def cost(flops, bytes_accessed):
    return pl.CostEstimate(flops=int(flops), bytes_accessed=int(bytes_accessed), transcendentals=0)


def split(x):
    hi = x.astype(BF16)
    return hi, (x - hi.astype(F32)).astype(BF16)


def split3(x):
    hi = x.astype(BF16)
    rest = x - hi.astype(F32)
    mid = rest.astype(BF16)
    return hi, mid, (rest - mid.astype(F32)).astype(BF16)


def mm(a, b, dims):
    return lax.dot_general(a, b, dims, preferred_element_type=F32)


def mm3(a, b, dims):
    a_hi, a_lo = split(a)
    b_hi, b_lo = split(b)
    return mm(a_hi, b_hi, dims) + (mm(a_hi, b_lo, dims) + mm(a_lo, b_hi, dims))


def outer_sum(k, v):
    made = mm(jnp.concatenate(split(k), axis=1), jnp.concatenate(split(v), axis=1), TN)
    return made[:DH, :DH] + (made[:DH, DH:] + made[DH:, :DH])


def state_kernel(k_ref, v_ref, ld_ref, *refs):
    out_ref = refs[-1]
    heads, tok = ld_ref.shape
    ld = ld_ref[...]
    later = lax.broadcasted_iota(jnp.int32, (tok, tok), 1) > lax.broadcasted_iota(jnp.int32, (tok, tok), 0)
    later = jnp.where(later, 1.0, 0.0).astype(BF16)
    hi, mid, low = split3(ld)
    fade = jnp.exp(mm(later, hi, NT) + (mm(later, mid, NT) + mm(later, low, NT)))
    total = jnp.sum(ld, axis=1, keepdims=True)
    for h in range(heads):
        cols = pl.ds(h * DH, DH)
        out_ref[h, :DH, :] = outer_sum(k_ref[:, cols] * fade[:, h : h + 1], v_ref[:, cols])
        out_ref[h, DH:, :] = jnp.broadcast_to(total[h : h + 1, :], (ROWS - DH, DH))


def own_state(keys, values, log_decay, group, heads, after=()):
    tok = keys.shape[0]
    width = heads * DH
    wide = pl.BlockSpec((tok, width), lambda i: (0, group))
    return pl.pallas_call(
        state_kernel,
        out_shape=jax.ShapeDtypeStruct((heads, ROWS, DH), F32),
        grid=(1,),
        in_specs=[wide, wide, pl.BlockSpec((heads, tok), lambda i: (group, 0))] + [ANY] * len(after),
        out_specs=pl.BlockSpec((heads, ROWS, DH), lambda i: (0, 0, 0)),
        compiler_params=params(),
        cost_estimate=cost(8 * tok * width * DH, 4 * (2 * tok * width)),
        name="own_state",
    )(keys, values, log_decay, *after)


def merge_kernel(bit, upper_ref, mine_ref, other_ref, *refs):
    out_ref = refs[-1]
    upper = upper_ref[bit] == 1
    for h in range(mine_ref.shape[0]):
        mine, other = mine_ref[h], other_ref[h]
        low = jnp.where(upper, other, mine)
        high = jnp.where(upper, mine, other)
        faded = jnp.exp(high[DH : DH + 1, :])
        out_ref[h, :DH, :] = faded * low[:DH] + high[:DH]
        out_ref[h, DH:, :] = low[DH:] + high[DH:]


def merged(bit, upper, mine, other, after=()):
    return pl.pallas_call(
        functools.partial(merge_kernel, bit),
        out_shape=jax.ShapeDtypeStruct(mine.shape, F32),
        in_specs=[SMEM, VMEM, VMEM] + [ANY] * len(after),
        out_specs=VMEM,
        compiler_params=params(),
        cost_estimate=cost(3 * mine.size, 12 * mine.size),
        name="merge",
    )(upper, mine, other, *after)


def near_kernel(levels, q_ref, k_ref, v_ref, ld_ref, w_ref, *refs):
    out_ref, far_ref = refs[-2:]
    _, heads, tok = ld_ref.shape
    chunks = tok // CHUNK
    tile_bits = CHUNK.bit_length() - 1
    row = lax.broadcasted_iota(jnp.int32, (CHUNK, CHUNK), 0)
    col = lax.broadcasted_iota(jnp.int32, (CHUNK, CHUNK), 1)
    apart = row ^ col
    causal = row >= col
    upto = jnp.where(row <= col, 1.0, 0.0).astype(BF16)
    ld = ld_ref[0]
    cums = []
    for m in range(chunks):
        hi, mid, low = split3(ld[:, m * CHUNK : (m + 1) * CHUNK])
        cums.append(mm(hi, upto, NN) + (mm(mid, upto, NN) + mm(low, upto, NN)))
    start = jnp.zeros((heads, 1), F32)
    fulls = []
    for m in range(chunks):
        fulls.append(cums[m] + start)
        start = start + cums[m][:, CHUNK - 1 : CHUNK]
    cum = jnp.concatenate(cums, axis=1)
    full = jnp.concatenate(fulls, axis=1)
    pad = jnp.zeros((8 - heads % 8, tok), F32)
    cum_cols = jnp.transpose(jnp.concatenate([cum, pad], axis=0))
    for h in range(heads):
        cols = pl.ds(h * DH, DH)
        w = w_ref[h]
        far_decay = jnp.exp(full[h : h + 1])
        weights = jnp.concatenate([w[: levels], w[levels :] * far_decay], axis=0)
        weight_cols = jnp.transpose(weights)
        far_ref[h] = weight_cols
        states = []
        ends = []
        for m in range(chunks):
            rows = pl.ds(m * CHUNK, CHUNK)
            at = slice(m * CHUNK, (m + 1) * CHUNK)
            q = q_ref[rows, cols] * DH**-0.5
            k = k_ref[rows, cols]
            v = v_ref[rows, cols]
            w = weight_cols[at]
            c = cum_cols[at, h : h + 1]
            near = jnp.broadcast_to(w[:, 0:1], (CHUNK, CHUNK))
            for bit in range(tile_bits):
                near = jnp.where(apart >= 2**bit, w[:, bit + 1 : bit + 2], near)
            gap = jnp.where(causal, c - cums[m][h : h + 1, :], -1e30)
            scores = mm3(q, k, NT) * (near * jnp.exp(gap))
            out = mm3(scores, v, NN)
            for bit in range(2):
                if m >> bit & 1:
                    first = (m >> bit) - 1 << bit
                    seen = states[first]
                    for n in range(first + 1, first + 2**bit):
                        seen = jnp.exp(ends[n]) * seen + states[n]
                    gone = c
                    for n in range(first + 2**bit, m):
                        gone = gone + ends[n]
                    level = tile_bits + 1 + bit
                    out = out + (w[:, level : level + 1] * jnp.exp(gone)) * mm3(q, seen, NN)
            out_ref[rows, cols] = out
            if m < chunks - 1:
                end = cums[m][h : h + 1, CHUNK - 1 : CHUNK]
                states.append(outer_sum(k * jnp.exp(end - c), v))
                ends.append(end)


def near_part(queries, keys, values, log_decay, level_weights, first, heads, after=()):
    tok = queries.shape[0]
    width = heads * DH
    levels = level_weights.shape[1]
    wide = pl.BlockSpec((tok, width), lambda i: (0, first // heads))
    return pl.pallas_call(
        functools.partial(near_kernel, tok.bit_length()),
        out_shape=(
            jax.ShapeDtypeStruct((tok, width), F32),
            jax.ShapeDtypeStruct((heads, tok, levels), F32),
        ),
        grid=(1,),
        in_specs=[
            wide,
            wide,
            wide,
            pl.BlockSpec((1, heads, tok), lambda i: (first // heads, 0, 0)),
            pl.BlockSpec((heads, levels, tok), lambda i: (first // heads, 0, 0)),
        ]
        + [ANY] * len(after),
        out_specs=[
            pl.BlockSpec((tok, width), lambda i: (0, 0)),
            pl.BlockSpec((heads, tok, levels), lambda i: (0, 0, 0)),
        ],
        compiler_params=params(),
        cost_estimate=cost(60 * tok * width * DH, 16 * tok * width),
        name="near",
    )(queries, keys, values, log_decay.reshape(-1, heads, tok), level_weights, *after)


def far_kernel(count, skip, last, pieces, upper_ref, q_ref, *refs):
    near_refs, refs = refs[:pieces], refs[pieces:]
    w_refs, refs = refs[:2], refs[2:]
    gain_ref, state_refs, out_ref = refs[0], refs[1 : 1 + count], refs[-1]
    halves = pl.num_programs(0) // 2
    h = pl.program_id(0)

    def run(near_ref, w_ref):
        q_hi, q_lo = split(q_ref[...] * DH**-0.5)
        q_both = jnp.concatenate([q_hi, q_lo], axis=1)
        w = w_ref[0]
        out = near_ref[...]
        before = jnp.zeros((1, DH), F32)
        for level in range(count):
            upper = upper_ref[level] == 1
            ref = state_refs[level]
            if level >= skip:
                reach = jnp.where(upper, jnp.exp(before), 0.0)
                s_hi, s_lo = split(ref[0, :DH, :] * reach)
                made = mm(q_both, jnp.concatenate([s_hi, s_hi], axis=0), NN) + mm(q_hi, s_lo, NN)
                at = w.shape[1] - upper_ref.shape[0] + level
                out = out + w[:, at : at + 1] * made
            end = ref.shape[1] - (ROWS - DH)
            before = before + jnp.where(upper, ref[0, end : end + 1, :], 0.0)
        if last:
            mean = jnp.mean(out * out, axis=1, keepdims=True)
            out = out * (1.0 / jnp.sqrt(mean + 1e-06)) * gain_ref[...]
            hi, lo = split(out)
            out_ref[...] = jnp.concatenate([hi, lo, hi], axis=1)
        else:
            out_ref[...] = out

    @pl.when(h < halves)
    def _():
        run(near_refs[0], w_refs[0])

    @pl.when(h >= halves)
    def _():
        run(near_refs[-1], w_refs[1])


def far_part(upper, queries, so_far, weights, gain, states, first, skip, last, after=()):
    heads = states[0].shape[0]
    tok = queries.shape[0]
    levels = weights[0].shape[2]
    half = heads // 2
    if len(so_far) == 1:
        near_maps = [lambda h: (0, h)]
    else:
        near_maps = [lambda h: (0, jnp.minimum(h, half - 1)), lambda h: (0, jnp.maximum(h - half, 0))]
    w_maps = [lambda h: (jnp.minimum(h, half - 1), 0, 0), lambda h: (jnp.maximum(h - half, 0), 0, 0)]
    out, width = (BF16, 3 * DH) if last else (F32, DH)
    count = len(states)
    return pl.pallas_call(
        functools.partial(far_kernel, count, skip, last, len(so_far)),
        out_shape=jax.ShapeDtypeStruct((tok, heads * width), out),
        grid=(heads,),
        in_specs=[SMEM, pl.BlockSpec((tok, DH), lambda h: (0, first + h))]
        + [pl.BlockSpec((tok, DH), m) for m in near_maps]
        + [pl.BlockSpec((1, tok, levels), m) for m in w_maps]
        + [pl.BlockSpec((1, DH), lambda h: (0, first + h))]
        + [
            pl.BlockSpec((1, ROWS, DH), lambda h: (h, 0, 0))
            if level >= skip
            else pl.BlockSpec((1, ROWS - DH, DH), lambda h: (h, DH // (ROWS - DH), 0))
            for level in range(count)
        ]
        + [ANY] * len(after),
        out_specs=pl.BlockSpec((tok, width), lambda h: (0, h)),
        compiler_params=params(),
        cost_estimate=cost(8 * count * tok * heads * DH * DH, 16 * tok * heads * DH),
        name="far",
    )(upper, queries, *so_far, *weights, gain, *states, *after)


def project_kernel(side_ref, x_ref, w_ref, *refs):
    out_ref = refs[-1]
    w_hi, w_lo = split(w_ref[...])
    parts = []
    for h in range(w_hi.shape[1] // DH):
        at = slice(h * DH, (h + 1) * DH)
        parts += [w_hi[:, at], w_hi[:, at], w_lo[:, at]]
    made = mm(x_ref[...], jnp.concatenate(parts, axis=1), NT)
    if len(refs) == 2:
        made = made + refs[0][...]
    out_ref[...] = made


def project(side, x, weight, part, sides, so_far=None):
    tok, depth = x.shape
    width = weight.shape[0] // sides
    tile = 256
    steps = width // tile
    moving = pl.BlockSpec((tok, tile), lambda i, side: (0, i))
    more = [] if so_far is None else [so_far]
    return pl.pallas_call(
        project_kernel,
        out_shape=jax.ShapeDtypeStruct((tok, width), F32),
        grid_spec=pltpu.PrefetchScalarGridSpec(
            num_scalar_prefetch=1,
            grid=(steps,),
            in_specs=[
                pl.BlockSpec((tok, depth), lambda i, side: (0, 0)),
                pl.BlockSpec((tile, depth // 3), lambda i, side: (side[0] * steps + i, part)),
            ]
            + [moving] * len(more),
            out_specs=moving,
        ),
        compiler_params=params(),
        cost_estimate=cost(2 * tok * depth * width, 4 * (depth * width + 2 * tok * width)),
        name="project",
    )(side, x, weight, *more)


def local(queries, keys, values, log_decay, level_weights, norm_gain, out_weight):
    head_count, tok = log_decay.shape
    n_seq = lax.axis_size("seq")
    sides = lax.axis_size("head")
    seq_bits = n_seq.bit_length() - 1
    seq_index = lax.axis_index("seq")
    size = head_count // 2
    small = size // 2
    early = 4

    weight = lax.all_gather(out_weight.T, "seq", axis=0, tiled=True)
    upper = (seq_index >> jnp.arange(seq_bits, dtype=jnp.int32)) & 1
    gain = norm_gain.reshape(1, -1)

    def send(block, bit):
        def wanted(s):
            above = s >> bit
            return not (bit == seq_bits - 1 and above & 1) and not (bit == seq_bits - 2 and above == 3)

        return lax.ppermute(block, "seq", [(s, s ^ 2**bit) for s in range(n_seq) if wanted(s)])

    def near(n, *after):
        return near_part(queries, keys, values, log_decay, level_weights, n * small, small, after)

    def far(group, made, states, skip, last, *after):
        outs = [o for o, _ in made] if isinstance(made, list) else [made]
        return far_part(
            upper, queries, outs, near_cols[group], gain, states, group * size, skip, last, after
        )

    near_cols = {}
    a = [own_state(keys, values, log_decay, 0, size)]
    came_a = [send(a[0], 0)]
    n0 = near(0, a[0])
    a.append(merged(0, upper, a[0], came_a[0], (n0[0],)))
    came_a.append(send(a[1], 1))
    n1 = near(1, a[1])
    a.append(merged(1, upper, a[1], came_a[1], (n1[0],)))
    came_a.append(send(a[2], 2))
    b = [own_state(keys, values, log_decay, 1, size, (a[2],))]
    came_b = [send(b[0], 0)]
    n2 = near(2, b[0])
    a.append(merged(2, upper, a[2], came_a[2], (n2[0],)))
    came_a.append(send(a[3], 3))
    b.append(merged(0, upper, b[0], came_b[0], (a[3],)))
    came_b.append(send(b[1], 1))
    n3 = near(3, b[1])
    a.append(merged(3, upper, a[3], came_a[3], (n3[0],)))
    came_a.append(send(a[4], 4))
    b.append(merged(1, upper, b[1], came_b[1], (a[4],)))
    came_b.append(send(b[2], 2))
    near_cols[0] = [n0[1], n1[1]]
    near_cols[1] = [n2[1], n3[1]]
    far_a = far(0, [n0, n1], came_a[:early], 0, False, b[2])
    a.append(merged(4, upper, a[4], came_a[4], (far_a,)))
    came_a.append(send(a[5], 5))
    b.append(merged(2, upper, b[2], came_b[2], (a[5],)))
    came_b.append(send(b[3], 3))
    b.append(merged(3, upper, b[3], came_b[3]))
    came_b.append(send(b[4], 4))
    x_a = far(0, far_a, came_a, early, True, b[4])
    far_b = far(1, [n2, n3], came_b[:early], 0, False, x_a)
    b.append(merged(4, upper, b[4], came_b[4], (far_b,)))
    came_b.append(send(b[5], 5))

    me = lax.axis_index("head").astype(jnp.int32)
    mine = me.reshape(1)
    theirs = (sides - 1 - me).reshape(1)
    to_send = project(theirs, x_a, weight, 0, sides)
    to_keep = project(mine, x_a, weight, 0, sides)
    x_b = far(1, far_b, came_b, early, True, to_keep)
    to_send = project(theirs, x_b, weight, 1, sides, to_send)
    came = lax.ppermute(to_send, "head", [(s, sides - 1 - s) for s in range(sides)])
    to_keep = project(mine, x_b, weight, 1, sides, to_keep)
    return to_keep + came


def solution(mesh):
    return jax.shard_map(
        local,
        mesh=mesh,
        in_specs=(
            P("seq", "head"),
            P("seq", "head"),
            P("seq", "head"),
            P("head", "seq"),
            P("head", None, "seq"),
            P("head"),
            P("head", "seq"),
        ),
        out_specs=P("seq", "head"),
        check_vma=False,
    )
```

```python
import functools

import jax
import jax.numpy as jnp
from jax import lax
from jax.experimental import pallas as pl
from jax.experimental.pallas import tpu as pltpu
from jax.sharding import PartitionSpec as P

HIGH = lax.Precision.HIGHEST
DH = 128
CHUNK = 128
ROWS = DH + 8
F32 = jnp.float32
BF16 = jnp.bfloat16
NT = (((1,), (1,)), ((), ()))
TN = (((0,), (0,)), ((), ()))
NN = (((1,), (0,)), ((), ()))
ANY = pl.BlockSpec(memory_space=pl.ANY)
VMEM = pl.BlockSpec(memory_space=pltpu.VMEM)
SMEM = pl.BlockSpec(memory_space=pltpu.SMEM)


def params(mib=52):
    return pltpu.CompilerParams(vmem_limit_bytes=mib * 2**20)


def cost(flops, bytes_accessed):
    return pl.CostEstimate(flops=int(flops), bytes_accessed=int(bytes_accessed), transcendentals=0)


def split(x):
    hi = x.astype(BF16)
    return hi, (x - hi.astype(F32)).astype(BF16)


def split3(x):
    hi = x.astype(BF16)
    rest = x - hi.astype(F32)
    mid = rest.astype(BF16)
    return hi, mid, (rest - mid.astype(F32)).astype(BF16)


def mm(a, b, dims):
    return lax.dot_general(a, b, dims, preferred_element_type=F32)


def mm3(a, b, dims):
    a_hi, a_lo = split(a)
    b_hi, b_lo = split(b)
    return mm(a_hi, b_hi, dims) + (mm(a_hi, b_lo, dims) + mm(a_lo, b_hi, dims))


def outer_sum(k, v):
    made = mm(jnp.concatenate(split(k), axis=1), jnp.concatenate(split(v), axis=1), TN)
    return made[:DH, :DH] + (made[:DH, DH:] + made[DH:, :DH])


def state_kernel(k_ref, v_ref, ld_ref, *refs):
    out_ref, fade_ref = refs[-2:]
    heads, tok = ld_ref.shape
    step = k_ref.shape[1] // DH
    i = pl.program_id(0)

    @pl.when(i == 0)
    def _():
        ld = ld_ref[...]
        later = lax.broadcasted_iota(jnp.int32, (tok, tok), 1) > lax.broadcasted_iota(jnp.int32, (tok, tok), 0)
        later = jnp.where(later, 1.0, 0.0).astype(BF16)
        made = mm(later, jnp.concatenate(split3(ld), axis=0), NT)
        fade = jnp.exp(made[:, :heads] + (made[:, heads : 2 * heads] + made[:, 2 * heads :]))
        for j in range(heads // step):
            fade_ref[j] = fade[:, j * step : (j + 1) * step]

    fade = fade_ref[i]
    for h in range(step):
        cols = pl.ds(h * DH, DH)
        out_ref[h, :DH, :] = outer_sum(k_ref[:, cols] * fade[:, h : h + 1], v_ref[:, cols])
        total = jnp.sum(ld_ref[pl.ds(i * step + h, 1), :], axis=1, keepdims=True)
        out_ref[h, DH:, :] = jnp.broadcast_to(total, (ROWS - DH, DH))


def own_state(keys, values, log_decay, group, heads, after=()):
    tok = keys.shape[0]
    step = 2
    steps = heads // step
    wide = pl.BlockSpec((tok, step * DH), lambda i: (0, group * steps + i))
    return pl.pallas_call(
        state_kernel,
        out_shape=jax.ShapeDtypeStruct((heads, ROWS, DH), F32),
        grid=(steps,),
        in_specs=[wide, wide, pl.BlockSpec((heads, tok), lambda i: (group, 0))] + [ANY] * len(after),
        out_specs=pl.BlockSpec((step, ROWS, DH), lambda i: (i, 0, 0)),
        scratch_shapes=[pltpu.VMEM((steps, tok, step), F32)],
        compiler_params=params(),
        cost_estimate=cost(8 * tok * heads * DH * DH, 8 * tok * heads * DH),
        name="own_state",
    )(keys, values, log_decay, *after)


def merge_kernel(bit, upper_ref, mine_ref, other_ref, *refs):
    out_ref = refs[-1]
    upper = upper_ref[bit] == 1
    for h in range(mine_ref.shape[0]):
        mine, other = mine_ref[h], other_ref[h]
        low = jnp.where(upper, other, mine)
        high = jnp.where(upper, mine, other)
        faded = jnp.exp(high[DH : DH + 1, :])
        out_ref[h, :DH, :] = faded * low[:DH] + high[:DH]
        out_ref[h, DH:, :] = low[DH:] + high[DH:]


def merged(bit, upper, mine, other, after=()):
    return pl.pallas_call(
        functools.partial(merge_kernel, bit),
        out_shape=jax.ShapeDtypeStruct(mine.shape, F32),
        in_specs=[SMEM, VMEM, VMEM] + [ANY] * len(after),
        out_specs=VMEM,
        compiler_params=params(16),
        cost_estimate=cost(3 * mine.size, 12 * mine.size),
        name="merge",
    )(upper, mine, other, *after)


def prepare_kernel(ld_ref, w_ref, *refs):
    sums_ref, cols_ref, weights_ref = refs[-3:]
    heads, tok = ld_ref.shape
    levels = w_ref.shape[1]
    chunks = tok // CHUNK
    near_levels = tok.bit_length()
    row = lax.broadcasted_iota(jnp.int32, (CHUNK, CHUNK), 0)
    col = lax.broadcasted_iota(jnp.int32, (CHUNK, CHUNK), 1)
    upto = jnp.where(row <= col, 1.0, 0.0).astype(BF16)
    sums = []
    for m in range(chunks):
        hi, mid, low = split3(ld_ref[:, m * CHUNK : (m + 1) * CHUNK])
        sums.append(mm(hi, upto, NN) + (mm(mid, upto, NN) + mm(low, upto, NN)))
    start = jnp.zeros((heads, 1), F32)
    fulls = []
    halves = []
    for m in range(chunks):
        fulls.append(sums[m] + start)
        halves.append(sums[m] + (sums[m - 1][:, CHUNK - 1 :] if m % 4 == 3 else 0.0))
        start = start + sums[m][:, CHUNK - 1 :]
    cum = jnp.concatenate(sums, axis=1)
    one = jnp.exp(cum)
    two = jnp.exp(jnp.concatenate(halves, axis=1))
    far = jnp.exp(jnp.concatenate(fulls, axis=1))
    for h in range(heads):
        sums_ref[h] = cum[h : h + 1]
    fill = jnp.zeros((CHUNK - heads, tok), F32)
    cols_ref[...] = jnp.transpose(jnp.concatenate([cum, fill], axis=0))
    level = lax.broadcasted_iota(jnp.int32, (levels, tok), 0)
    per = CHUNK // levels
    for g in range(heads // per):
        made = []
        for h in range(g * per, (g + 1) * per):
            decay = jnp.where(level >= near_levels, far[h : h + 1], two[h : h + 1])
            decay = jnp.where(level == near_levels - 2, one[h : h + 1], decay)
            decay = jnp.where(level < near_levels - 2, 1.0, decay)
            made.append(w_ref[h] * decay)
        weights_ref[:, g * CHUNK : (g + 1) * CHUNK] = jnp.transpose(jnp.concatenate(made, axis=0))


def prepare(log_decay, level_weights, after=()):
    heads, tok = log_decay.shape
    levels = level_weights.shape[1]
    return pl.pallas_call(
        prepare_kernel,
        out_shape=(
            jax.ShapeDtypeStruct((heads, 1, tok), F32),
            jax.ShapeDtypeStruct((tok, CHUNK), F32),
            jax.ShapeDtypeStruct((tok, heads * levels), F32),
        ),
        in_specs=[VMEM, VMEM] + [ANY] * len(after),
        out_specs=[VMEM] * 3,
        compiler_params=params(),
        cost_estimate=cost(0, 8 * heads * levels * tok),
        name="prepare",
    )(log_decay, level_weights, *after)


def near_kernel(first, levels, q_ref, k_ref, v_ref, sums_ref, cols_ref, w_ref, *refs):
    out_ref, token_ref = refs[-2:]
    tok = q_ref.shape[0]
    chunks = tok // CHUNK
    tile_bits = CHUNK.bit_length() - 1
    row = lax.broadcasted_iota(jnp.int32, (CHUNK, CHUNK), 0)
    col = lax.broadcasted_iota(jnp.int32, (CHUNK, CHUNK), 1)
    apart = row ^ col
    causal = row >= col
    head = first + pl.program_id(0)
    per = CHUNK // levels
    token_ref[...] = jnp.zeros_like(token_ref)
    states = []
    ends = []
    for m in range(chunks):
        rows = pl.ds(m * CHUNK, CHUNK)
        q = q_ref[rows, :] * DH**-0.5
        k = k_ref[rows, :]
        v = v_ref[rows, :]
        w = pltpu.roll(w_ref[rows, :], (per - head % per) * levels, 1)
        c_cols = pltpu.roll(cols_ref[rows, :], CHUNK - head, 1)
        c = c_cols[:, 0:1]
        near = jnp.broadcast_to(w[:, 0:1], (CHUNK, CHUNK))
        for bit in range(tile_bits):
            near = jnp.where(apart >= 2**bit, w[:, bit + 1 : bit + 2], near)
        gap = jnp.where(causal, c - sums_ref[0, :, m * CHUNK : (m + 1) * CHUNK], -1e30)
        q_hi, q_lo = split(q)
        k_hi, k_lo = split(k)
        q_both = jnp.concatenate([q_hi, q_lo], axis=1)
        scores = mm(q_both, jnp.concatenate([k_hi, k_hi], axis=1), NT) + mm(q_hi, k_lo, NT)
        scores = scores * (near * jnp.exp(gap))
        s_hi, s_lo = split(scores)
        v_hi, v_lo = split(v)
        s_both = jnp.concatenate([s_hi, s_lo], axis=1)
        out = mm(s_both, jnp.concatenate([v_hi, v_hi], axis=0), NN) + mm(s_hi, v_lo, NN)
        for bit in range(2):
            if m >> bit & 1:
                at = (m >> bit) - 1 << bit
                seen = states[at]
                for n in range(at + 1, at + 2**bit):
                    seen = jnp.exp(ends[n]) * seen + states[n]
                level = tile_bits + 1 + bit
                s_hi, s_lo = split(seen)
                made = mm(q_both, jnp.concatenate([s_hi, s_hi], axis=0), NN) + mm(q_hi, s_lo, NN)
                out = out + w[:, level : level + 1] * made
        out_ref[rows, :] = out
        if m < chunks - 1:
            end = c[CHUNK - 1 : CHUNK]
            states.append(outer_sum(k * jnp.exp(end - c), v))
            ends.append(end)


def near_part(queries, keys, values, sums, cols, weights, levels, first, heads, so_far=None, after=()):
    tok = queries.shape[0]
    per = CHUNK // levels
    one = pl.BlockSpec((tok, DH), lambda h: (0, first + h))
    more = [] if so_far is None else [so_far]
    return pl.pallas_call(
        functools.partial(near_kernel, first, levels),
        out_shape=(
            jax.ShapeDtypeStruct(queries.shape, F32),
            jax.ShapeDtypeStruct((8, CHUNK), F32),
        ),
        grid=(heads,),
        in_specs=[
            one,
            one,
            one,
            pl.BlockSpec((1, 1, tok), lambda h: (first + h, 0, 0)),
            pl.BlockSpec(cols.shape, lambda h: (0, 0)),
            pl.BlockSpec((tok, CHUNK), lambda h: (0, (first + h) // per)),
        ]
        + [ANY] * (len(more) + len(after)),
        out_specs=[one, pl.BlockSpec((8, CHUNK), lambda h: (0, 0))],
        input_output_aliases={6: 0} if more else {},
        compiler_params=params(),
        cost_estimate=cost(60 * tok * heads * DH * DH, 16 * tok * heads * DH),
        name="near",
    )(queries, keys, values, sums, cols, weights, *more, *after)


def far_kernel(first, levels, skip, last, count, upper_ref, q_ref, near_ref, w_ref, gain_ref, *refs):
    step = q_ref.shape[1] // DH
    outs = 3 if last else 2
    out_refs, token_ref = refs[-outs:-1], refs[-1]
    per = CHUNK // levels
    total = upper_ref.shape[0]
    head = first + pl.program_id(0) * step
    token_ref[...] = jnp.zeros_like(token_ref)
    w = pltpu.roll(w_ref[...], (per - head % per) * levels, 1)
    for h in range(step):
        cols = pl.ds(h * DH, DH)
        q_hi, q_lo = split(q_ref[:, cols] * DH**-0.5)
        out = near_ref[:, cols]
        before = jnp.zeros((1, DH), F32)
        used = []
        states = []
        for level in range(count):
            ref = refs[level]
            upper = upper_ref[level] == 1
            end = ref.shape[1] - (ROWS - DH)
            if level >= skip:
                reach = jnp.where(upper, jnp.exp(before), 0.0)
                hi, lo = split(ref[h, :DH, :] * reach)
                states.append(jnp.concatenate([hi, hi, lo], axis=0))
                used.append(h * levels + levels - total + level)
            before = before + jnp.where(upper, ref[h, end : end + 1, :], 0.0)
        made = mm(jnp.concatenate([q_hi, q_lo, q_hi], axis=1), jnp.concatenate(states, axis=1), NN)
        for n, at in enumerate(used):
            out = out + w[:, at : at + 1] * made[:, n * DH : (n + 1) * DH]
        if last:
            squares = jnp.concatenate(split(out * out), axis=1)
            mean = mm(squares, jnp.full((2 * DH, DH), 1.0 / DH, BF16), NN)
            out = out * lax.rsqrt(mean + 1e-06) * gain_ref[:, cols]
            hi, lo = split(out)
            out_refs[0][:, cols] = hi
            out_refs[1][:, cols] = lo
        else:
            out_refs[0][:, cols] = out


def far_part(upper, queries, so_far, at, weights, levels, gain, states, first, skip, last, after=()):
    heads = states[0].shape[0]
    tok = queries.shape[0]
    per = CHUNK // levels
    step = 2
    out = jax.ShapeDtypeStruct((tok, heads * DH), BF16 if last else F32)
    outs = 2 if last else 1
    tail = ROWS - DH
    return pl.pallas_call(
        functools.partial(far_kernel, first, levels, skip, last, len(states)),
        out_shape=(out,) * outs + (jax.ShapeDtypeStruct((8, CHUNK), F32),),
        grid=(heads // step,),
        in_specs=[
            SMEM,
            pl.BlockSpec((tok, step * DH), lambda i: (0, first // step + i)),
            pl.BlockSpec((tok, step * DH), lambda i: (0, at // step + i)),
            pl.BlockSpec((tok, CHUNK), lambda i: (0, (first + i * step) // per)),
            pl.BlockSpec((1, step * DH), lambda i: (0, first // step + i)),
        ]
        + [
            pl.BlockSpec((step, ROWS, DH), lambda i: (i, 0, 0))
            if level >= skip
            else pl.BlockSpec((step, tail, DH), lambda i: (i, DH // tail, 0))
            for level in range(len(states))
        ]
        + [ANY] * len(after),
        out_specs=[pl.BlockSpec((tok, step * DH), lambda i: (0, i))] * outs
        + [pl.BlockSpec((8, CHUNK), lambda i: (0, 0))],
        compiler_params=params(),
        cost_estimate=cost(8 * len(states) * tok * heads * DH * DH, 16 * tok * heads * DH),
        name="far",
    )(upper, queries, so_far, weights, gain, *states, *after)


def project_kernel(has_more, side_ref, hi_ref, lo_ref, w_ref, *refs):
    out_ref = refs[-1]
    w_hi, w_lo = split(w_ref[...])
    x_hi, x_lo = hi_ref[...], lo_ref[...]
    made = mm(x_hi, w_hi, NT) + (mm(x_hi, w_lo, NT) + mm(x_lo, w_hi, NT))
    if has_more:
        made = made + refs[0][...]
    out_ref[...] = made


def project(side, x_hi, x_lo, weight, part, sides, so_far=None, after=()):
    tok, depth = x_hi.shape
    width = weight.shape[0] // sides
    tile = 256
    steps = width // tile
    whole = pl.BlockSpec((tok, depth), lambda i, side: (0, 0))
    moving = pl.BlockSpec((tok, tile), lambda i, side: (0, i))
    more = [] if so_far is None else [so_far]
    return pl.pallas_call(
        functools.partial(project_kernel, bool(more)),
        out_shape=jax.ShapeDtypeStruct((tok, width), F32),
        grid_spec=pltpu.PrefetchScalarGridSpec(
            num_scalar_prefetch=1,
            grid=(steps,),
            in_specs=[
                whole,
                whole,
                pl.BlockSpec((tile, depth), lambda i, side: (side[0] * steps + i, part)),
            ]
            + [moving] * len(more)
            + [ANY] * len(after),
            out_specs=moving,
        ),
        compiler_params=params(),
        cost_estimate=cost(6 * tok * depth * width, 4 * (depth * width + 2 * tok * width)),
        name="project",
    )(side, x_hi, x_lo, weight, *more, *after)


def local(queries, keys, values, log_decay, level_weights, norm_gain, out_weight):
    head_count = log_decay.shape[0]
    levels = level_weights.shape[1]
    n_seq = lax.axis_size("seq")
    sides = lax.axis_size("head")
    seq_bits = n_seq.bit_length() - 1
    seq_index = lax.axis_index("seq")
    size = head_count // 2

    weight = lax.all_gather(out_weight.T, "seq", axis=0, tiled=True)
    upper = (seq_index >> jnp.arange(seq_bits, dtype=jnp.int32)) & 1
    gain = norm_gain.reshape(1, -1)

    def send(block, bit):
        def wanted(s):
            above = s >> bit
            return not (bit == seq_bits - 1 and above & 1) and not (bit == seq_bits - 2 and above == 3)

        return lax.ppermute(block, "seq", [(s, s ^ 2**bit) for s in range(n_seq) if wanted(s)])

    small = size // 2
    early = 4

    def near(n, so_far, *after):
        return near_part(
            queries, keys, values, sums, cols, weights, levels, n * small, small, so_far, after
        )

    def far(so_far, at, states, group, skip, last, *after):
        return far_part(
            upper, queries, so_far, at, weights, levels, gain, states, group * size, skip, last, after
        )

    a, came_a, b, came_b = [], [], [], []

    def go(blocks, came, *after):
        bit = len(blocks) - 1
        blocks.append(merged(bit, upper, blocks[bit], came[bit], after))
        came.append(send(blocks[-1], bit + 1))

    a.append(own_state(keys, values, log_decay, 0, size))
    came_a.append(send(a[0], 0))
    sums, cols, weights = prepare(log_decay, level_weights, (a[0],))
    close, token = near(0, None)
    go(a, came_a, token)
    close, token = near(1, close, a[1])
    go(a, came_a, token)
    b.append(own_state(keys, values, log_decay, 1, size, (a[2],)))
    came_b.append(send(b[0], 0))
    close, token = near(2, close, b[0])
    go(a, came_a, token)
    go(b, came_b, a[3])
    close, token = near(3, close, b[1])
    go(a, came_a, token)
    go(b, came_b, a[4])
    far_a, token = far(close, 0, came_a[:early], 0, 0, False, b[2])
    go(a, came_a, token)
    go(b, came_b, a[5])
    go(b, came_b)
    a_hi, a_lo, token = far(far_a, 0, came_a, 0, early, True, b[4])
    far_b, token = far(close, size, came_b[:early], 1, 0, False, token)
    go(b, came_b, token)

    me = lax.axis_index("head").astype(jnp.int32)
    mine = me.reshape(1)
    theirs = (sides - 1 - me).reshape(1)
    to_send = project(theirs, a_hi, a_lo, weight, 0, sides, None, (b[5],))
    to_keep = project(mine, a_hi, a_lo, weight, 0, sides, None, (b[5],))
    b_hi, b_lo, _ = far(far_b, 0, came_b, 1, early, True, to_send, to_keep)
    to_send = project(theirs, b_hi, b_lo, weight, 1, sides, to_send)
    came = lax.ppermute(to_send, "head", [(s, sides - 1 - s) for s in range(sides)])
    to_keep = project(mine, b_hi, b_lo, weight, 1, sides, to_keep)
    return to_keep + came


def solution(mesh):
    return jax.shard_map(
        local,
        mesh=mesh,
        in_specs=(
            P("seq", "head"),
            P("seq", "head"),
            P("seq", "head"),
            P("head", "seq"),
            P("head", None, "seq"),
            P("head"),
            P("head", "seq"),
        ),
        out_specs=P("seq", "head"),
        check_vma=False,
    )
```

```python
import functools

import jax
import jax.numpy as jnp
from jax import lax
from jax.experimental import pallas as pl
from jax.experimental.pallas import tpu as pltpu
from jax.sharding import PartitionSpec as P

HIGH = lax.Precision.HIGHEST
DH = 128
CHUNK = 128
ROWS = DH + 8
F32 = jnp.float32
BF16 = jnp.bfloat16
NT = (((1,), (1,)), ((), ()))
TN = (((0,), (0,)), ((), ()))
NN = (((1,), (0,)), ((), ()))
ANY = pl.BlockSpec(memory_space=pl.ANY)
VMEM = pl.BlockSpec(memory_space=pltpu.VMEM)
SMEM = pl.BlockSpec(memory_space=pltpu.SMEM)


def params(mib=52):
    return pltpu.CompilerParams(vmem_limit_bytes=mib * 2**20)


def cost(flops, bytes_accessed):
    return pl.CostEstimate(flops=int(flops), bytes_accessed=int(bytes_accessed), transcendentals=0)


def split(x):
    hi = x.astype(BF16)
    return hi, (x - hi.astype(F32)).astype(BF16)


def split3(x):
    hi = x.astype(BF16)
    rest = x - hi.astype(F32)
    mid = rest.astype(BF16)
    return hi, mid, (rest - mid.astype(F32)).astype(BF16)


def mm(a, b, dims):
    return lax.dot_general(a, b, dims, preferred_element_type=F32)


def mm3(a, b, dims):
    a_hi, a_lo = split(a)
    b_hi, b_lo = split(b)
    return mm(a_hi, b_hi, dims) + (mm(a_hi, b_lo, dims) + mm(a_lo, b_hi, dims))


def outer_sum(k, v):
    made = mm(jnp.concatenate(split(k), axis=1), jnp.concatenate(split(v), axis=1), TN)
    return made[:DH, :DH] + (made[:DH, DH:] + made[DH:, :DH])


def state_kernel(k_ref, v_ref, ld_ref, *refs):
    out_ref, fade_ref = refs[-2:]
    heads, tok = ld_ref.shape
    step = k_ref.shape[1] // DH
    i = pl.program_id(0)

    @pl.when(i == 0)
    def _():
        ld = ld_ref[...]
        later = lax.broadcasted_iota(jnp.int32, (tok, tok), 1) > lax.broadcasted_iota(jnp.int32, (tok, tok), 0)
        later = jnp.where(later, 1.0, 0.0).astype(BF16)
        made = mm(later, jnp.concatenate(split3(ld), axis=0), NT)
        fade = jnp.exp(made[:, :heads] + (made[:, heads : 2 * heads] + made[:, 2 * heads :]))
        for j in range(heads // step):
            fade_ref[j] = fade[:, j * step : (j + 1) * step]

    fade = fade_ref[i]
    for h in range(step):
        cols = pl.ds(h * DH, DH)
        out_ref[h, :DH, :] = outer_sum(k_ref[:, cols] * fade[:, h : h + 1], v_ref[:, cols])
        total = jnp.sum(ld_ref[pl.ds(i * step + h, 1), :], axis=1, keepdims=True)
        out_ref[h, DH:, :] = jnp.broadcast_to(total, (ROWS - DH, DH))


def own_state(keys, values, log_decay, group, heads, after=()):
    tok = keys.shape[0]
    step = 2
    steps = heads // step
    wide = pl.BlockSpec((tok, step * DH), lambda i: (0, group * steps + i))
    return pl.pallas_call(
        state_kernel,
        out_shape=jax.ShapeDtypeStruct((heads, ROWS, DH), F32),
        grid=(steps,),
        in_specs=[wide, wide, pl.BlockSpec((heads, tok), lambda i: (group, 0))] + [ANY] * len(after),
        out_specs=pl.BlockSpec((step, ROWS, DH), lambda i: (i, 0, 0)),
        scratch_shapes=[pltpu.VMEM((steps, tok, step), F32)],
        compiler_params=params(),
        cost_estimate=cost(8 * tok * heads * DH * DH, 8 * tok * heads * DH),
        name="own_state",
    )(keys, values, log_decay, *after)


def merge_kernel(bit, upper_ref, mine_ref, other_ref, *refs):
    out_ref = refs[-1]
    upper = upper_ref[bit] == 1
    for h in range(mine_ref.shape[0]):
        mine, other = mine_ref[h], other_ref[h]
        low = jnp.where(upper, other, mine)
        high = jnp.where(upper, mine, other)
        faded = jnp.exp(high[DH : DH + 1, :])
        out_ref[h, :DH, :] = faded * low[:DH] + high[:DH]
        out_ref[h, DH:, :] = low[DH:] + high[DH:]


def merged(bit, upper, mine, other, after=()):
    return pl.pallas_call(
        functools.partial(merge_kernel, bit),
        out_shape=jax.ShapeDtypeStruct(mine.shape, F32),
        in_specs=[SMEM, VMEM, VMEM] + [ANY] * len(after),
        out_specs=VMEM,
        compiler_params=params(16),
        cost_estimate=cost(3 * mine.size, 12 * mine.size),
        name="merge",
    )(upper, mine, other, *after)


def prepare_kernel(ld_ref, w_ref, *refs):
    sums_ref, cols_ref, weights_ref = refs[-3:]
    heads, tok = ld_ref.shape
    levels = w_ref.shape[1]
    chunks = tok // CHUNK
    near_levels = tok.bit_length()
    row = lax.broadcasted_iota(jnp.int32, (CHUNK, CHUNK), 0)
    col = lax.broadcasted_iota(jnp.int32, (CHUNK, CHUNK), 1)
    upto = jnp.where(row <= col, 1.0, 0.0).astype(BF16)
    sums = []
    for m in range(chunks):
        hi, mid, low = split3(ld_ref[:, m * CHUNK : (m + 1) * CHUNK])
        sums.append(mm(hi, upto, NN) + (mm(mid, upto, NN) + mm(low, upto, NN)))
    start = jnp.zeros((heads, 1), F32)
    fulls = []
    halves = []
    for m in range(chunks):
        fulls.append(sums[m] + start)
        halves.append(sums[m] + (sums[m - 1][:, CHUNK - 1 :] if m % 4 == 3 else 0.0))
        start = start + sums[m][:, CHUNK - 1 :]
    cum = jnp.concatenate(sums, axis=1)
    one = jnp.exp(cum)
    two = jnp.exp(jnp.concatenate(halves, axis=1))
    far = jnp.exp(jnp.concatenate(fulls, axis=1))
    for h in range(heads):
        sums_ref[h] = cum[h : h + 1]
    fill = jnp.zeros((CHUNK - heads, tok), F32)
    cols_ref[...] = jnp.transpose(jnp.concatenate([cum, fill], axis=0))
    level = lax.broadcasted_iota(jnp.int32, (levels, tok), 0)
    per = CHUNK // levels
    for g in range(heads // per):
        made = []
        for h in range(g * per, (g + 1) * per):
            decay = jnp.where(level >= near_levels, far[h : h + 1], two[h : h + 1])
            decay = jnp.where(level == near_levels - 2, one[h : h + 1], decay)
            decay = jnp.where(level < near_levels - 2, 1.0, decay)
            made.append(w_ref[h] * decay)
        weights_ref[:, g * CHUNK : (g + 1) * CHUNK] = jnp.transpose(jnp.concatenate(made, axis=0))


def prepare(log_decay, level_weights, after=()):
    heads, tok = log_decay.shape
    levels = level_weights.shape[1]
    return pl.pallas_call(
        prepare_kernel,
        out_shape=(
            jax.ShapeDtypeStruct((heads, 1, tok), F32),
            jax.ShapeDtypeStruct((tok, CHUNK), F32),
            jax.ShapeDtypeStruct((tok, heads * levels), F32),
        ),
        in_specs=[VMEM, VMEM] + [ANY] * len(after),
        out_specs=[VMEM] * 3,
        compiler_params=params(),
        cost_estimate=cost(0, 8 * heads * levels * tok),
        name="prepare",
    )(log_decay, level_weights, *after)


def near_kernel(first, levels, q_ref, k_ref, v_ref, sums_ref, cols_ref, w_ref, *refs):
    out_ref, token_ref = refs[-2:]
    tok = q_ref.shape[0]
    chunks = tok // CHUNK
    tile_bits = CHUNK.bit_length() - 1
    row = lax.broadcasted_iota(jnp.int32, (CHUNK, CHUNK), 0)
    col = lax.broadcasted_iota(jnp.int32, (CHUNK, CHUNK), 1)
    apart = row ^ col
    causal = row >= col
    head = first + pl.program_id(0)
    per = CHUNK // levels
    token_ref[...] = jnp.zeros_like(token_ref)
    states = []
    ends = []
    for m in range(chunks):
        rows = pl.ds(m * CHUNK, CHUNK)
        q = q_ref[rows, :] * DH**-0.5
        k = k_ref[rows, :]
        v = v_ref[rows, :]
        w = pltpu.roll(w_ref[rows, :], (per - head % per) * levels, 1)
        c_cols = pltpu.roll(cols_ref[rows, :], CHUNK - head, 1)
        c = c_cols[:, 0:1]
        near = jnp.broadcast_to(w[:, 0:1], (CHUNK, CHUNK))
        for bit in range(tile_bits):
            near = jnp.where(apart >= 2**bit, w[:, bit + 1 : bit + 2], near)
        gap = jnp.where(causal, c - sums_ref[0, :, m * CHUNK : (m + 1) * CHUNK], -1e30)
        q_hi, q_lo = split(q)
        k_hi, k_lo = split(k)
        q_both = jnp.concatenate([q_hi, q_lo], axis=1)
        scores = mm(q_both, jnp.concatenate([k_hi, k_hi], axis=1), NT) + mm(q_hi, k_lo, NT)
        scores = scores * (near * jnp.exp(gap))
        s_hi, s_lo = split(scores)
        v_hi, v_lo = split(v)
        s_both = jnp.concatenate([s_hi, s_lo], axis=1)
        out = mm(s_both, jnp.concatenate([v_hi, v_hi], axis=0), NN) + mm(s_hi, v_lo, NN)
        for bit in range(2):
            if m >> bit & 1:
                at = (m >> bit) - 1 << bit
                seen = states[at]
                for n in range(at + 1, at + 2**bit):
                    seen = jnp.exp(ends[n]) * seen + states[n]
                level = tile_bits + 1 + bit
                s_hi, s_lo = split(seen)
                made = mm(q_both, jnp.concatenate([s_hi, s_hi], axis=0), NN) + mm(q_hi, s_lo, NN)
                out = out + w[:, level : level + 1] * made
        out_ref[rows, :] = out
        if m < chunks - 1:
            end = c[CHUNK - 1 : CHUNK]
            states.append(outer_sum(k * jnp.exp(end - c), v))
            ends.append(end)


def near_part(queries, keys, values, sums, cols, weights, levels, first, heads, so_far=None, after=()):
    tok = queries.shape[0]
    per = CHUNK // levels
    one = pl.BlockSpec((tok, DH), lambda h: (0, first + h))
    more = [] if so_far is None else [so_far]
    return pl.pallas_call(
        functools.partial(near_kernel, first, levels),
        out_shape=(
            jax.ShapeDtypeStruct(queries.shape, F32),
            jax.ShapeDtypeStruct((8, CHUNK), F32),
        ),
        grid=(heads,),
        in_specs=[
            one,
            one,
            one,
            pl.BlockSpec((1, 1, tok), lambda h: (first + h, 0, 0)),
            pl.BlockSpec(cols.shape, lambda h: (0, 0)),
            pl.BlockSpec((tok, CHUNK), lambda h: (0, (first + h) // per)),
        ]
        + [ANY] * (len(more) + len(after)),
        out_specs=[one, pl.BlockSpec((8, CHUNK), lambda h: (0, 0))],
        input_output_aliases={6: 0} if more else {},
        compiler_params=params(),
        cost_estimate=cost(60 * tok * heads * DH * DH, 16 * tok * heads * DH),
        name="near",
    )(queries, keys, values, sums, cols, weights, *more, *after)


def far_kernel(first, levels, skip, last, count, upper_ref, q_ref, near_ref, w_ref, gain_ref, *refs):
    step = q_ref.shape[1] // DH
    outs = 3 if last else 2
    out_refs, token_ref = refs[-outs:-1], refs[-1]
    per = CHUNK // levels
    total = upper_ref.shape[0]
    head = first + pl.program_id(0) * step
    token_ref[...] = jnp.zeros_like(token_ref)
    w = pltpu.roll(w_ref[...], (per - head % per) * levels, 1)
    for h in range(step):
        cols = pl.ds(h * DH, DH)
        q_hi, q_lo = split(q_ref[:, cols] * DH**-0.5)
        out = near_ref[:, cols]
        before = jnp.zeros((1, DH), F32)
        used = []
        states = []
        for level in range(count):
            ref = refs[level]
            upper = upper_ref[level] == 1
            end = ref.shape[1] - (ROWS - DH)
            if level >= skip:
                reach = jnp.where(upper, jnp.exp(before), 0.0)
                hi, lo = split(ref[h, :DH, :] * reach)
                states.append(jnp.concatenate([hi, hi, lo], axis=0))
                used.append(h * levels + levels - total + level)
            before = before + jnp.where(upper, ref[h, end : end + 1, :], 0.0)
        made = mm(jnp.concatenate([q_hi, q_lo, q_hi], axis=1), jnp.concatenate(states, axis=1), NN)
        for n, at in enumerate(used):
            out = out + w[:, at : at + 1] * made[:, n * DH : (n + 1) * DH]
        if last:
            squares = jnp.concatenate(split(out * out), axis=1)
            mean = mm(squares, jnp.full((2 * DH, DH), 1.0 / DH, BF16), NN)
            out = out * lax.rsqrt(mean + 1e-06) * gain_ref[:, cols]
            hi, lo = split(out)
            out_refs[0][:, cols] = hi
            out_refs[1][:, cols] = lo
        else:
            out_refs[0][:, cols] = out


def far_part(upper, queries, so_far, at, weights, levels, gain, states, first, skip, last, after=()):
    heads = states[0].shape[0]
    tok = queries.shape[0]
    per = CHUNK // levels
    step = 2
    out = jax.ShapeDtypeStruct((tok, heads * DH), BF16 if last else F32)
    outs = 2 if last else 1
    tail = ROWS - DH
    return pl.pallas_call(
        functools.partial(far_kernel, first, levels, skip, last, len(states)),
        out_shape=(out,) * outs + (jax.ShapeDtypeStruct((8, CHUNK), F32),),
        grid=(heads // step,),
        in_specs=[
            SMEM,
            pl.BlockSpec((tok, step * DH), lambda i: (0, first // step + i)),
            pl.BlockSpec((tok, step * DH), lambda i: (0, at // step + i)),
            pl.BlockSpec((tok, CHUNK), lambda i: (0, (first + i * step) // per)),
            pl.BlockSpec((1, step * DH), lambda i: (0, first // step + i)),
        ]
        + [
            pl.BlockSpec((step, ROWS, DH), lambda i: (i, 0, 0))
            if level >= skip
            else pl.BlockSpec((step, tail, DH), lambda i: (i, DH // tail, 0))
            for level in range(len(states))
        ]
        + [ANY] * len(after),
        out_specs=[pl.BlockSpec((tok, step * DH), lambda i: (0, i))] * outs
        + [pl.BlockSpec((8, CHUNK), lambda i: (0, 0))],
        compiler_params=params(),
        cost_estimate=cost(8 * len(states) * tok * heads * DH * DH, 16 * tok * heads * DH),
        name="far",
    )(upper, queries, so_far, weights, gain, *states, *after)


def project_kernel(has_more, side_ref, hi_ref, lo_ref, w_ref, *refs):
    out_ref = refs[-1]
    w_hi, w_lo = split(w_ref[...])
    x_hi, x_lo = hi_ref[...], lo_ref[...]
    made = mm(x_hi, w_hi, NT) + (mm(x_hi, w_lo, NT) + mm(x_lo, w_hi, NT))
    if has_more:
        made = made + refs[0][...]
    out_ref[...] = made


def project(side, x_hi, x_lo, weight, part, sides, so_far=None, after=()):
    tok, depth = x_hi.shape
    width = weight.shape[0] // sides
    tile = 256
    steps = width // tile
    whole = pl.BlockSpec((tok, depth), lambda i, side: (0, 0))
    moving = pl.BlockSpec((tok, tile), lambda i, side: (0, i))
    more = [] if so_far is None else [so_far]
    return pl.pallas_call(
        functools.partial(project_kernel, bool(more)),
        out_shape=jax.ShapeDtypeStruct((tok, width), F32),
        grid_spec=pltpu.PrefetchScalarGridSpec(
            num_scalar_prefetch=1,
            grid=(steps,),
            in_specs=[
                whole,
                whole,
                pl.BlockSpec((tile, depth), lambda i, side: (side[0] * steps + i, part)),
            ]
            + [moving] * len(more)
            + [ANY] * len(after),
            out_specs=moving,
        ),
        compiler_params=params(),
        cost_estimate=cost(6 * tok * depth * width, 4 * (depth * width + 2 * tok * width)),
        name="project",
    )(side, x_hi, x_lo, weight, *more, *after)


def local(queries, keys, values, log_decay, level_weights, norm_gain, out_weight):
    head_count = log_decay.shape[0]
    levels = level_weights.shape[1]
    n_seq = lax.axis_size("seq")
    sides = lax.axis_size("head")
    seq_bits = n_seq.bit_length() - 1
    seq_index = lax.axis_index("seq")
    size = head_count // 2

    weight = lax.all_gather(out_weight.T, "seq", axis=0, tiled=True)
    upper = (seq_index >> jnp.arange(seq_bits, dtype=jnp.int32)) & 1
    gain = norm_gain.reshape(1, -1)

    def send(block, bit):
        def wanted(s):
            above = s >> bit
            return not (bit == seq_bits - 1 and above & 1) and not (bit == seq_bits - 2 and above == 3)

        flip = 3 << bit - 1 if bit % 2 else 1 << bit
        return lax.ppermute(block, "seq", [(s, s ^ flip) for s in range(n_seq) if wanted(s)])

    small = size // 2
    early = 4

    def near(n, so_far, *after):
        return near_part(
            queries, keys, values, sums, cols, weights, levels, n * small, small, so_far, after
        )

    def far(so_far, at, states, group, skip, last, *after):
        return far_part(
            upper, queries, so_far, at, weights, levels, gain, states, group * size, skip, last, after
        )

    a, came_a, b, came_b = [], [], [], []

    def go(blocks, came, *after):
        bit = len(blocks) - 1
        blocks.append(merged(bit, upper, blocks[bit], came[bit], after))
        came.append(send(blocks[-1], bit + 1))

    a.append(own_state(keys, values, log_decay, 0, size))
    came_a.append(send(a[0], 0))
    sums, cols, weights = prepare(log_decay, level_weights, (a[0],))
    close, token = near(0, None)
    go(a, came_a, token)
    b.append(own_state(keys, values, log_decay, 1, size, (a[1],)))
    came_b.append(send(b[0], 0))
    close, token = near(1, close, b[0])
    go(a, came_a, token)
    go(b, came_b, a[2])
    close, token = near(2, close, b[1])
    go(a, came_a, token)
    go(b, came_b, a[3])
    close, token = near(3, close, b[2])
    go(a, came_a, token)
    go(b, came_b, a[4])
    far_a, token = far(close, 0, came_a[:early], 0, 0, False, b[3])
    go(a, came_a, token)
    go(b, came_b, a[5])
    far_b, token = far(close, size, came_b[:early], 1, 0, False, b[4])
    go(b, came_b, token)
    a_hi, a_lo, _ = far(far_a, 0, came_a, 0, early, True, b[5])

    me = lax.axis_index("head").astype(jnp.int32)
    mine = me.reshape(1)
    theirs = (sides - 1 - me).reshape(1)
    to_send = project(theirs, a_hi, a_lo, weight, 0, sides)
    b_hi, b_lo, token = far(far_b, 0, came_b, 1, early, True, to_send)
    to_send = project(theirs, b_hi, b_lo, weight, 1, sides, to_send)
    came = lax.ppermute(to_send, "head", [(s, sides - 1 - s) for s in range(sides)])
    to_keep = project(mine, a_hi, a_lo, weight, 0, sides, None, (to_send,))
    to_keep = project(mine, b_hi, b_lo, weight, 1, sides, to_keep)
    return to_keep + came


def solution(mesh):
    return jax.shard_map(
        local,
        mesh=mesh,
        in_specs=(
            P("seq", "head"),
            P("seq", "head"),
            P("seq", "head"),
            P("head", "seq"),
            P("head", None, "seq"),
            P("head"),
            P("head", "seq"),
        ),
        out_specs=P("seq", "head"),
        check_vma=False,
    )
```

```python
import functools

import jax
import jax.numpy as jnp
from jax import lax
from jax.experimental import pallas as pl
from jax.experimental.pallas import tpu as pltpu
from jax.sharding import PartitionSpec as P

HIGH = lax.Precision.HIGHEST
DH = 128
CHUNK = 128
ROWS = DH + 8
F32 = jnp.float32
BF16 = jnp.bfloat16
NT = (((1,), (1,)), ((), ()))
TN = (((0,), (0,)), ((), ()))
NN = (((1,), (0,)), ((), ()))
ANY = pl.BlockSpec(memory_space=pl.ANY)
VMEM = pl.BlockSpec(memory_space=pltpu.VMEM)
SMEM = pl.BlockSpec(memory_space=pltpu.SMEM)


def params(mib=52):
    return pltpu.CompilerParams(vmem_limit_bytes=mib * 2**20)


def cost(flops, bytes_accessed):
    return pl.CostEstimate(flops=int(flops), bytes_accessed=int(bytes_accessed), transcendentals=0)


def split(x):
    hi = x.astype(BF16)
    return hi, (x - hi.astype(F32)).astype(BF16)


def split3(x):
    hi = x.astype(BF16)
    rest = x - hi.astype(F32)
    mid = rest.astype(BF16)
    return hi, mid, (rest - mid.astype(F32)).astype(BF16)


def mm(a, b, dims):
    return lax.dot_general(a, b, dims, preferred_element_type=F32)


def mm3(a, b, dims):
    a_hi, a_lo = split(a)
    b_hi, b_lo = split(b)
    return mm(a_hi, b_hi, dims) + (mm(a_hi, b_lo, dims) + mm(a_lo, b_hi, dims))


def outer_sum(k, v):
    made = mm(jnp.concatenate(split(k), axis=1), jnp.concatenate(split(v), axis=1), TN)
    return made[:DH, :DH] + (made[:DH, DH:] + made[DH:, :DH])


def state_kernel(k_ref, v_ref, ld_ref, *refs):
    out_ref, fade_ref = refs[-2:]
    heads, tok = ld_ref.shape
    step = k_ref.shape[1] // DH
    i = pl.program_id(0)

    @pl.when(i == 0)
    def _():
        ld = ld_ref[...]
        later = lax.broadcasted_iota(jnp.int32, (tok, tok), 1) > lax.broadcasted_iota(jnp.int32, (tok, tok), 0)
        later = jnp.where(later, 1.0, 0.0).astype(BF16)
        made = mm(later, jnp.concatenate(split3(ld), axis=0), NT)
        fade = jnp.exp(made[:, :heads] + (made[:, heads : 2 * heads] + made[:, 2 * heads :]))
        for j in range(heads // step):
            fade_ref[j] = fade[:, j * step : (j + 1) * step]

    fade = fade_ref[i]
    for h in range(step):
        cols = pl.ds(h * DH, DH)
        out_ref[h, :DH, :] = outer_sum(k_ref[:, cols] * fade[:, h : h + 1], v_ref[:, cols])
        total = jnp.sum(ld_ref[pl.ds(i * step + h, 1), :], axis=1, keepdims=True)
        out_ref[h, DH:, :] = jnp.broadcast_to(total, (ROWS - DH, DH))


def own_state(keys, values, log_decay, group, heads, after=()):
    tok = keys.shape[0]
    step = 2
    steps = heads // step
    wide = pl.BlockSpec((tok, step * DH), lambda i: (0, group * steps + i))
    return pl.pallas_call(
        state_kernel,
        out_shape=jax.ShapeDtypeStruct((heads, ROWS, DH), F32),
        grid=(steps,),
        in_specs=[wide, wide, pl.BlockSpec((heads, tok), lambda i: (group, 0))] + [ANY] * len(after),
        out_specs=pl.BlockSpec((step, ROWS, DH), lambda i: (i, 0, 0)),
        scratch_shapes=[pltpu.VMEM((steps, tok, step), F32)],
        compiler_params=params(),
        cost_estimate=cost(8 * tok * heads * DH * DH, 8 * tok * heads * DH),
        name="own_state",
    )(keys, values, log_decay, *after)


def merge_kernel(bit, upper_ref, mine_ref, other_ref, *refs):
    out_ref = refs[-1]
    upper = upper_ref[bit] == 1
    for h in range(mine_ref.shape[0]):
        mine, other = mine_ref[h], other_ref[h]
        low = jnp.where(upper, other, mine)
        high = jnp.where(upper, mine, other)
        faded = jnp.exp(high[DH : DH + 1, :])
        out_ref[h, :DH, :] = faded * low[:DH] + high[:DH]
        out_ref[h, DH:, :] = low[DH:] + high[DH:]


def merged(bit, upper, mine, other, after=()):
    return pl.pallas_call(
        functools.partial(merge_kernel, bit),
        out_shape=jax.ShapeDtypeStruct(mine.shape, F32),
        in_specs=[SMEM, VMEM, VMEM] + [ANY] * len(after),
        out_specs=VMEM,
        compiler_params=params(16),
        cost_estimate=cost(3 * mine.size, 12 * mine.size),
        name="merge",
    )(upper, mine, other, *after)


def prepare_kernel(ld_ref, w_ref, *refs):
    sums_ref, cols_ref, weights_ref = refs[-3:]
    heads, tok = ld_ref.shape
    levels = w_ref.shape[1]
    chunks = tok // CHUNK
    near_levels = tok.bit_length()
    row = lax.broadcasted_iota(jnp.int32, (CHUNK, CHUNK), 0)
    col = lax.broadcasted_iota(jnp.int32, (CHUNK, CHUNK), 1)
    upto = jnp.where(row <= col, 1.0, 0.0).astype(BF16)
    sums = []
    for m in range(chunks):
        hi, mid, low = split3(ld_ref[:, m * CHUNK : (m + 1) * CHUNK])
        sums.append(mm(hi, upto, NN) + (mm(mid, upto, NN) + mm(low, upto, NN)))
    start = jnp.zeros((heads, 1), F32)
    fulls = []
    halves = []
    for m in range(chunks):
        fulls.append(sums[m] + start)
        halves.append(sums[m] + (sums[m - 1][:, CHUNK - 1 :] if m % 4 == 3 else 0.0))
        start = start + sums[m][:, CHUNK - 1 :]
    cum = jnp.concatenate(sums, axis=1)
    one = jnp.exp(cum)
    two = jnp.exp(jnp.concatenate(halves, axis=1))
    far = jnp.exp(jnp.concatenate(fulls, axis=1))
    for h in range(heads):
        sums_ref[h] = cum[h : h + 1]
    fill = jnp.zeros((CHUNK - heads, tok), F32)
    cols_ref[...] = jnp.transpose(jnp.concatenate([cum, fill], axis=0))
    level = lax.broadcasted_iota(jnp.int32, (levels, tok), 0)
    per = CHUNK // levels
    for g in range(heads // per):
        made = []
        for h in range(g * per, (g + 1) * per):
            decay = jnp.where(level >= near_levels, far[h : h + 1], two[h : h + 1])
            decay = jnp.where(level == near_levels - 2, one[h : h + 1], decay)
            decay = jnp.where(level < near_levels - 2, 1.0, decay)
            made.append(w_ref[h] * decay)
        weights_ref[:, g * CHUNK : (g + 1) * CHUNK] = jnp.transpose(jnp.concatenate(made, axis=0))


def prepare(log_decay, level_weights, after=()):
    heads, tok = log_decay.shape
    levels = level_weights.shape[1]
    return pl.pallas_call(
        prepare_kernel,
        out_shape=(
            jax.ShapeDtypeStruct((heads, 1, tok), F32),
            jax.ShapeDtypeStruct((tok, CHUNK), F32),
            jax.ShapeDtypeStruct((tok, heads * levels), F32),
        ),
        in_specs=[VMEM, VMEM] + [ANY] * len(after),
        out_specs=[VMEM] * 3,
        compiler_params=params(),
        cost_estimate=cost(0, 8 * heads * levels * tok),
        name="prepare",
    )(log_decay, level_weights, *after)


def near_kernel(first, levels, q_ref, k_ref, v_ref, sums_ref, cols_ref, w_ref, *refs):
    out_ref, token_ref = refs[-2:]
    tok = q_ref.shape[0]
    chunks = tok // CHUNK
    tile_bits = CHUNK.bit_length() - 1
    row = lax.broadcasted_iota(jnp.int32, (CHUNK, CHUNK), 0)
    col = lax.broadcasted_iota(jnp.int32, (CHUNK, CHUNK), 1)
    apart = row ^ col
    causal = row >= col
    head = first + pl.program_id(0)
    per = CHUNK // levels
    token_ref[...] = jnp.zeros_like(token_ref)
    states = []
    ends = []
    for m in range(chunks):
        rows = pl.ds(m * CHUNK, CHUNK)
        q = q_ref[rows, :] * DH**-0.5
        k = k_ref[rows, :]
        v = v_ref[rows, :]
        w = pltpu.roll(w_ref[rows, :], (per - head % per) * levels, 1)
        c_cols = pltpu.roll(cols_ref[rows, :], CHUNK - head, 1)
        c = c_cols[:, 0:1]
        near = jnp.broadcast_to(w[:, 0:1], (CHUNK, CHUNK))
        for bit in range(tile_bits):
            near = jnp.where(apart >= 2**bit, w[:, bit + 1 : bit + 2], near)
        gap = jnp.where(causal, c - sums_ref[0, :, m * CHUNK : (m + 1) * CHUNK], -1e30)
        q_hi, q_lo = split(q)
        k_hi, k_lo = split(k)
        q_both = jnp.concatenate([q_hi, q_lo], axis=1)
        scores = mm(q_both, jnp.concatenate([k_hi, k_hi], axis=1), NT) + mm(q_hi, k_lo, NT)
        scores = scores * (near * jnp.exp(gap))
        s_hi, s_lo = split(scores)
        v_hi, v_lo = split(v)
        s_both = jnp.concatenate([s_hi, s_lo], axis=1)
        out = mm(s_both, jnp.concatenate([v_hi, v_hi], axis=0), NN) + mm(s_hi, v_lo, NN)
        for bit in range(2):
            if m >> bit & 1:
                at = (m >> bit) - 1 << bit
                seen = states[at]
                for n in range(at + 1, at + 2**bit):
                    seen = jnp.exp(ends[n]) * seen + states[n]
                level = tile_bits + 1 + bit
                s_hi, s_lo = split(seen)
                made = mm(q_both, jnp.concatenate([s_hi, s_hi], axis=0), NN) + mm(q_hi, s_lo, NN)
                out = out + w[:, level : level + 1] * made
        out_ref[rows, :] = out
        if m < chunks - 1:
            end = c[CHUNK - 1 : CHUNK]
            states.append(outer_sum(k * jnp.exp(end - c), v))
            ends.append(end)


def near_part(queries, keys, values, sums, cols, weights, levels, first, heads, so_far=None, after=()):
    tok = queries.shape[0]
    per = CHUNK // levels
    one = pl.BlockSpec((tok, DH), lambda h: (0, first + h))
    more = [] if so_far is None else [so_far]
    return pl.pallas_call(
        functools.partial(near_kernel, first, levels),
        out_shape=(
            jax.ShapeDtypeStruct(queries.shape, F32),
            jax.ShapeDtypeStruct((8, CHUNK), F32),
        ),
        grid=(heads,),
        in_specs=[
            one,
            one,
            one,
            pl.BlockSpec((1, 1, tok), lambda h: (first + h, 0, 0)),
            pl.BlockSpec(cols.shape, lambda h: (0, 0)),
            pl.BlockSpec((tok, CHUNK), lambda h: (0, (first + h) // per)),
        ]
        + [ANY] * (len(more) + len(after)),
        out_specs=[one, pl.BlockSpec((8, CHUNK), lambda h: (0, 0))],
        input_output_aliases={6: 0} if more else {},
        compiler_params=params(),
        cost_estimate=cost(60 * tok * heads * DH * DH, 16 * tok * heads * DH),
        name="near",
    )(queries, keys, values, sums, cols, weights, *more, *after)


def add_levels(q_hi, q_lo, out, w, first_column, states):
    parts = []
    for state in states:
        hi, lo = split(state)
        parts.append(jnp.concatenate([hi, hi, lo], axis=0))
    made = mm(jnp.concatenate([q_hi, q_lo, q_hi], axis=1), jnp.concatenate(parts, axis=1), NN)
    for n in range(len(parts)):
        at = first_column + n
        out = out + w[:, at : at + 1] * made[:, n * DH : (n + 1) * DH]
    return out


def early_kernel(first, levels, count, upper_ref, q_ref, near_ref, w_ref, *refs):
    out_ref, before_ref = refs[-2:]
    step = q_ref.shape[1] // DH
    per = CHUNK // levels
    total = upper_ref.shape[0]
    head = first + pl.program_id(0) * step
    w = pltpu.roll(w_ref[...], (per - head % per) * levels, 1)
    for h in range(step):
        cols = pl.ds(h * DH, DH)
        q_hi, q_lo = split(q_ref[:, cols] * DH**-0.5)
        before = jnp.zeros((1, DH), F32)
        states = []
        for level in range(count):
            upper = upper_ref[level] == 1
            reach = jnp.where(upper, jnp.exp(before), 0.0)
            states.append(refs[level][h, :DH, :] * reach)
            before = before + jnp.where(upper, refs[level][h, DH : DH + 1, :], 0.0)
        out_ref[:, cols] = add_levels(q_hi, q_lo, near_ref[:, cols], w, h * levels + levels - total, states)
        before_ref[h] = jnp.broadcast_to(before, before_ref.shape[1:])


def early_levels(upper, queries, near, weights, levels, states, first, after=()):
    heads = states[0].shape[0]
    tok = queries.shape[0]
    per = CHUNK // levels
    step = 2
    wide = pl.BlockSpec((tok, step * DH), lambda i: (0, first // step + i))
    return pl.pallas_call(
        functools.partial(early_kernel, first, levels, len(states)),
        out_shape=(
            jax.ShapeDtypeStruct((tok, heads * DH), F32),
            jax.ShapeDtypeStruct((heads, 8, DH), F32),
        ),
        grid=(heads // step,),
        in_specs=[
            SMEM,
            wide,
            wide,
            pl.BlockSpec((tok, CHUNK), lambda i: (0, (first + i * step) // per)),
        ]
        + [pl.BlockSpec((step, ROWS, DH), lambda i: (i, 0, 0))] * len(states)
        + [ANY] * len(after),
        out_specs=[
            pl.BlockSpec((tok, step * DH), lambda i: (0, i)),
            pl.BlockSpec((step, 8, DH), lambda i: (i, 0, 0)),
        ],
        compiler_params=params(),
        cost_estimate=cost(8 * len(states) * tok * heads * DH * DH, 16 * tok * heads * DH),
        name="early",
    )(upper, queries, near, weights, *states, *after)


TILE = 256


def tile_copy(side, steps, part, j, w_ref, buffer_ref, sems, slot):
    depth = buffer_ref.shape[2]
    rows = pl.ds(pl.multiple_of((side * steps + j) * TILE, TILE), TILE)
    return pltpu.make_async_copy(
        w_ref.at[rows, pl.ds(part * depth, depth)], buffer_ref.at[slot], sems.at[slot]
    )


def project_tiles(side, steps, part, w_ref, buffer_ref, sems, slot, x_hi, x_lo, more_ref, out_ref):
    @pl.loop(0, steps)
    def _(j):
        tile_copy(side, steps, part, j, w_ref, buffer_ref, sems, slot + j).wait()
        w_hi, w_lo = split(buffer_ref[slot + j])
        cols = pl.ds(pl.multiple_of(j * TILE, TILE), TILE)
        made = mm(x_hi[...], w_hi, NT) + (mm(x_hi[...], w_lo, NT) + mm(x_lo[...], w_hi, NT))
        if more_ref is not None:
            made = made + more_ref[:, cols]
        out_ref[:, cols] = made


def finish_kernel(first, levels, skip, both, more, sides_ref, upper_ref, q_ref, near_ref, before_ref, *refs):
    w_ref, gain_ref, *refs = refs
    total = upper_ref.shape[0]
    states, weight_ref, refs = refs[: total - skip], refs[total - skip], refs[total - skip + 1 :]
    more_ref = refs[0] if more else None
    send_ref, second, third, buffer_ref, sems, q_buffer, q_sems = refs[-7:]
    x_hi, x_lo = (refs[-9:-7]) if both else (second, third)
    heads = states[0].shape[0]
    steps = send_ref.shape[1] // TILE
    part = first // heads
    pair = 2

    def q_copy(n):
        cols = pl.ds(pl.multiple_of((first + n * pair) * DH, pair * DH), pair * DH)
        return pltpu.make_async_copy(q_ref.at[:, cols], q_buffer.at[n], q_sems.at[n])

    for n in range(heads // pair):
        q_copy(n).start()
    used = 2 if both else 1
    for side in range(used):
        for j in range(steps):
            tile_copy(sides_ref[side], steps, part, j, weight_ref, buffer_ref, sems, side * steps + j).start()

    per = CHUNK // levels

    @pl.loop(0, heads // pair)
    def _(n):
        q_copy(n).wait()
        group = pl.multiple_of((first + n * pair) // per * CHUNK, CHUNK)
        w = pltpu.roll(w_ref[:, pl.ds(group, CHUNK)], (per - (first + n * pair) % per) * levels, 1)
        for i in range(pair):
            h = n * pair + i
            cols = pl.ds(pl.multiple_of(h * DH, DH), DH)
            all_cols = pl.ds(pl.multiple_of((first + h) * DH, DH), DH)
            q_hi, q_lo = split(q_buffer[n, :, i * DH : (i + 1) * DH] * DH**-0.5)
            before = before_ref[h, 0:1, :]
            scaled = []
            for m, ref in enumerate(states):
                upper = upper_ref[skip + m] == 1
                scaled.append(ref[h, :DH, :] * jnp.where(upper, jnp.exp(before), 0.0))
                before = before + jnp.where(upper, ref[h, DH : DH + 1, :], 0.0)
            column = i * levels + levels - total + skip
            out = add_levels(q_hi, q_lo, near_ref[:, cols], w, column, scaled)
            squares = jnp.concatenate(split(out * out), axis=1)
            mean = mm(squares, jnp.full((2 * DH, DH), 1.0 / DH, BF16), NN)
            out = out * lax.rsqrt(mean + 1e-06) * gain_ref[:, all_cols]
            hi, lo = split(out)
            x_hi[:, cols] = hi
            x_lo[:, cols] = lo

    project_tiles(
        sides_ref[0], steps, part, weight_ref, buffer_ref, sems, 0, x_hi, x_lo, more_ref, send_ref
    )
    if both:
        project_tiles(
            sides_ref[1], steps, part, weight_ref, buffer_ref, sems, steps, x_hi, x_lo, None, second
        )


def finish(sides, upper, queries, near, before, weights, levels, gain, states, weight, first, both, more=None):
    heads = states[0].shape[0]
    tok = queries.shape[0]
    width = weight.shape[0] // 2
    depth = heads * DH
    skip = upper.shape[0] - len(states)
    used = 2 if both else 1
    tiles = used * width // TILE
    sums = jax.ShapeDtypeStruct((tok, width), F32)
    half = jax.ShapeDtypeStruct((tok, depth), BF16)
    extra = [] if more is None else [more]
    kept = [pltpu.VMEM((tok, depth), BF16)] * 2 if both else []
    third = [] if both else [half]

    def body(*refs):
        if both:
            ins = refs[: 8 + len(states) + len(extra)]
            send, keep, hi, lo, *scratch = refs[len(ins) :]
            finish_kernel(first, levels, skip, both, bool(extra), *ins, hi, lo, send, keep, None, *scratch)
        else:
            finish_kernel(first, levels, skip, both, bool(extra), *refs)

    return pl.pallas_call(
        body,
        out_shape=[sums] + ([sums] if both else [half]) + third,
        in_specs=[SMEM, SMEM, ANY] + [VMEM] * (4 + len(states)) + [ANY] + [VMEM] * len(extra),
        out_specs=[VMEM] * (2 + len(third)),
        scratch_shapes=kept
        + [
            pltpu.VMEM((tiles, TILE, depth), F32),
            pltpu.SemaphoreType.DMA((tiles,)),
            pltpu.VMEM((heads // 2, tok, 2 * DH), F32),
            pltpu.SemaphoreType.DMA((heads // 2,)),
        ],
        compiler_params=params(44),
        cost_estimate=cost(6 * tok * depth * width * used, 4 * depth * width * used + 16 * tok * depth),
        name="finish",
    )(sides, upper, queries, near, before, weights, gain, *states, weight, *extra)


def project_kernel(part, sides_ref, x_hi, x_lo, weight_ref, more_ref, *refs):
    out_ref, buffer_ref, sems = refs[-3:]
    steps = out_ref.shape[1] // TILE
    for j in range(steps):
        tile_copy(sides_ref[1], steps, part, j, weight_ref, buffer_ref, sems, j).start()
    project_tiles(sides_ref[1], steps, part, weight_ref, buffer_ref, sems, 0, x_hi, x_lo, more_ref, out_ref)


def project(sides, x_hi, x_lo, weight, part, more, after=()):
    tok, depth = x_hi.shape
    width = weight.shape[0] // 2
    return pl.pallas_call(
        functools.partial(project_kernel, part),
        out_shape=jax.ShapeDtypeStruct((tok, width), F32),
        in_specs=[SMEM, VMEM, VMEM, ANY, VMEM] + [ANY] * len(after),
        out_specs=VMEM,
        scratch_shapes=[
            pltpu.VMEM((width // TILE, TILE, depth), F32),
            pltpu.SemaphoreType.DMA((width // TILE,)),
        ],
        compiler_params=params(44),
        cost_estimate=cost(6 * tok * depth * width, 4 * (depth * width + 2 * tok * width)),
        name="project",
    )(sides, x_hi, x_lo, weight, more, *after)


def local(queries, keys, values, log_decay, level_weights, norm_gain, out_weight):
    head_count = log_decay.shape[0]
    levels = level_weights.shape[1]
    n_seq = lax.axis_size("seq")
    sides = lax.axis_size("head")
    seq_bits = n_seq.bit_length() - 1
    seq_index = lax.axis_index("seq")
    size = head_count // 2

    weight = lax.all_gather(out_weight.T, "seq", axis=0, tiled=True)
    upper = (seq_index >> jnp.arange(seq_bits, dtype=jnp.int32)) & 1
    gain = norm_gain.reshape(1, -1)

    def send(block, bit):
        def wanted(s):
            above = s >> bit
            return not (bit == seq_bits - 1 and above & 1) and not (bit == seq_bits - 2 and above == 3)

        flip = 3 << bit - 1 if bit % 2 else 1 << bit
        return lax.ppermute(block, "seq", [(s, s ^ flip) for s in range(n_seq) if wanted(s)])

    small = size // 2
    early = 4

    def near(n, so_far, *after):
        return near_part(
            queries, keys, values, sums, cols, weights, levels, n * small, small, so_far, after
        )

    def first_levels(group, states, *after):
        return early_levels(upper, queries, close, weights, levels, states, group * size, after)

    a, came_a, b, came_b = [], [], [], []

    def go(blocks, came, *after):
        bit = len(blocks) - 1
        blocks.append(merged(bit, upper, blocks[bit], came[bit], after))
        came.append(send(blocks[-1], bit + 1))

    a.append(own_state(keys, values, log_decay, 0, size))
    came_a.append(send(a[0], 0))
    sums, cols, weights = prepare(log_decay, level_weights, (a[0],))
    close, token = near(0, None)
    go(a, came_a, token)
    b.append(own_state(keys, values, log_decay, 1, size, (a[1],)))
    came_b.append(send(b[0], 0))
    close, token = near(1, close, b[0])
    go(a, came_a, token)
    go(b, came_b, a[2])
    close, token = near(2, close, b[1])
    go(a, came_a, token)
    go(b, came_b, a[3])
    close, token = near(3, close, b[2])
    go(a, came_a, token)
    go(b, came_b, a[4])
    go(a, came_a, b[3])
    go(b, came_b, a[5])
    far_a, before_a = first_levels(0, came_a[: early + 1], b[4])
    far_b, before_b = first_levels(1, came_b[:early], before_a)
    go(b, came_b, before_b)

    me = lax.axis_index("head").astype(jnp.int32)
    both = jnp.stack([sides - 1 - me, me])
    to_send, to_keep = finish(
        both, upper, queries, far_a, before_a, weights, levels, gain, came_a[early + 1 :], weight, 0, True
    )
    to_send, b_hi, b_lo = finish(
        both, upper, queries, far_b, before_b, weights, levels, gain, came_b[early:], weight, size, False, to_send
    )
    came = lax.ppermute(to_send, "head", [(s, sides - 1 - s) for s in range(sides)])
    to_keep = project(both, b_hi, b_lo, weight, 1, to_keep)
    return to_keep + came


def solution(mesh):
    return jax.shard_map(
        local,
        mesh=mesh,
        in_specs=(
            P("seq", "head"),
            P("seq", "head"),
            P("seq", "head"),
            P("head", "seq"),
            P("head", None, "seq"),
            P("head"),
            P("head", "seq"),
        ),
        out_specs=P("seq", "head"),
        check_vma=False,
    )
```

```python
import functools

import jax
import jax.numpy as jnp
from jax import lax
from jax.experimental import pallas as pl
from jax.experimental.pallas import tpu as pltpu
from jax.sharding import PartitionSpec as P

HIGH = lax.Precision.HIGHEST
DH = 128
CHUNK = 128
ROWS = DH + 8
F32 = jnp.float32
BF16 = jnp.bfloat16
NT = (((1,), (1,)), ((), ()))
TN = (((0,), (0,)), ((), ()))
NN = (((1,), (0,)), ((), ()))
ANY = pl.BlockSpec(memory_space=pl.ANY)
VMEM = pl.BlockSpec(memory_space=pltpu.VMEM)
SMEM = pl.BlockSpec(memory_space=pltpu.SMEM)


def params(mib=52):
    return pltpu.CompilerParams(vmem_limit_bytes=mib * 2**20)


def cost(flops, bytes_accessed):
    return pl.CostEstimate(flops=int(flops), bytes_accessed=int(bytes_accessed), transcendentals=0)


def split(x):
    hi = x.astype(BF16)
    return hi, (x - hi.astype(F32)).astype(BF16)


def split3(x):
    hi = x.astype(BF16)
    rest = x - hi.astype(F32)
    mid = rest.astype(BF16)
    return hi, mid, (rest - mid.astype(F32)).astype(BF16)


def mm(a, b, dims):
    return lax.dot_general(a, b, dims, preferred_element_type=F32)


def mm3(a, b, dims):
    a_hi, a_lo = split(a)
    b_hi, b_lo = split(b)
    return mm(a_hi, b_hi, dims) + (mm(a_hi, b_lo, dims) + mm(a_lo, b_hi, dims))


def outer_sum(k, v):
    made = mm(jnp.concatenate(split(k), axis=1), jnp.concatenate(split(v), axis=1), TN)
    return made[:DH, :DH] + (made[:DH, DH:] + made[DH:, :DH])


def state_kernel(k_ref, v_ref, ld_ref, *refs):
    out_ref, fade_ref = refs[-2:]
    heads, tok = ld_ref.shape
    step = k_ref.shape[1] // DH
    i = pl.program_id(0)

    @pl.when(i == 0)
    def _():
        ld = ld_ref[...]
        later = lax.broadcasted_iota(jnp.int32, (tok, tok), 1) > lax.broadcasted_iota(jnp.int32, (tok, tok), 0)
        later = jnp.where(later, 1.0, 0.0).astype(BF16)
        made = mm(later, jnp.concatenate(split3(ld), axis=0), NT)
        fade = jnp.exp(made[:, :heads] + (made[:, heads : 2 * heads] + made[:, 2 * heads :]))
        for j in range(heads // step):
            fade_ref[j] = fade[:, j * step : (j + 1) * step]

    fade = fade_ref[i]
    for h in range(step):
        cols = pl.ds(h * DH, DH)
        out_ref[h, :DH, :] = outer_sum(k_ref[:, cols] * fade[:, h : h + 1], v_ref[:, cols])
        total = jnp.sum(ld_ref[pl.ds(i * step + h, 1), :], axis=1, keepdims=True)
        out_ref[h, DH:, :] = jnp.broadcast_to(total, (ROWS - DH, DH))


def own_state(keys, values, log_decay, group, heads, after=()):
    tok = keys.shape[0]
    step = 2
    steps = heads // step
    wide = pl.BlockSpec((tok, step * DH), lambda i: (0, group * steps + i))
    return pl.pallas_call(
        state_kernel,
        out_shape=jax.ShapeDtypeStruct((heads, ROWS, DH), F32),
        grid=(steps,),
        in_specs=[wide, wide, pl.BlockSpec((heads, tok), lambda i: (group, 0))] + [ANY] * len(after),
        out_specs=pl.BlockSpec((step, ROWS, DH), lambda i: (i, 0, 0)),
        scratch_shapes=[pltpu.VMEM((steps, tok, step), F32)],
        compiler_params=params(),
        cost_estimate=cost(8 * tok * heads * DH * DH, 8 * tok * heads * DH),
        name="own_state",
    )(keys, values, log_decay, *after)


def merge_kernel(bit, carries, upper_ref, mine_ref, other_ref, *refs):
    out_ref = refs[-2] if carries else refs[-1]
    upper = upper_ref[bit] == 1
    for h in range(mine_ref.shape[0]):
        mine, other = mine_ref[h], other_ref[h]
        low = jnp.where(upper, other, mine)
        high = jnp.where(upper, mine, other)
        faded = jnp.exp(high[DH : DH + 1, :])
        out_ref[h, :DH, :] = faded * low[:DH] + high[:DH]
        out_ref[h, DH:, :] = low[DH:] + high[DH:]


def merged(bit, upper, mine, other, after=(), carry=None):
    more = [] if carry is None else [carry]
    outs = pl.pallas_call(
        functools.partial(merge_kernel, bit, bool(more)),
        out_shape=[jax.ShapeDtypeStruct(mine.shape, F32)] + [jax.ShapeDtypeStruct(c.shape, F32) for c in more],
        in_specs=[SMEM, VMEM, VMEM] + [ANY] * (len(more) + len(after)),
        out_specs=[VMEM] + [ANY] * len(more),
        input_output_aliases={3: 1} if more else {},
        compiler_params=params(16),
        cost_estimate=cost(3 * mine.size, 12 * mine.size),
        name="merge",
    )(upper, mine, other, *more, *after)
    return outs if more else outs[0]


def prepare_kernel(ld_ref, w_ref, *refs):
    sums_ref, cols_ref, weights_ref = refs[-3:]
    heads, tok = ld_ref.shape
    levels = w_ref.shape[1]
    chunks = tok // CHUNK
    near_levels = tok.bit_length()
    row = lax.broadcasted_iota(jnp.int32, (CHUNK, CHUNK), 0)
    col = lax.broadcasted_iota(jnp.int32, (CHUNK, CHUNK), 1)
    upto = jnp.where(row <= col, 1.0, 0.0).astype(BF16)
    sums = []
    for m in range(chunks):
        hi, mid, low = split3(ld_ref[:, m * CHUNK : (m + 1) * CHUNK])
        sums.append(mm(hi, upto, NN) + (mm(mid, upto, NN) + mm(low, upto, NN)))
    start = jnp.zeros((heads, 1), F32)
    fulls = []
    halves = []
    for m in range(chunks):
        fulls.append(sums[m] + start)
        halves.append(sums[m] + (sums[m - 1][:, CHUNK - 1 :] if m % 4 == 3 else 0.0))
        start = start + sums[m][:, CHUNK - 1 :]
    cum = jnp.concatenate(sums, axis=1)
    one = jnp.exp(cum)
    two = jnp.exp(jnp.concatenate(halves, axis=1))
    far = jnp.exp(jnp.concatenate(fulls, axis=1))
    for h in range(heads):
        sums_ref[h] = cum[h : h + 1]
    fill = jnp.zeros((CHUNK - heads, tok), F32)
    cols_ref[...] = jnp.transpose(jnp.concatenate([cum, fill], axis=0))
    level = lax.broadcasted_iota(jnp.int32, (levels, tok), 0)
    per = CHUNK // levels
    for g in range(heads // per):
        made = []
        for h in range(g * per, (g + 1) * per):
            decay = jnp.where(level >= near_levels, far[h : h + 1], two[h : h + 1])
            decay = jnp.where(level == near_levels - 2, one[h : h + 1], decay)
            decay = jnp.where(level < near_levels - 2, 1.0, decay)
            made.append(w_ref[h] * decay)
        weights_ref[:, g * CHUNK : (g + 1) * CHUNK] = jnp.transpose(jnp.concatenate(made, axis=0))


def prepare(log_decay, level_weights, after=()):
    heads, tok = log_decay.shape
    levels = level_weights.shape[1]
    return pl.pallas_call(
        prepare_kernel,
        out_shape=(
            jax.ShapeDtypeStruct((heads, 1, tok), F32),
            jax.ShapeDtypeStruct((tok, CHUNK), F32),
            jax.ShapeDtypeStruct((tok, heads * levels), F32),
        ),
        in_specs=[VMEM, VMEM] + [ANY] * len(after),
        out_specs=[VMEM] * 3,
        compiler_params=params(),
        cost_estimate=cost(0, 8 * heads * levels * tok),
        name="prepare",
    )(log_decay, level_weights, *after)


def near_kernel(first, levels, q_ref, k_ref, v_ref, sums_ref, cols_ref, w_ref, *refs):
    out_ref, token_ref = refs[-2:]
    tok = q_ref.shape[0]
    chunks = tok // CHUNK
    tile_bits = CHUNK.bit_length() - 1
    row = lax.broadcasted_iota(jnp.int32, (CHUNK, CHUNK), 0)
    col = lax.broadcasted_iota(jnp.int32, (CHUNK, CHUNK), 1)
    apart = row ^ col
    causal = row >= col
    head = first + pl.program_id(0)
    per = CHUNK // levels
    token_ref[...] = jnp.zeros_like(token_ref)
    states = []
    ends = []
    for m in range(chunks):
        rows = pl.ds(m * CHUNK, CHUNK)
        q = q_ref[rows, :] * DH**-0.5
        k = k_ref[rows, :]
        v = v_ref[rows, :]
        w = pltpu.roll(w_ref[rows, :], (per - head % per) * levels, 1)
        c_cols = pltpu.roll(cols_ref[rows, :], CHUNK - head, 1)
        c = c_cols[:, 0:1]
        near = jnp.broadcast_to(w[:, 0:1], (CHUNK, CHUNK))
        for bit in range(tile_bits):
            near = jnp.where(apart >= 2**bit, w[:, bit + 1 : bit + 2], near)
        gap = jnp.where(causal, c - sums_ref[0, :, m * CHUNK : (m + 1) * CHUNK], -1e30)
        q_hi, q_lo = split(q)
        k_hi, k_lo = split(k)
        q_both = jnp.concatenate([q_hi, q_lo], axis=1)
        scores = mm(q_both, jnp.concatenate([k_hi, k_hi], axis=1), NT) + mm(q_hi, k_lo, NT)
        scores = scores * (near * jnp.exp(gap))
        s_hi, s_lo = split(scores)
        v_hi, v_lo = split(v)
        s_both = jnp.concatenate([s_hi, s_lo], axis=1)
        out = mm(s_both, jnp.concatenate([v_hi, v_hi], axis=0), NN) + mm(s_hi, v_lo, NN)
        for bit in range(2):
            if m >> bit & 1:
                at = (m >> bit) - 1 << bit
                seen = states[at]
                for n in range(at + 1, at + 2**bit):
                    seen = jnp.exp(ends[n]) * seen + states[n]
                level = tile_bits + 1 + bit
                s_hi, s_lo = split(seen)
                made = mm(q_both, jnp.concatenate([s_hi, s_hi], axis=0), NN) + mm(q_hi, s_lo, NN)
                out = out + w[:, level : level + 1] * made
        out_ref[rows, :] = out
        if m < chunks - 1:
            end = c[CHUNK - 1 : CHUNK]
            states.append(outer_sum(k * jnp.exp(end - c), v))
            ends.append(end)


def near_part(queries, keys, values, sums, cols, weights, levels, first, heads, so_far=None, after=()):
    tok = queries.shape[0]
    per = CHUNK // levels
    one = pl.BlockSpec((tok, DH), lambda h: (0, first + h))
    more = [] if so_far is None else [so_far]
    return pl.pallas_call(
        functools.partial(near_kernel, first, levels),
        out_shape=(
            jax.ShapeDtypeStruct(queries.shape, F32),
            jax.ShapeDtypeStruct((8, CHUNK), F32),
        ),
        grid=(heads,),
        in_specs=[
            one,
            one,
            one,
            pl.BlockSpec((1, 1, tok), lambda h: (first + h, 0, 0)),
            pl.BlockSpec(cols.shape, lambda h: (0, 0)),
            pl.BlockSpec((tok, CHUNK), lambda h: (0, (first + h) // per)),
        ]
        + [ANY] * (len(more) + len(after)),
        out_specs=[one, pl.BlockSpec((8, CHUNK), lambda h: (0, 0))],
        input_output_aliases={6: 0} if more else {},
        compiler_params=params(),
        cost_estimate=cost(60 * tok * heads * DH * DH, 16 * tok * heads * DH),
        name="near",
    )(queries, keys, values, sums, cols, weights, *more, *after)


def add_levels(q_hi, q_lo, out, w, first_column, states):
    parts = []
    for state in states:
        hi, lo = split(state)
        parts.append(jnp.concatenate([hi, hi, lo], axis=0))
    made = mm(jnp.concatenate([q_hi, q_lo, q_hi], axis=1), jnp.concatenate(parts, axis=1), NN)
    for n in range(len(parts)):
        at = first_column + n
        out = out + w[:, at : at + 1] * made[:, n * DH : (n + 1) * DH]
    return out


def early_kernel(first, levels, count, upper_ref, q_ref, near_ref, w_ref, *refs):
    out_ref, before_ref = refs[-2:]
    step = q_ref.shape[1] // DH
    per = CHUNK // levels
    total = upper_ref.shape[0]
    head = first + pl.program_id(0) * step
    w = pltpu.roll(w_ref[...], (per - head % per) * levels, 1)
    for h in range(step):
        cols = pl.ds(h * DH, DH)
        q_hi, q_lo = split(q_ref[:, cols] * DH**-0.5)
        before = jnp.zeros((1, DH), F32)
        states = []
        for level in range(count):
            upper = upper_ref[level] == 1
            reach = jnp.where(upper, jnp.exp(before), 0.0)
            states.append(refs[level][h, :DH, :] * reach)
            before = before + jnp.where(upper, refs[level][h, DH : DH + 1, :], 0.0)
        out_ref[:, cols] = add_levels(q_hi, q_lo, near_ref[:, cols], w, h * levels + levels - total, states)
        before_ref[h] = jnp.broadcast_to(before, before_ref.shape[1:])


def early_levels(upper, queries, near, weights, levels, states, first, after=()):
    heads = states[0].shape[0]
    tok = queries.shape[0]
    per = CHUNK // levels
    step = 2
    wide = pl.BlockSpec((tok, step * DH), lambda i: (0, first // step + i))
    return pl.pallas_call(
        functools.partial(early_kernel, first, levels, len(states)),
        out_shape=(
            jax.ShapeDtypeStruct((tok, heads * DH), F32),
            jax.ShapeDtypeStruct((heads, 8, DH), F32),
        ),
        grid=(heads // step,),
        in_specs=[
            SMEM,
            wide,
            wide,
            pl.BlockSpec((tok, CHUNK), lambda i: (0, (first + i * step) // per)),
        ]
        + [pl.BlockSpec((step, ROWS, DH), lambda i: (i, 0, 0))] * len(states)
        + [ANY] * len(after),
        out_specs=[
            pl.BlockSpec((tok, step * DH), lambda i: (0, i)),
            pl.BlockSpec((step, 8, DH), lambda i: (i, 0, 0)),
        ],
        compiler_params=params(),
        cost_estimate=cost(8 * len(states) * tok * heads * DH * DH, 16 * tok * heads * DH),
        name="early",
    )(upper, queries, near, weights, *states, *after)


TILE = 256


def tile_copy(side, steps, part, j, w_ref, buffer_ref, sems, slot):
    depth = buffer_ref.shape[2]
    rows = pl.ds(pl.multiple_of((side * steps + j) * TILE, TILE), TILE)
    return pltpu.make_async_copy(
        w_ref.at[rows, pl.ds(part * depth, depth)], buffer_ref.at[slot], sems.at[slot]
    )


def project_tiles(side, steps, part, w_ref, buffer_ref, sems, slot, x_hi, x_lo, more_ref, out_ref):
    @pl.loop(0, steps)
    def _(j):
        tile_copy(side, steps, part, j, w_ref, buffer_ref, sems, slot + j).wait()
        w_hi, w_lo = split(buffer_ref[slot + j])
        cols = pl.ds(pl.multiple_of(j * TILE, TILE), TILE)
        made = mm(x_hi[...], w_hi, NT) + (mm(x_hi[...], w_lo, NT) + mm(x_lo[...], w_hi, NT))
        if more_ref is not None:
            made = made + more_ref[:, cols]
        out_ref[:, cols] = made


def finish_kernel(first, levels, skip, tiles, upper_ref, q_ref, near_ref, before_ref, w_ref, gain_ref, *refs):
    total = upper_ref.shape[0]
    states, refs = refs[: total - skip], refs[total - skip :]
    if tiles:
        sides_ref, weight_ref, more_ref, x_hi, x_lo, send_ref, q_buffer, q_sems, buffer_ref, sems = refs
    else:
        x_hi, x_lo, token_ref, q_buffer, q_sems = refs[-5:]
        token_ref[...] = jnp.zeros_like(token_ref)
    heads = states[0].shape[0]
    part = first // heads
    pair = 2

    def q_copy(n):
        cols = pl.ds(pl.multiple_of((first + n * pair) * DH, pair * DH), pair * DH)
        return pltpu.make_async_copy(q_ref.at[:, cols], q_buffer.at[n], q_sems.at[n])

    for n in range(heads // pair):
        q_copy(n).start()
    for j in range(tiles):
        tile_copy(sides_ref[0], tiles, part, j, weight_ref, buffer_ref, sems, j).start()

    per = CHUNK // levels

    @pl.loop(0, heads // pair)
    def _(n):
        q_copy(n).wait()
        group = pl.multiple_of((first + n * pair) // per * CHUNK, CHUNK)
        w = pltpu.roll(w_ref[:, pl.ds(group, CHUNK)], (per - (first + n * pair) % per) * levels, 1)
        for i in range(pair):
            h = n * pair + i
            cols = pl.ds(pl.multiple_of(h * DH, DH), DH)
            all_cols = pl.ds(pl.multiple_of((first + h) * DH, DH), DH)
            q_hi, q_lo = split(q_buffer[n, :, i * DH : (i + 1) * DH] * DH**-0.5)
            before = before_ref[h, 0:1, :]
            scaled = []
            for m, ref in enumerate(states):
                upper = upper_ref[skip + m] == 1
                scaled.append(ref[h, :DH, :] * jnp.where(upper, jnp.exp(before), 0.0))
                before = before + jnp.where(upper, ref[h, DH : DH + 1, :], 0.0)
            column = i * levels + levels - total + skip
            out = add_levels(q_hi, q_lo, near_ref[:, cols], w, column, scaled)
            squares = jnp.concatenate(split(out * out), axis=1)
            mean = mm(squares, jnp.full((2 * DH, DH), 1.0 / DH, BF16), NN)
            out = out * lax.rsqrt(mean + 1e-06) * gain_ref[:, all_cols]
            hi, lo = split(out)
            x_hi[:, cols] = hi
            x_lo[:, cols] = lo

    if tiles:
        project_tiles(
            sides_ref[0], tiles, part, weight_ref, buffer_ref, sems, 0, x_hi, x_lo, more_ref, send_ref
        )


def finish(upper, queries, near, before, weights, levels, gain, states, first, sides=None, weight=None, more=None, after=()):
    heads = states[0].shape[0]
    tok = queries.shape[0]
    depth = heads * DH
    skip = upper.shape[0] - len(states)
    half = jax.ShapeDtypeStruct((tok, depth), BF16)
    tiles = 0 if weight is None else more.shape[1] // TILE
    extra = [sides, weight, more] if tiles else []
    outs = [half, half, jax.ShapeDtypeStruct(more.shape if tiles else (8, CHUNK), F32)]
    return pl.pallas_call(
        functools.partial(finish_kernel, first, levels, skip, tiles),
        out_shape=outs,
        in_specs=[SMEM, ANY]
        + [VMEM] * (4 + len(states))
        + ([SMEM, ANY, VMEM] if tiles else [])
        + [ANY] * len(after),
        out_specs=[VMEM] * len(outs),
        scratch_shapes=[
            pltpu.VMEM((heads // 2, tok, 2 * DH), F32),
            pltpu.SemaphoreType.DMA((heads // 2,)),
        ]
        + ([pltpu.VMEM((tiles, TILE, depth), F32), pltpu.SemaphoreType.DMA((tiles,))] if tiles else []),
        compiler_params=params(44),
        cost_estimate=cost(8 * tok * depth * DH + 6 * tok * depth * tiles * TILE, 16 * tok * depth),
        name="finish",
    )(upper, queries, near, before, weights, gain, *states, *extra, *after)


def project_kernel(part, used, more, sides_ref, x_hi, x_lo, weight_ref, *refs):
    *out_refs, buffer_ref, sems = refs[-(len(used) + 2) :]
    steps = out_refs[0].shape[1] // TILE
    for n, side in enumerate(used):
        for j in range(steps):
            tile_copy(sides_ref[side], steps, part, j, weight_ref, buffer_ref, sems, n * steps + j).start()
    for n, side in enumerate(used):
        project_tiles(
            sides_ref[side],
            steps,
            part,
            weight_ref,
            buffer_ref,
            sems,
            n * steps,
            x_hi,
            x_lo,
            refs[0] if more else None,
            out_refs[n],
        )


def project(sides, used, x_hi, x_lo, weight, part, more=None, after=()):
    tok, depth = x_hi.shape
    width = weight.shape[0] // 2
    tiles = len(used) * width // TILE
    extra = [] if more is None else [more]
    return pl.pallas_call(
        functools.partial(project_kernel, part, used, bool(extra)),
        out_shape=[jax.ShapeDtypeStruct((tok, width), F32)] * len(used),
        in_specs=[SMEM, VMEM, VMEM, ANY] + [VMEM] * len(extra) + [ANY] * len(after),
        out_specs=[VMEM] * len(used),
        scratch_shapes=[pltpu.VMEM((tiles, TILE, depth), F32), pltpu.SemaphoreType.DMA((tiles,))],
        compiler_params=params(44),
        cost_estimate=cost(6 * tok * depth * width * len(used), 4 * (depth * width + 2 * tok * width)),
        name="project",
    )(sides, x_hi, x_lo, weight, *extra, *after)


def local(queries, keys, values, log_decay, level_weights, norm_gain, out_weight):
    head_count = log_decay.shape[0]
    levels = level_weights.shape[1]
    n_seq = lax.axis_size("seq")
    sides = lax.axis_size("head")
    seq_bits = n_seq.bit_length() - 1
    seq_index = lax.axis_index("seq")
    size = head_count // 2

    weight = lax.all_gather(out_weight.T, "seq", axis=0, tiled=True)
    upper = (seq_index >> jnp.arange(seq_bits, dtype=jnp.int32)) & 1
    gain = norm_gain.reshape(1, -1)

    def send(block, bit):
        def wanted(s):
            above = s >> bit
            return not (bit == seq_bits - 1 and above & 1) and not (bit == seq_bits - 2 and above == 3)

        flip = 3 << bit - 1 if bit % 2 else 1 << bit
        return lax.ppermute(block, "seq", [(s, s ^ flip) for s in range(n_seq) if wanted(s)])

    small = size // 2
    early = 4

    def near(n, so_far, *after):
        return near_part(
            queries, keys, values, sums, cols, weights, levels, n * small, small, so_far, after
        )

    def first_levels(group, states, *after):
        return early_levels(upper, queries, close, weights, levels, states, group * size, after)

    a, came_a, b, came_b = [], [], [], []

    def go(blocks, came, *after):
        bit = len(blocks) - 1
        blocks.append(merged(bit, upper, blocks[bit], came[bit], after))
        came.append(send(blocks[-1], bit + 1))

    a.append(own_state(keys, values, log_decay, 0, size))
    came_a.append(send(a[0], 0))
    own_b = own_state(keys, values, log_decay, 1, size, (a[0],))
    sums, cols, weights = prepare(log_decay, level_weights, (own_b,))
    after_a, own_b = merged(0, upper, a[0], came_a[0], (weights,), own_b)
    a.append(after_a)
    came_a.append(send(a[1], 1))
    b.append(own_b)
    came_b.append(send(b[0], 0))
    close, token = near(0, None, b[0])
    go(a, came_a, token)
    go(b, came_b, a[2])
    close, token = near(1, close, b[1])
    go(a, came_a, token)
    go(b, came_b, a[3])
    close, token = near(2, close, b[2])
    go(a, came_a, token)
    go(b, came_b, a[4])
    close, token = near(3, close, b[3])
    go(a, came_a, token)
    go(b, came_b, a[5])
    far_a, before_a = first_levels(0, came_a[: early + 1], b[4])
    far_b, before_b = first_levels(1, came_b[:early], before_a)
    a_hi, a_lo, token = finish(
        upper, queries, far_a, before_a, weights, levels, gain, came_a[early + 1 :], 0, after=(before_b,)
    )
    go(b, came_b, token)

    me = lax.axis_index("head").astype(jnp.int32)
    both = jnp.stack([sides - 1 - me, me])
    to_send, to_keep = project(both, (0, 1), a_hi, a_lo, weight, 0, after=(b[5],))
    b_hi, b_lo, to_send = finish(
        upper, queries, far_b, before_b, weights, levels, gain, came_b[early:], size, both, weight, to_send
    )
    came = lax.ppermute(to_send, "head", [(s, sides - 1 - s) for s in range(sides)])
    [to_keep] = project(both, (1,), b_hi, b_lo, weight, 1, to_keep)
    return to_keep + came


def solution(mesh):
    return jax.shard_map(
        local,
        mesh=mesh,
        in_specs=(
            P("seq", "head"),
            P("seq", "head"),
            P("seq", "head"),
            P("head", "seq"),
            P("head", None, "seq"),
            P("head"),
            P("head", "seq"),
        ),
        out_specs=P("seq", "head"),
        check_vma=False,
    )
```

```python
import functools

import jax
import jax.numpy as jnp
from jax import lax
from jax.experimental import pallas as pl
from jax.experimental.pallas import tpu as pltpu
from jax.sharding import PartitionSpec as P

HIGH = lax.Precision.HIGHEST
DH = 128
CHUNK = 128
ROWS = DH + 8
F32 = jnp.float32
BF16 = jnp.bfloat16
NT = (((1,), (1,)), ((), ()))
TN = (((0,), (0,)), ((), ()))
NN = (((1,), (0,)), ((), ()))
ANY = pl.BlockSpec(memory_space=pl.ANY)
VMEM = pl.BlockSpec(memory_space=pltpu.VMEM)
SMEM = pl.BlockSpec(memory_space=pltpu.SMEM)


def params(mib=52):
    return pltpu.CompilerParams(vmem_limit_bytes=mib * 2**20)


def cost(flops, bytes_accessed):
    return pl.CostEstimate(flops=int(flops), bytes_accessed=int(bytes_accessed), transcendentals=0)


def split(x):
    hi = x.astype(BF16)
    return hi, (x - hi.astype(F32)).astype(BF16)


def split3(x):
    hi = x.astype(BF16)
    rest = x - hi.astype(F32)
    mid = rest.astype(BF16)
    return hi, mid, (rest - mid.astype(F32)).astype(BF16)


def mm(a, b, dims):
    return lax.dot_general(a, b, dims, preferred_element_type=F32)


def mm3(a, b, dims):
    a_hi, a_lo = split(a)
    b_hi, b_lo = split(b)
    return mm(a_hi, b_hi, dims) + (mm(a_hi, b_lo, dims) + mm(a_lo, b_hi, dims))


def outer_sum(k, v):
    made = mm(jnp.concatenate(split(k), axis=1), jnp.concatenate(split(v), axis=1), TN)
    return made[:DH, :DH] + (made[:DH, DH:] + made[DH:, :DH])


def state_kernel(group, heads, pair, k_ref, v_ref, ld_ref, *refs):
    out_ref, fade_ref, k_buffer, v_buffer, k_sems, v_sems = refs[-6:]
    tok = ld_ref.shape[1]
    steps = heads // pair

    def copies(n):
        cols = pl.ds(pl.multiple_of((group * heads + n * pair) * DH, pair * DH), pair * DH)
        return (
            pltpu.make_async_copy(k_ref.at[:, cols], k_buffer.at[n], k_sems.at[n]),
            pltpu.make_async_copy(v_ref.at[:, cols], v_buffer.at[n], v_sems.at[n]),
        )

    for n in range(steps):
        for copy in copies(n):
            copy.start()
    ld = ld_ref[group * heads : (group + 1) * heads, :]
    later = lax.broadcasted_iota(jnp.int32, (tok, tok), 1) > lax.broadcasted_iota(jnp.int32, (tok, tok), 0)
    later = jnp.where(later, 1.0, 0.0).astype(BF16)
    made = mm(later, jnp.concatenate(split3(ld), axis=0), NT)
    fade = jnp.exp(made[:, :heads] + (made[:, heads : 2 * heads] + made[:, 2 * heads :]))
    for n in range(steps):
        fade_ref[n] = fade[:, n * pair : (n + 1) * pair]
    totals = jnp.sum(ld, axis=1, keepdims=True)
    for h in range(heads):
        out_ref[h, DH:, :] = jnp.broadcast_to(totals[h : h + 1, :], (ROWS - DH, DH))

    @pl.loop(0, steps)
    def _(n):
        for copy in copies(n):
            copy.wait()
        fades = fade_ref[n]
        for h in range(pair):
            cols = pl.ds(h * DH, DH)
            faded = k_buffer[n, :, cols] * fades[:, h : h + 1]
            out_ref[n * pair + h, :DH, :] = outer_sum(faded, v_buffer[n, :, cols])


def own_state(keys, values, log_decay, group, heads, after=()):
    tok = keys.shape[0]
    pair = 2
    steps = heads // pair
    return pl.pallas_call(
        functools.partial(state_kernel, group, heads, pair),
        out_shape=jax.ShapeDtypeStruct((heads, ROWS, DH), F32),
        in_specs=[ANY, ANY, VMEM] + [ANY] * len(after),
        out_specs=VMEM,
        scratch_shapes=[
            pltpu.VMEM((steps, tok, pair), F32),
            pltpu.VMEM((steps, tok, pair * DH), F32),
            pltpu.VMEM((steps, tok, pair * DH), F32),
            pltpu.SemaphoreType.DMA((steps,)),
            pltpu.SemaphoreType.DMA((steps,)),
        ],
        compiler_params=params(60),
        cost_estimate=cost(8 * tok * heads * DH * DH, 8 * tok * heads * DH),
        name="own_state",
    )(keys, values, log_decay, *after)


def merge_kernel(bit, carries, upper_ref, mine_ref, other_ref, *refs):
    out_ref = refs[-2] if carries else refs[-1]
    upper = upper_ref[bit] == 1
    for h in range(mine_ref.shape[0]):
        mine, other = mine_ref[h], other_ref[h]
        low = jnp.where(upper, other, mine)
        high = jnp.where(upper, mine, other)
        faded = jnp.exp(high[DH : DH + 1, :])
        out_ref[h, :DH, :] = faded * low[:DH] + high[:DH]
        out_ref[h, DH:, :] = low[DH:] + high[DH:]


def merged(bit, upper, mine, other, after=(), carry=None):
    more = [] if carry is None else [carry]
    outs = pl.pallas_call(
        functools.partial(merge_kernel, bit, bool(more)),
        out_shape=[jax.ShapeDtypeStruct(mine.shape, F32)] + [jax.ShapeDtypeStruct(c.shape, F32) for c in more],
        in_specs=[SMEM, VMEM, VMEM] + [ANY] * (len(more) + len(after)),
        out_specs=[VMEM] + [ANY] * len(more),
        input_output_aliases={3: 1} if more else {},
        compiler_params=params(16),
        cost_estimate=cost(3 * mine.size, 12 * mine.size),
        name="merge",
    )(upper, mine, other, *more, *after)
    return outs if more else outs[0]


def prepare_kernel(ld_ref, w_ref, *refs):
    sums_ref, cols_ref, weights_ref = refs[-3:]
    heads, tok = ld_ref.shape
    levels = w_ref.shape[1]
    chunks = tok // CHUNK
    near_levels = tok.bit_length()
    row = lax.broadcasted_iota(jnp.int32, (CHUNK, CHUNK), 0)
    col = lax.broadcasted_iota(jnp.int32, (CHUNK, CHUNK), 1)
    upto = jnp.where(row <= col, 1.0, 0.0).astype(BF16)
    sums = []
    for m in range(chunks):
        hi, mid, low = split3(ld_ref[:, m * CHUNK : (m + 1) * CHUNK])
        sums.append(mm(hi, upto, NN) + (mm(mid, upto, NN) + mm(low, upto, NN)))
    start = jnp.zeros((heads, 1), F32)
    fulls = []
    halves = []
    for m in range(chunks):
        fulls.append(sums[m] + start)
        halves.append(sums[m] + (sums[m - 1][:, CHUNK - 1 :] if m % 4 == 3 else 0.0))
        start = start + sums[m][:, CHUNK - 1 :]
    cum = jnp.concatenate(sums, axis=1)
    one = jnp.exp(cum)
    two = jnp.exp(jnp.concatenate(halves, axis=1))
    far = jnp.exp(jnp.concatenate(fulls, axis=1))
    for h in range(heads):
        sums_ref[h] = cum[h : h + 1]
    fill = jnp.zeros((CHUNK - heads, tok), F32)
    cols_ref[...] = jnp.transpose(jnp.concatenate([cum, fill], axis=0))
    level = lax.broadcasted_iota(jnp.int32, (levels, tok), 0)
    per = CHUNK // levels
    for g in range(heads // per):
        made = []
        for h in range(g * per, (g + 1) * per):
            decay = jnp.where(level >= near_levels, far[h : h + 1], two[h : h + 1])
            decay = jnp.where(level == near_levels - 2, one[h : h + 1], decay)
            decay = jnp.where(level < near_levels - 2, 1.0, decay)
            made.append(w_ref[h] * decay)
        weights_ref[:, g * CHUNK : (g + 1) * CHUNK] = jnp.transpose(jnp.concatenate(made, axis=0))


def prepare(log_decay, level_weights, after=()):
    heads, tok = log_decay.shape
    levels = level_weights.shape[1]
    return pl.pallas_call(
        prepare_kernel,
        out_shape=(
            jax.ShapeDtypeStruct((heads, 1, tok), F32),
            jax.ShapeDtypeStruct((tok, CHUNK), F32),
            jax.ShapeDtypeStruct((tok, heads * levels), F32),
        ),
        in_specs=[VMEM, VMEM] + [ANY] * len(after),
        out_specs=[VMEM] * 3,
        compiler_params=params(),
        cost_estimate=cost(0, 8 * heads * levels * tok),
        name="prepare",
    )(log_decay, level_weights, *after)


def near_kernel(first, levels, q_ref, k_ref, v_ref, sums_ref, cols_ref, w_ref, *refs):
    out_ref, token_ref = refs[-2:]
    tok = q_ref.shape[0]
    chunks = tok // CHUNK
    tile_bits = CHUNK.bit_length() - 1
    row = lax.broadcasted_iota(jnp.int32, (CHUNK, CHUNK), 0)
    col = lax.broadcasted_iota(jnp.int32, (CHUNK, CHUNK), 1)
    apart = row ^ col
    causal = row >= col
    head = first + pl.program_id(0)
    per = CHUNK // levels
    token_ref[...] = jnp.zeros_like(token_ref)
    states = []
    ends = []
    for m in range(chunks):
        rows = pl.ds(m * CHUNK, CHUNK)
        q = q_ref[rows, :] * DH**-0.5
        k = k_ref[rows, :]
        v = v_ref[rows, :]
        w = pltpu.roll(w_ref[rows, :], (per - head % per) * levels, 1)
        c_cols = pltpu.roll(cols_ref[rows, :], CHUNK - head, 1)
        c = c_cols[:, 0:1]
        near = jnp.broadcast_to(w[:, 0:1], (CHUNK, CHUNK))
        for bit in range(tile_bits):
            near = jnp.where(apart >= 2**bit, w[:, bit + 1 : bit + 2], near)
        gap = jnp.where(causal, c - sums_ref[0, :, m * CHUNK : (m + 1) * CHUNK], -1e30)
        q_hi, q_lo = split(q)
        k_hi, k_lo = split(k)
        q_both = jnp.concatenate([q_hi, q_lo], axis=1)
        scores = mm(q_both, jnp.concatenate([k_hi, k_hi], axis=1), NT) + mm(q_hi, k_lo, NT)
        scores = scores * (near * jnp.exp(gap))
        s_hi, s_lo = split(scores)
        v_hi, v_lo = split(v)
        s_both = jnp.concatenate([s_hi, s_lo], axis=1)
        out = mm(s_both, jnp.concatenate([v_hi, v_hi], axis=0), NN) + mm(s_hi, v_lo, NN)
        for bit in range(2):
            if m >> bit & 1:
                at = (m >> bit) - 1 << bit
                seen = states[at]
                for n in range(at + 1, at + 2**bit):
                    seen = jnp.exp(ends[n]) * seen + states[n]
                level = tile_bits + 1 + bit
                s_hi, s_lo = split(seen)
                made = mm(q_both, jnp.concatenate([s_hi, s_hi], axis=0), NN) + mm(q_hi, s_lo, NN)
                out = out + w[:, level : level + 1] * made
        out_ref[rows, :] = out
        if m < chunks - 1:
            end = c[CHUNK - 1 : CHUNK]
            states.append(outer_sum(k * jnp.exp(end - c), v))
            ends.append(end)


def near_part(queries, keys, values, sums, cols, weights, levels, first, heads, so_far=None, after=()):
    tok = queries.shape[0]
    per = CHUNK // levels
    one = pl.BlockSpec((tok, DH), lambda h: (0, first + h))
    more = [] if so_far is None else [so_far]
    return pl.pallas_call(
        functools.partial(near_kernel, first, levels),
        out_shape=(
            jax.ShapeDtypeStruct(queries.shape, F32),
            jax.ShapeDtypeStruct((8, CHUNK), F32),
        ),
        grid=(heads,),
        in_specs=[
            one,
            one,
            one,
            pl.BlockSpec((1, 1, tok), lambda h: (first + h, 0, 0)),
            pl.BlockSpec(cols.shape, lambda h: (0, 0)),
            pl.BlockSpec((tok, CHUNK), lambda h: (0, (first + h) // per)),
        ]
        + [ANY] * (len(more) + len(after)),
        out_specs=[one, pl.BlockSpec((8, CHUNK), lambda h: (0, 0))],
        input_output_aliases={6: 0} if more else {},
        compiler_params=params(),
        cost_estimate=cost(60 * tok * heads * DH * DH, 16 * tok * heads * DH),
        name="near",
    )(queries, keys, values, sums, cols, weights, *more, *after)


def add_levels(q_hi, q_lo, out, w, first_column, states):
    parts = []
    for state in states:
        hi, lo = split(state)
        parts.append(jnp.concatenate([hi, hi, lo], axis=0))
    made = mm(jnp.concatenate([q_hi, q_lo, q_hi], axis=1), jnp.concatenate(parts, axis=1), NN)
    for n in range(len(parts)):
        at = first_column + n
        out = out + w[:, at : at + 1] * made[:, n * DH : (n + 1) * DH]
    return out


def early_kernel(first, levels, count, upper_ref, q_ref, near_ref, w_ref, *refs):
    out_ref, before_ref = refs[-2:]
    step = q_ref.shape[1] // DH
    per = CHUNK // levels
    total = upper_ref.shape[0]
    head = first + pl.program_id(0) * step
    w = pltpu.roll(w_ref[...], (per - head % per) * levels, 1)
    for h in range(step):
        cols = pl.ds(h * DH, DH)
        q_hi, q_lo = split(q_ref[:, cols] * DH**-0.5)
        before = jnp.zeros((1, DH), F32)
        states = []
        for level in range(count):
            upper = upper_ref[level] == 1
            reach = jnp.where(upper, jnp.exp(before), 0.0)
            states.append(refs[level][h, :DH, :] * reach)
            before = before + jnp.where(upper, refs[level][h, DH : DH + 1, :], 0.0)
        out_ref[:, cols] = add_levels(q_hi, q_lo, near_ref[:, cols], w, h * levels + levels - total, states)
        before_ref[h] = jnp.broadcast_to(before, before_ref.shape[1:])


def early_levels(upper, queries, near, weights, levels, states, first, after=()):
    heads = states[0].shape[0]
    tok = queries.shape[0]
    per = CHUNK // levels
    step = 2
    wide = pl.BlockSpec((tok, step * DH), lambda i: (0, first // step + i))
    return pl.pallas_call(
        functools.partial(early_kernel, first, levels, len(states)),
        out_shape=(
            jax.ShapeDtypeStruct((tok, heads * DH), F32),
            jax.ShapeDtypeStruct((heads, 8, DH), F32),
        ),
        grid=(heads // step,),
        in_specs=[
            SMEM,
            wide,
            wide,
            pl.BlockSpec((tok, CHUNK), lambda i: (0, (first + i * step) // per)),
        ]
        + [pl.BlockSpec((step, ROWS, DH), lambda i: (i, 0, 0))] * len(states)
        + [ANY] * len(after),
        out_specs=[
            pl.BlockSpec((tok, step * DH), lambda i: (0, i)),
            pl.BlockSpec((step, 8, DH), lambda i: (i, 0, 0)),
        ],
        compiler_params=params(),
        cost_estimate=cost(8 * len(states) * tok * heads * DH * DH, 16 * tok * heads * DH),
        name="early",
    )(upper, queries, near, weights, *states, *after)


TILE = 256


def tile_copy(side, steps, part, j, w_ref, buffer_ref, sems, slot):
    depth = buffer_ref.shape[2]
    rows = pl.ds(pl.multiple_of((side * steps + j) * TILE, TILE), TILE)
    return pltpu.make_async_copy(
        w_ref.at[rows, pl.ds(part * depth, depth)], buffer_ref.at[slot], sems.at[slot]
    )


def project_tiles(side, steps, part, w_ref, buffer_ref, sems, slot, x_hi, x_lo, more_ref, out_ref):
    @pl.loop(0, steps)
    def _(j):
        tile_copy(side, steps, part, j, w_ref, buffer_ref, sems, slot + j).wait()
        w_hi, w_lo = split(buffer_ref[slot + j])
        cols = pl.ds(pl.multiple_of(j * TILE, TILE), TILE)
        made = mm(x_hi[...], w_hi, NT) + (mm(x_hi[...], w_lo, NT) + mm(x_lo[...], w_hi, NT))
        if more_ref is not None:
            made = made + more_ref[:, cols]
        out_ref[:, cols] = made


def finish_kernel(first, levels, skip, used, more, upper_ref, q_ref, near_ref, before_ref, w_ref, gain_ref, *refs):
    total = upper_ref.shape[0]
    states, refs = refs[: total - skip], refs[total - skip :]
    sides_ref, weight_ref, *refs = refs
    more_ref, refs = (refs[0], refs[1:]) if more else (None, refs)
    x_hi, x_lo, *sum_refs, q_buffer, q_sems, buffer_ref, sems = refs[-(6 + used) :]
    tiles = sum_refs[0].shape[1] // TILE
    heads = states[0].shape[0]
    part = first // heads
    pair = 2

    def q_copy(n):
        cols = pl.ds(pl.multiple_of((first + n * pair) * DH, pair * DH), pair * DH)
        return pltpu.make_async_copy(q_ref.at[:, cols], q_buffer.at[n], q_sems.at[n])

    for n in range(heads // pair):
        q_copy(n).start()
    for n in range(used):
        for j in range(tiles):
            tile_copy(sides_ref[n], tiles, part, j, weight_ref, buffer_ref, sems, n * tiles + j).start()

    per = CHUNK // levels

    @pl.loop(0, heads // pair)
    def _(n):
        q_copy(n).wait()
        group = pl.multiple_of((first + n * pair) // per * CHUNK, CHUNK)
        w = pltpu.roll(w_ref[:, pl.ds(group, CHUNK)], (per - (first + n * pair) % per) * levels, 1)
        for i in range(pair):
            h = n * pair + i
            cols = pl.ds(pl.multiple_of(h * DH, DH), DH)
            all_cols = pl.ds(pl.multiple_of((first + h) * DH, DH), DH)
            q_hi, q_lo = split(q_buffer[n, :, i * DH : (i + 1) * DH] * DH**-0.5)
            before = before_ref[h, 0:1, :]
            scaled = []
            for m, ref in enumerate(states):
                upper = upper_ref[skip + m] == 1
                scaled.append(ref[h, :DH, :] * jnp.where(upper, jnp.exp(before), 0.0))
                before = before + jnp.where(upper, ref[h, DH : DH + 1, :], 0.0)
            column = i * levels + levels - total + skip
            out = add_levels(q_hi, q_lo, near_ref[:, cols], w, column, scaled)
            squares = jnp.concatenate(split(out * out), axis=1)
            mean = mm(squares, jnp.full((2 * DH, DH), 1.0 / DH, BF16), NN)
            out = out * lax.rsqrt(mean + 1e-06) * gain_ref[:, all_cols]
            hi, lo = split(out)
            x_hi[:, cols] = hi
            x_lo[:, cols] = lo

    for n in range(used):
        project_tiles(
            sides_ref[n], tiles, part, weight_ref, buffer_ref, sems, n * tiles, x_hi, x_lo, more_ref, sum_refs[n]
        )


def finish(sides, used, upper, queries, near, before, weights, levels, gain, states, first, weight, more=None, after=()):
    heads = states[0].shape[0]
    tok = queries.shape[0]
    depth = heads * DH
    width = weight.shape[0] // 2
    skip = upper.shape[0] - len(states)
    half = jax.ShapeDtypeStruct((tok, depth), BF16)
    tiles = used * width // TILE
    extra = [] if more is None else [more]
    outs = [half, half] + [jax.ShapeDtypeStruct((tok, width), F32)] * used
    return pl.pallas_call(
        functools.partial(finish_kernel, first, levels, skip, used, bool(extra)),
        out_shape=outs,
        in_specs=[SMEM, ANY]
        + [VMEM] * (4 + len(states))
        + [SMEM, ANY]
        + [VMEM] * len(extra)
        + [ANY] * len(after),
        out_specs=[VMEM] * len(outs),
        scratch_shapes=[
            pltpu.VMEM((heads // 2, tok, 2 * DH), F32),
            pltpu.SemaphoreType.DMA((heads // 2,)),
            pltpu.VMEM((tiles, TILE, depth), F32),
            pltpu.SemaphoreType.DMA((tiles,)),
        ],
        compiler_params=params(44),
        cost_estimate=cost(8 * tok * depth * DH + 6 * tok * depth * tiles * TILE, 16 * tok * depth),
        name="finish",
    )(upper, queries, near, before, weights, gain, *states, sides, weight, *extra, *after)


def project_kernel(part, used, more, sides_ref, x_hi, x_lo, weight_ref, *refs):
    *out_refs, buffer_ref, sems = refs[-(len(used) + 2) :]
    steps = out_refs[0].shape[1] // TILE
    for n, side in enumerate(used):
        for j in range(steps):
            tile_copy(sides_ref[side], steps, part, j, weight_ref, buffer_ref, sems, n * steps + j).start()
    for n, side in enumerate(used):
        project_tiles(
            sides_ref[side],
            steps,
            part,
            weight_ref,
            buffer_ref,
            sems,
            n * steps,
            x_hi,
            x_lo,
            refs[0] if more else None,
            out_refs[n],
        )


def project(sides, used, x_hi, x_lo, weight, part, more=None, after=()):
    tok, depth = x_hi.shape
    width = weight.shape[0] // 2
    tiles = len(used) * width // TILE
    extra = [] if more is None else [more]
    return pl.pallas_call(
        functools.partial(project_kernel, part, used, bool(extra)),
        out_shape=[jax.ShapeDtypeStruct((tok, width), F32)] * len(used),
        in_specs=[SMEM, VMEM, VMEM, ANY] + [VMEM] * len(extra) + [ANY] * len(after),
        out_specs=[VMEM] * len(used),
        scratch_shapes=[pltpu.VMEM((tiles, TILE, depth), F32), pltpu.SemaphoreType.DMA((tiles,))],
        compiler_params=params(44),
        cost_estimate=cost(6 * tok * depth * width * len(used), 4 * (depth * width + 2 * tok * width)),
        name="project",
    )(sides, x_hi, x_lo, weight, *extra, *after)


def local(queries, keys, values, log_decay, level_weights, norm_gain, out_weight):
    head_count = log_decay.shape[0]
    levels = level_weights.shape[1]
    n_seq = lax.axis_size("seq")
    sides = lax.axis_size("head")
    seq_bits = n_seq.bit_length() - 1
    seq_index = lax.axis_index("seq")
    size = head_count // 2

    weight = lax.all_gather(out_weight.T, "seq", axis=0, tiled=True)
    upper = (seq_index >> jnp.arange(seq_bits, dtype=jnp.int32)) & 1
    gain = norm_gain.reshape(1, -1)

    def send(block, bit):
        def wanted(s):
            above = s >> bit
            return not (bit == seq_bits - 1 and above & 1) and not (bit == seq_bits - 2 and above == 3)

        flip = 3 << bit - 1 if bit % 2 else 1 << bit
        return lax.ppermute(block, "seq", [(s, s ^ flip) for s in range(n_seq) if wanted(s)])

    small = size // 2
    early = 4

    def near(n, so_far, *after):
        return near_part(
            queries, keys, values, sums, cols, weights, levels, n * small, small, so_far, after
        )

    def first_levels(group, states, *after):
        return early_levels(upper, queries, close, weights, levels, states, group * size, after)

    a, came_a, b, came_b = [], [], [], []

    def go(blocks, came, *after):
        bit = len(blocks) - 1
        blocks.append(merged(bit, upper, blocks[bit], came[bit], after))
        came.append(send(blocks[-1], bit + 1))

    a.append(own_state(keys, values, log_decay, 0, size))
    came_a.append(send(a[0], 0))
    own_b = own_state(keys, values, log_decay, 1, size, (a[0],))
    sums, cols, weights = prepare(log_decay, level_weights, (own_b,))
    after_a, own_b = merged(0, upper, a[0], came_a[0], (weights,), own_b)
    a.append(after_a)
    came_a.append(send(a[1], 1))
    b.append(own_b)
    came_b.append(send(b[0], 0))
    close, token = near(0, None, b[0])
    go(a, came_a, token)
    go(b, came_b, a[2])
    close, token = near(1, close, b[1])
    go(a, came_a, token)
    go(b, came_b, a[3])
    close, token = near(2, close, b[2])
    go(a, came_a, token)
    go(b, came_b, a[4])
    close, token = near(3, close, b[3])
    go(b, came_b, token)
    go(a, came_a, b[4])
    far_a, before_a = first_levels(0, came_a[: early + 1], a[5])
    far_b, before_b = first_levels(1, came_b[:early], before_a)
    go(b, came_b, before_b)
    me = lax.axis_index("head").astype(jnp.int32)
    both = jnp.stack([sides - 1 - me, me])
    _, _, to_send, to_keep = finish(
        both, 2, upper, queries, far_a, before_a, weights, levels, gain, came_a[early + 1 :], 0, weight, None, (b[5],)
    )
    b_hi, b_lo, to_send = finish(
        both, 1, upper, queries, far_b, before_b, weights, levels, gain, came_b[early:], size, weight, to_send
    )
    came = lax.ppermute(to_send, "head", [(s, sides - 1 - s) for s in range(sides)])
    [to_keep] = project(both, (1,), b_hi, b_lo, weight, 1, to_keep)
    return to_keep + came


def solution(mesh):
    return jax.shard_map(
        local,
        mesh=mesh,
        in_specs=(
            P("seq", "head"),
            P("seq", "head"),
            P("seq", "head"),
            P("head", "seq"),
            P("head", None, "seq"),
            P("head"),
            P("head", "seq"),
        ),
        out_specs=P("seq", "head"),
        check_vma=False,
    )
```

```python
import functools

import jax
import jax.numpy as jnp
from jax import lax
from jax.experimental import pallas as pl
from jax.experimental.pallas import tpu as pltpu
from jax.sharding import PartitionSpec as P

HIGH = lax.Precision.HIGHEST
DH = 128
CHUNK = 128
ROWS = DH + 8
F32 = jnp.float32
BF16 = jnp.bfloat16
NT = (((1,), (1,)), ((), ()))
TN = (((0,), (0,)), ((), ()))
NN = (((1,), (0,)), ((), ()))
ANY = pl.BlockSpec(memory_space=pl.ANY)
VMEM = pl.BlockSpec(memory_space=pltpu.VMEM)
SMEM = pl.BlockSpec(memory_space=pltpu.SMEM)


def params(mib=52):
    return pltpu.CompilerParams(vmem_limit_bytes=mib * 2**20)


def cost(flops, bytes_accessed):
    return pl.CostEstimate(flops=int(flops), bytes_accessed=int(bytes_accessed), transcendentals=0)


def split(x):
    hi = x.astype(BF16)
    return hi, (x - hi.astype(F32)).astype(BF16)


def split3(x):
    hi = x.astype(BF16)
    rest = x - hi.astype(F32)
    mid = rest.astype(BF16)
    return hi, mid, (rest - mid.astype(F32)).astype(BF16)


def mm(a, b, dims):
    return lax.dot_general(a, b, dims, preferred_element_type=F32)


def mm3(a, b, dims):
    a_hi, a_lo = split(a)
    b_hi, b_lo = split(b)
    return mm(a_hi, b_hi, dims) + (mm(a_hi, b_lo, dims) + mm(a_lo, b_hi, dims))


def outer_sum(k, v):
    made = mm(jnp.concatenate(split(k), axis=1), jnp.concatenate(split(v), axis=1), TN)
    return made[:DH, :DH] + (made[:DH, DH:] + made[DH:, :DH])


def state_kernel(k_ref, v_ref, ld_ref, *refs):
    out_ref, fade_ref = refs[-2:]
    heads, tok = ld_ref.shape
    step = k_ref.shape[1] // DH
    i = pl.program_id(0)

    @pl.when(i == 0)
    def _():
        ld = ld_ref[...]
        later = lax.broadcasted_iota(jnp.int32, (tok, tok), 1) > lax.broadcasted_iota(jnp.int32, (tok, tok), 0)
        later = jnp.where(later, 1.0, 0.0).astype(BF16)
        made = mm(later, jnp.concatenate(split3(ld), axis=0), NT)
        fade = jnp.exp(made[:, :heads] + (made[:, heads : 2 * heads] + made[:, 2 * heads :]))
        for j in range(heads // step):
            fade_ref[j] = fade[:, j * step : (j + 1) * step]

    fade = fade_ref[i]
    for h in range(step):
        cols = pl.ds(h * DH, DH)
        out_ref[h, :DH, :] = outer_sum(k_ref[:, cols] * fade[:, h : h + 1], v_ref[:, cols])
        total = jnp.sum(ld_ref[pl.ds(i * step + h, 1), :], axis=1, keepdims=True)
        out_ref[h, DH:, :] = jnp.broadcast_to(total, (ROWS - DH, DH))


def own_state(keys, values, log_decay, group, heads, after=()):
    tok = keys.shape[0]
    step = 2
    steps = heads // step
    wide = pl.BlockSpec((tok, step * DH), lambda i: (0, group * steps + i))
    return pl.pallas_call(
        state_kernel,
        out_shape=jax.ShapeDtypeStruct((heads, ROWS, DH), F32),
        grid=(steps,),
        in_specs=[wide, wide, pl.BlockSpec((heads, tok), lambda i: (group, 0))] + [ANY] * len(after),
        out_specs=pl.BlockSpec((step, ROWS, DH), lambda i: (i, 0, 0)),
        scratch_shapes=[pltpu.VMEM((steps, tok, step), F32)],
        compiler_params=params(),
        cost_estimate=cost(8 * tok * heads * DH * DH, 8 * tok * heads * DH),
        name="own_state",
    )(keys, values, log_decay, *after)


def merge_kernel(bit, carries, upper_ref, mine_ref, other_ref, *refs):
    out_ref = refs[-2] if carries else refs[-1]
    upper = upper_ref[bit] == 1
    for h in range(mine_ref.shape[0]):
        mine, other = mine_ref[h], other_ref[h]
        low = jnp.where(upper, other, mine)
        high = jnp.where(upper, mine, other)
        faded = jnp.exp(high[DH : DH + 1, :])
        out_ref[h, :DH, :] = faded * low[:DH] + high[:DH]
        out_ref[h, DH:, :] = low[DH:] + high[DH:]


def merged(bit, upper, mine, other, after=(), carry=None):
    more = [] if carry is None else [carry]
    outs = pl.pallas_call(
        functools.partial(merge_kernel, bit, bool(more)),
        out_shape=[jax.ShapeDtypeStruct(mine.shape, F32)] + [jax.ShapeDtypeStruct(c.shape, F32) for c in more],
        in_specs=[SMEM, VMEM, VMEM] + [ANY] * (len(more) + len(after)),
        out_specs=[VMEM] + [ANY] * len(more),
        input_output_aliases={3: 1} if more else {},
        compiler_params=params(16),
        cost_estimate=cost(3 * mine.size, 12 * mine.size),
        name="merge",
    )(upper, mine, other, *more, *after)
    return outs if more else outs[0]


def prepare_kernel(ld_ref, w_ref, *refs):
    sums_ref, cols_ref, weights_ref = refs[-3:]
    heads, tok = ld_ref.shape
    levels = w_ref.shape[1]
    chunks = tok // CHUNK
    near_levels = tok.bit_length()
    row = lax.broadcasted_iota(jnp.int32, (CHUNK, CHUNK), 0)
    col = lax.broadcasted_iota(jnp.int32, (CHUNK, CHUNK), 1)
    upto = jnp.where(row <= col, 1.0, 0.0).astype(BF16)
    sums = []
    for m in range(chunks):
        hi, mid, low = split3(ld_ref[:, m * CHUNK : (m + 1) * CHUNK])
        sums.append(mm(hi, upto, NN) + (mm(mid, upto, NN) + mm(low, upto, NN)))
    start = jnp.zeros((heads, 1), F32)
    fulls = []
    halves = []
    for m in range(chunks):
        fulls.append(sums[m] + start)
        halves.append(sums[m] + (sums[m - 1][:, CHUNK - 1 :] if m % 4 == 3 else 0.0))
        start = start + sums[m][:, CHUNK - 1 :]
    cum = jnp.concatenate(sums, axis=1)
    one = jnp.exp(cum)
    two = jnp.exp(jnp.concatenate(halves, axis=1))
    far = jnp.exp(jnp.concatenate(fulls, axis=1))
    for h in range(heads):
        sums_ref[h] = cum[h : h + 1]
    fill = jnp.zeros((CHUNK - heads, tok), F32)
    cols_ref[...] = jnp.transpose(jnp.concatenate([cum, fill], axis=0))
    level = lax.broadcasted_iota(jnp.int32, (levels, tok), 0)
    per = CHUNK // levels
    for g in range(heads // per):
        made = []
        for h in range(g * per, (g + 1) * per):
            decay = jnp.where(level >= near_levels, far[h : h + 1], two[h : h + 1])
            decay = jnp.where(level == near_levels - 2, one[h : h + 1], decay)
            decay = jnp.where(level < near_levels - 2, 1.0, decay)
            made.append(w_ref[h] * decay)
        weights_ref[:, g * CHUNK : (g + 1) * CHUNK] = jnp.transpose(jnp.concatenate(made, axis=0))


def prepare(log_decay, level_weights, after=()):
    heads, tok = log_decay.shape
    levels = level_weights.shape[1]
    return pl.pallas_call(
        prepare_kernel,
        out_shape=(
            jax.ShapeDtypeStruct((heads, 1, tok), F32),
            jax.ShapeDtypeStruct((tok, CHUNK), F32),
            jax.ShapeDtypeStruct((tok, heads * levels), F32),
        ),
        in_specs=[VMEM, VMEM] + [ANY] * len(after),
        out_specs=[VMEM] * 3,
        compiler_params=params(),
        cost_estimate=cost(0, 8 * heads * levels * tok),
        name="prepare",
    )(log_decay, level_weights, *after)


def near_kernel(first, levels, q_ref, k_ref, v_ref, sums_ref, cols_ref, w_ref, *refs):
    out_ref, token_ref = refs[-2:]
    tok = q_ref.shape[0]
    chunks = tok // CHUNK
    tile_bits = CHUNK.bit_length() - 1
    row = lax.broadcasted_iota(jnp.int32, (CHUNK, CHUNK), 0)
    col = lax.broadcasted_iota(jnp.int32, (CHUNK, CHUNK), 1)
    apart = row ^ col
    causal = row >= col
    head = first + pl.program_id(0)
    per = CHUNK // levels
    token_ref[...] = jnp.zeros_like(token_ref)
    states = []
    ends = []
    for m in range(chunks):
        rows = pl.ds(m * CHUNK, CHUNK)
        q = q_ref[rows, :] * DH**-0.5
        k = k_ref[rows, :]
        v = v_ref[rows, :]
        w = pltpu.roll(w_ref[rows, :], (per - head % per) * levels, 1)
        c_cols = pltpu.roll(cols_ref[rows, :], CHUNK - head, 1)
        c = c_cols[:, 0:1]
        near = jnp.broadcast_to(w[:, 0:1], (CHUNK, CHUNK))
        for bit in range(tile_bits):
            near = jnp.where(apart >= 2**bit, w[:, bit + 1 : bit + 2], near)
        gap = jnp.where(causal, c - sums_ref[0, :, m * CHUNK : (m + 1) * CHUNK], -1e30)
        q_hi, q_lo = split(q)
        k_hi, k_lo = split(k)
        q_both = jnp.concatenate([q_hi, q_lo], axis=1)
        scores = mm(q_both, jnp.concatenate([k_hi, k_hi], axis=1), NT) + mm(q_hi, k_lo, NT)
        scores = scores * (near * jnp.exp(gap))
        s_hi, s_lo = split(scores)
        v_hi, v_lo = split(v)
        s_both = jnp.concatenate([s_hi, s_lo], axis=1)
        out = mm(s_both, jnp.concatenate([v_hi, v_hi], axis=0), NN) + mm(s_hi, v_lo, NN)
        for bit in range(2):
            if m >> bit & 1:
                at = (m >> bit) - 1 << bit
                seen = states[at]
                for n in range(at + 1, at + 2**bit):
                    seen = jnp.exp(ends[n]) * seen + states[n]
                level = tile_bits + 1 + bit
                s_hi, s_lo = split(seen)
                made = mm(q_both, jnp.concatenate([s_hi, s_hi], axis=0), NN) + mm(q_hi, s_lo, NN)
                out = out + w[:, level : level + 1] * made
        out_ref[rows, :] = out
        if m < chunks - 1:
            end = c[CHUNK - 1 : CHUNK]
            states.append(outer_sum(k * jnp.exp(end - c), v))
            ends.append(end)


def near_part(queries, keys, values, sums, cols, weights, levels, first, heads, so_far=None, after=()):
    tok = queries.shape[0]
    per = CHUNK // levels
    one = pl.BlockSpec((tok, DH), lambda h: (0, first + h))
    more = [] if so_far is None else [so_far]
    return pl.pallas_call(
        functools.partial(near_kernel, first, levels),
        out_shape=(
            jax.ShapeDtypeStruct(queries.shape, F32),
            jax.ShapeDtypeStruct((8, CHUNK), F32),
        ),
        grid=(heads,),
        in_specs=[
            one,
            one,
            one,
            pl.BlockSpec((1, 1, tok), lambda h: (first + h, 0, 0)),
            pl.BlockSpec(cols.shape, lambda h: (0, 0)),
            pl.BlockSpec((tok, CHUNK), lambda h: (0, (first + h) // per)),
        ]
        + [ANY] * (len(more) + len(after)),
        out_specs=[one, pl.BlockSpec((8, CHUNK), lambda h: (0, 0))],
        input_output_aliases={6: 0} if more else {},
        compiler_params=params(),
        cost_estimate=cost(60 * tok * heads * DH * DH, 16 * tok * heads * DH),
        name="near",
    )(queries, keys, values, sums, cols, weights, *more, *after)


def add_levels(q_hi, q_lo, out, w, first_column, states):
    parts = []
    for state in states:
        hi, lo = split(state)
        parts.append(jnp.concatenate([hi, hi, lo], axis=0))
    made = mm(jnp.concatenate([q_hi, q_lo, q_hi], axis=1), jnp.concatenate(parts, axis=1), NN)
    for n in range(len(parts)):
        at = first_column + n
        out = out + w[:, at : at + 1] * made[:, n * DH : (n + 1) * DH]
    return out


def early_kernel(first, levels, count, upper_ref, q_ref, near_ref, w_ref, *refs):
    out_ref, before_ref = refs[-2:]
    step = q_ref.shape[1] // DH
    per = CHUNK // levels
    total = upper_ref.shape[0]
    head = first + pl.program_id(0) * step
    w = pltpu.roll(w_ref[...], (per - head % per) * levels, 1)
    for h in range(step):
        cols = pl.ds(h * DH, DH)
        q_hi, q_lo = split(q_ref[:, cols] * DH**-0.5)
        before = jnp.zeros((1, DH), F32)
        states = []
        for level in range(count):
            upper = upper_ref[level] == 1
            reach = jnp.where(upper, jnp.exp(before), 0.0)
            states.append(refs[level][h, :DH, :] * reach)
            before = before + jnp.where(upper, refs[level][h, DH : DH + 1, :], 0.0)
        out_ref[:, cols] = add_levels(q_hi, q_lo, near_ref[:, cols], w, h * levels + levels - total, states)
        before_ref[h] = jnp.broadcast_to(before, before_ref.shape[1:])


def early_levels(upper, queries, near, weights, levels, states, first, after=()):
    heads = states[0].shape[0]
    tok = queries.shape[0]
    per = CHUNK // levels
    step = 2
    wide = pl.BlockSpec((tok, step * DH), lambda i: (0, first // step + i))
    return pl.pallas_call(
        functools.partial(early_kernel, first, levels, len(states)),
        out_shape=(
            jax.ShapeDtypeStruct((tok, heads * DH), F32),
            jax.ShapeDtypeStruct((heads, 8, DH), F32),
        ),
        grid=(heads // step,),
        in_specs=[
            SMEM,
            wide,
            wide,
            pl.BlockSpec((tok, CHUNK), lambda i: (0, (first + i * step) // per)),
        ]
        + [pl.BlockSpec((step, ROWS, DH), lambda i: (i, 0, 0))] * len(states)
        + [ANY] * len(after),
        out_specs=[
            pl.BlockSpec((tok, step * DH), lambda i: (0, i)),
            pl.BlockSpec((step, 8, DH), lambda i: (i, 0, 0)),
        ],
        compiler_params=params(),
        cost_estimate=cost(8 * len(states) * tok * heads * DH * DH, 16 * tok * heads * DH),
        name="early",
    )(upper, queries, near, weights, *states, *after)


TILE = 256


def tile_copy(side, steps, part, j, w_ref, buffer_ref, sems, slot):
    depth = buffer_ref.shape[2]
    rows = pl.ds(pl.multiple_of((side * steps + j) * TILE, TILE), TILE)
    return pltpu.make_async_copy(
        w_ref.at[rows, pl.ds(part * depth, depth)], buffer_ref.at[slot], sems.at[slot]
    )


def project_tiles(side, steps, part, w_ref, buffer_ref, sems, slot, x_hi, x_lo, more_ref, out_ref):
    @pl.loop(0, steps)
    def _(j):
        tile_copy(side, steps, part, j, w_ref, buffer_ref, sems, slot + j).wait()
        w_hi, w_lo = split(buffer_ref[slot + j])
        cols = pl.ds(pl.multiple_of(j * TILE, TILE), TILE)
        made = mm(x_hi[...], w_hi, NT) + (mm(x_hi[...], w_lo, NT) + mm(x_lo[...], w_hi, NT))
        if more_ref is not None:
            made = made + more_ref[:, cols]
        out_ref[:, cols] = made


def finish_kernel(first, levels, skip, tiles, upper_ref, q_ref, near_ref, before_ref, w_ref, gain_ref, *refs):
    total = upper_ref.shape[0]
    states, refs = refs[: total - skip], refs[total - skip :]
    if tiles:
        sides_ref, weight_ref, more_ref, x_hi, x_lo, send_ref, q_buffer, q_sems, buffer_ref, sems = refs
    else:
        x_hi, x_lo, token_ref, q_buffer, q_sems = refs[-5:]
        token_ref[...] = jnp.zeros_like(token_ref)
    heads = states[0].shape[0]
    part = first // heads
    pair = 2

    def q_copy(n):
        cols = pl.ds(pl.multiple_of((first + n * pair) * DH, pair * DH), pair * DH)
        return pltpu.make_async_copy(q_ref.at[:, cols], q_buffer.at[n], q_sems.at[n])

    for n in range(heads // pair):
        q_copy(n).start()
    for j in range(tiles):
        tile_copy(sides_ref[0], tiles, part, j, weight_ref, buffer_ref, sems, j).start()

    per = CHUNK // levels

    @pl.loop(0, heads // pair)
    def _(n):
        q_copy(n).wait()
        group = pl.multiple_of((first + n * pair) // per * CHUNK, CHUNK)
        w = pltpu.roll(w_ref[:, pl.ds(group, CHUNK)], (per - (first + n * pair) % per) * levels, 1)
        for i in range(pair):
            h = n * pair + i
            cols = pl.ds(pl.multiple_of(h * DH, DH), DH)
            all_cols = pl.ds(pl.multiple_of((first + h) * DH, DH), DH)
            q_hi, q_lo = split(q_buffer[n, :, i * DH : (i + 1) * DH] * DH**-0.5)
            before = before_ref[h, 0:1, :]
            scaled = []
            for m, ref in enumerate(states):
                upper = upper_ref[skip + m] == 1
                scaled.append(ref[h, :DH, :] * jnp.where(upper, jnp.exp(before), 0.0))
                before = before + jnp.where(upper, ref[h, DH : DH + 1, :], 0.0)
            column = i * levels + levels - total + skip
            out = add_levels(q_hi, q_lo, near_ref[:, cols], w, column, scaled)
            squares = jnp.concatenate(split(out * out), axis=1)
            mean = mm(squares, jnp.full((2 * DH, DH), 1.0 / DH, BF16), NN)
            out = out * lax.rsqrt(mean + 1e-06) * gain_ref[:, all_cols]
            hi, lo = split(out)
            x_hi[:, cols] = hi
            x_lo[:, cols] = lo

    if tiles:
        project_tiles(
            sides_ref[0], tiles, part, weight_ref, buffer_ref, sems, 0, x_hi, x_lo, more_ref, send_ref
        )


def finish(upper, queries, near, before, weights, levels, gain, states, first, sides=None, weight=None, more=None, after=()):
    heads = states[0].shape[0]
    tok = queries.shape[0]
    depth = heads * DH
    skip = upper.shape[0] - len(states)
    half = jax.ShapeDtypeStruct((tok, depth), BF16)
    tiles = 0 if weight is None else more.shape[1] // TILE
    extra = [sides, weight, more] if tiles else []
    outs = [half, half, jax.ShapeDtypeStruct(more.shape if tiles else (8, CHUNK), F32)]
    return pl.pallas_call(
        functools.partial(finish_kernel, first, levels, skip, tiles),
        out_shape=outs,
        in_specs=[SMEM, ANY]
        + [VMEM] * (4 + len(states))
        + ([SMEM, ANY, VMEM] if tiles else [])
        + [ANY] * len(after),
        out_specs=[VMEM] * len(outs),
        scratch_shapes=[
            pltpu.VMEM((heads // 2, tok, 2 * DH), F32),
            pltpu.SemaphoreType.DMA((heads // 2,)),
        ]
        + ([pltpu.VMEM((tiles, TILE, depth), F32), pltpu.SemaphoreType.DMA((tiles,))] if tiles else []),
        compiler_params=params(44),
        cost_estimate=cost(8 * tok * depth * DH + 6 * tok * depth * tiles * TILE, 16 * tok * depth),
        name="finish",
    )(upper, queries, near, before, weights, gain, *states, *extra, *after)


def project_kernel(part, used, more, sides_ref, x_hi, x_lo, weight_ref, *refs):
    *out_refs, buffer_ref, sems = refs[-(len(used) + 2) :]
    steps = out_refs[0].shape[1] // TILE
    for n, side in enumerate(used):
        for j in range(steps):
            tile_copy(sides_ref[side], steps, part, j, weight_ref, buffer_ref, sems, n * steps + j).start()
    for n, side in enumerate(used):
        project_tiles(
            sides_ref[side],
            steps,
            part,
            weight_ref,
            buffer_ref,
            sems,
            n * steps,
            x_hi,
            x_lo,
            refs[0] if more else None,
            out_refs[n],
        )


def project(sides, used, x_hi, x_lo, weight, part, more=None, after=()):
    tok, depth = x_hi.shape
    width = weight.shape[0] // 2
    tiles = len(used) * width // TILE
    extra = [] if more is None else [more]
    return pl.pallas_call(
        functools.partial(project_kernel, part, used, bool(extra)),
        out_shape=[jax.ShapeDtypeStruct((tok, width), F32)] * len(used),
        in_specs=[SMEM, VMEM, VMEM, ANY] + [VMEM] * len(extra) + [ANY] * len(after),
        out_specs=[VMEM] * len(used),
        scratch_shapes=[pltpu.VMEM((tiles, TILE, depth), F32), pltpu.SemaphoreType.DMA((tiles,))],
        compiler_params=params(44),
        cost_estimate=cost(6 * tok * depth * width * len(used), 4 * (depth * width + 2 * tok * width)),
        name="project",
    )(sides, x_hi, x_lo, weight, *extra, *after)


def local(queries, keys, values, log_decay, level_weights, norm_gain, out_weight):
    head_count = log_decay.shape[0]
    levels = level_weights.shape[1]
    n_seq = lax.axis_size("seq")
    sides = lax.axis_size("head")
    seq_bits = n_seq.bit_length() - 1
    seq_index = lax.axis_index("seq")
    size = head_count // 2

    weight = lax.all_gather(out_weight.T, "seq", axis=0, tiled=True)
    upper = (seq_index >> jnp.arange(seq_bits, dtype=jnp.int32)) & 1
    gain = norm_gain.reshape(1, -1)

    def send(block, bit):
        def wanted(s):
            above = s >> bit
            return not (bit == seq_bits - 1 and above & 1) and not (bit == seq_bits - 2 and above == 3)

        flip = 3 << bit - 1 if bit % 2 else 1 << bit
        return lax.ppermute(block, "seq", [(s, s ^ flip) for s in range(n_seq) if wanted(s)])

    small = size // 2
    early = 4

    def near(n, so_far, *after):
        return near_part(
            queries, keys, values, sums, cols, weights, levels, n * small, small, so_far, after
        )

    def first_levels(group, states, *after):
        return early_levels(upper, queries, close, weights, levels, states, group * size, after)

    a, came_a, b, came_b = [], [], [], []

    def go(blocks, came, *after):
        bit = len(blocks) - 1
        blocks.append(merged(bit, upper, blocks[bit], came[bit], after))
        came.append(send(blocks[-1], bit + 1))

    a.append(own_state(keys, values, log_decay, 0, size))
    came_a.append(send(a[0], 0))
    own_b = own_state(keys, values, log_decay, 1, size, (a[0],))
    sums, cols, weights = prepare(log_decay, level_weights, (own_b,))
    after_a, own_b = merged(0, upper, a[0], came_a[0], (weights,), own_b)
    a.append(after_a)
    came_a.append(send(a[1], 1))
    b.append(own_b)
    came_b.append(send(b[0], 0))
    close, token = near(0, None, b[0])
    go(a, came_a, token)
    go(b, came_b, a[2])
    close, token = near(1, close, b[1])
    go(a, came_a, token)
    go(b, came_b, a[3])
    close, token = near(2, close, b[2])
    go(a, came_a, token)
    go(b, came_b, a[4])
    close, token = near(3, close, b[3])
    far_a, before_a = first_levels(0, came_a[:early], token)
    go(a, came_a, before_a)
    go(b, came_b, a[5])
    far_b, before_b = first_levels(1, came_b[:early], b[4])
    a_hi, a_lo, token = finish(
        upper, queries, far_a, before_a, weights, levels, gain, came_a[early:], 0, after=(before_b,)
    )
    go(b, came_b, token)

    me = lax.axis_index("head").astype(jnp.int32)
    both = jnp.stack([sides - 1 - me, me])
    to_send, to_keep = project(both, (0, 1), a_hi, a_lo, weight, 0, after=(b[5],))
    b_hi, b_lo, to_send = finish(
        upper, queries, far_b, before_b, weights, levels, gain, came_b[early:], size, both, weight, to_send
    )
    came = lax.ppermute(to_send, "head", [(s, sides - 1 - s) for s in range(sides)])
    [to_keep] = project(both, (1,), b_hi, b_lo, weight, 1, to_keep)
    return to_keep + came


def solution(mesh):
    return jax.shard_map(
        local,
        mesh=mesh,
        in_specs=(
            P("seq", "head"),
            P("seq", "head"),
            P("seq", "head"),
            P("head", "seq"),
            P("head", None, "seq"),
            P("head"),
            P("head", "seq"),
        ),
        out_specs=P("seq", "head"),
        check_vma=False,
    )
```

```python
import functools

import jax
import jax.numpy as jnp
from jax import lax
from jax.experimental import pallas as pl
from jax.experimental.pallas import tpu as pltpu
from jax.sharding import PartitionSpec as P

HIGH = lax.Precision.HIGHEST
DH = 128
CHUNK = 128
ROWS = DH + 8
F32 = jnp.float32
BF16 = jnp.bfloat16
NT = (((1,), (1,)), ((), ()))
TN = (((0,), (0,)), ((), ()))
NN = (((1,), (0,)), ((), ()))
ANY = pl.BlockSpec(memory_space=pl.ANY)
VMEM = pl.BlockSpec(memory_space=pltpu.VMEM)
SMEM = pl.BlockSpec(memory_space=pltpu.SMEM)


def params(mib=52):
    return pltpu.CompilerParams(vmem_limit_bytes=mib * 2**20)


def cost(flops, bytes_accessed):
    return pl.CostEstimate(flops=int(flops), bytes_accessed=int(bytes_accessed), transcendentals=0)


def split(x):
    hi = x.astype(BF16)
    return hi, (x - hi.astype(F32)).astype(BF16)


def split3(x):
    hi = x.astype(BF16)
    rest = x - hi.astype(F32)
    mid = rest.astype(BF16)
    return hi, mid, (rest - mid.astype(F32)).astype(BF16)


def mm(a, b, dims):
    return lax.dot_general(a, b, dims, preferred_element_type=F32)


def mm3(a, b, dims):
    a_hi, a_lo = split(a)
    b_hi, b_lo = split(b)
    return mm(a_hi, b_hi, dims) + (mm(a_hi, b_lo, dims) + mm(a_lo, b_hi, dims))


def outer_sum(k, v):
    made = mm(jnp.concatenate(split(k), axis=1), jnp.concatenate(split(v), axis=1), TN)
    return made[:DH, :DH] + (made[:DH, DH:] + made[DH:, :DH])


def state_kernel(k_ref, v_ref, ld_ref, *refs):
    out_ref, fade_ref = refs[-2:]
    heads, tok = ld_ref.shape
    step = k_ref.shape[1] // DH
    i = pl.program_id(0)

    @pl.when(i == 0)
    def _():
        ld = ld_ref[...]
        later = lax.broadcasted_iota(jnp.int32, (tok, tok), 1) > lax.broadcasted_iota(jnp.int32, (tok, tok), 0)
        later = jnp.where(later, 1.0, 0.0).astype(BF16)
        made = mm(later, jnp.concatenate(split3(ld), axis=0), NT)
        fade = jnp.exp(made[:, :heads] + (made[:, heads : 2 * heads] + made[:, 2 * heads :]))
        for j in range(heads // step):
            fade_ref[j] = fade[:, j * step : (j + 1) * step]

    fade = fade_ref[i]
    for h in range(step):
        cols = pl.ds(h * DH, DH)
        out_ref[h, :DH, :] = outer_sum(k_ref[:, cols] * fade[:, h : h + 1], v_ref[:, cols])
        total = jnp.sum(ld_ref[pl.ds(i * step + h, 1), :], axis=1, keepdims=True)
        out_ref[h, DH:, :] = jnp.broadcast_to(total, (ROWS - DH, DH))


def own_state(keys, values, log_decay, group, heads, after=()):
    tok = keys.shape[0]
    step = 2
    steps = heads // step
    wide = pl.BlockSpec((tok, step * DH), lambda i: (0, group * steps + i))
    return pl.pallas_call(
        state_kernel,
        out_shape=jax.ShapeDtypeStruct((heads, ROWS, DH), F32),
        grid=(steps,),
        in_specs=[wide, wide, pl.BlockSpec((heads, tok), lambda i: (group, 0))] + [ANY] * len(after),
        out_specs=pl.BlockSpec((step, ROWS, DH), lambda i: (i, 0, 0)),
        scratch_shapes=[pltpu.VMEM((steps, tok, step), F32)],
        compiler_params=params(),
        cost_estimate=cost(8 * tok * heads * DH * DH, 8 * tok * heads * DH),
        name="own_state",
    )(keys, values, log_decay, *after)


def merge_kernel(bit, carries, upper_ref, mine_ref, other_ref, *refs):
    out_ref = refs[-2] if carries else refs[-1]
    upper = upper_ref[bit] == 1
    for h in range(mine_ref.shape[0]):
        mine, other = mine_ref[h], other_ref[h]
        low = jnp.where(upper, other, mine)
        high = jnp.where(upper, mine, other)
        faded = jnp.exp(high[DH : DH + 1, :])
        out_ref[h, :DH, :] = faded * low[:DH] + high[:DH]
        out_ref[h, DH:, :] = low[DH:] + high[DH:]


def merged(bit, upper, mine, other, after=(), carry=None):
    more = [] if carry is None else [carry]
    outs = pl.pallas_call(
        functools.partial(merge_kernel, bit, bool(more)),
        out_shape=[jax.ShapeDtypeStruct(mine.shape, F32)] + [jax.ShapeDtypeStruct(c.shape, F32) for c in more],
        in_specs=[SMEM, VMEM, VMEM] + [ANY] * (len(more) + len(after)),
        out_specs=[VMEM] + [ANY] * len(more),
        input_output_aliases={3: 1} if more else {},
        compiler_params=params(16),
        cost_estimate=cost(3 * mine.size, 12 * mine.size),
        name="merge",
    )(upper, mine, other, *more, *after)
    return outs if more else outs[0]


def prepare_kernel(ld_ref, w_ref, *refs):
    sums_ref, cols_ref, weights_ref = refs[-3:]
    heads, tok = ld_ref.shape
    levels = w_ref.shape[1]
    chunks = tok // CHUNK
    near_levels = tok.bit_length()
    row = lax.broadcasted_iota(jnp.int32, (CHUNK, CHUNK), 0)
    col = lax.broadcasted_iota(jnp.int32, (CHUNK, CHUNK), 1)
    upto = jnp.where(row <= col, 1.0, 0.0).astype(BF16)
    sums = []
    for m in range(chunks):
        hi, mid, low = split3(ld_ref[:, m * CHUNK : (m + 1) * CHUNK])
        sums.append(mm(hi, upto, NN) + (mm(mid, upto, NN) + mm(low, upto, NN)))
    start = jnp.zeros((heads, 1), F32)
    fulls = []
    halves = []
    for m in range(chunks):
        fulls.append(sums[m] + start)
        halves.append(sums[m] + (sums[m - 1][:, CHUNK - 1 :] if m % 4 == 3 else 0.0))
        start = start + sums[m][:, CHUNK - 1 :]
    cum = jnp.concatenate(sums, axis=1)
    one = jnp.exp(cum)
    two = jnp.exp(jnp.concatenate(halves, axis=1))
    far = jnp.exp(jnp.concatenate(fulls, axis=1))
    for h in range(heads):
        sums_ref[h] = cum[h : h + 1]
    fill = jnp.zeros((CHUNK - heads, tok), F32)
    cols_ref[...] = jnp.transpose(jnp.concatenate([cum, fill], axis=0))
    level = lax.broadcasted_iota(jnp.int32, (levels, tok), 0)
    per = CHUNK // levels
    for g in range(heads // per):
        made = []
        for h in range(g * per, (g + 1) * per):
            decay = jnp.where(level >= near_levels, far[h : h + 1], two[h : h + 1])
            decay = jnp.where(level == near_levels - 2, one[h : h + 1], decay)
            decay = jnp.where(level < near_levels - 2, 1.0, decay)
            made.append(w_ref[h] * decay)
        weights_ref[:, g * CHUNK : (g + 1) * CHUNK] = jnp.transpose(jnp.concatenate(made, axis=0))


def prepare(log_decay, level_weights, after=()):
    heads, tok = log_decay.shape
    levels = level_weights.shape[1]
    return pl.pallas_call(
        prepare_kernel,
        out_shape=(
            jax.ShapeDtypeStruct((heads, 1, tok), F32),
            jax.ShapeDtypeStruct((tok, CHUNK), F32),
            jax.ShapeDtypeStruct((tok, heads * levels), F32),
        ),
        in_specs=[VMEM, VMEM] + [ANY] * len(after),
        out_specs=[VMEM] * 3,
        compiler_params=params(),
        cost_estimate=cost(0, 8 * heads * levels * tok),
        name="prepare",
    )(log_decay, level_weights, *after)


def near_kernel(first, levels, q_ref, k_ref, v_ref, sums_ref, cols_ref, w_ref, *refs):
    out_ref, token_ref = refs[-2:]
    tok = q_ref.shape[0]
    chunks = tok // CHUNK
    tile_bits = CHUNK.bit_length() - 1
    row = lax.broadcasted_iota(jnp.int32, (CHUNK, CHUNK), 0)
    col = lax.broadcasted_iota(jnp.int32, (CHUNK, CHUNK), 1)
    apart = row ^ col
    causal = row >= col
    head = first + pl.program_id(0)
    per = CHUNK // levels
    token_ref[...] = jnp.zeros_like(token_ref)
    states = []
    ends = []
    for m in range(chunks):
        rows = pl.ds(m * CHUNK, CHUNK)
        q = q_ref[rows, :] * DH**-0.5
        k = k_ref[rows, :]
        v = v_ref[rows, :]
        w = pltpu.roll(w_ref[rows, :], (per - head % per) * levels, 1)
        c_cols = pltpu.roll(cols_ref[rows, :], CHUNK - head, 1)
        c = c_cols[:, 0:1]
        near = jnp.broadcast_to(w[:, 0:1], (CHUNK, CHUNK))
        for bit in range(tile_bits):
            near = jnp.where(apart >= 2**bit, w[:, bit + 1 : bit + 2], near)
        gap = jnp.where(causal, c - sums_ref[0, :, m * CHUNK : (m + 1) * CHUNK], -1e30)
        q_hi, q_lo = split(q)
        k_hi, k_lo = split(k)
        q_both = jnp.concatenate([q_hi, q_lo], axis=1)
        scores = mm(q_both, jnp.concatenate([k_hi, k_hi], axis=1), NT) + mm(q_hi, k_lo, NT)
        scores = scores * (near * jnp.exp(gap))
        s_hi, s_lo = split(scores)
        v_hi, v_lo = split(v)
        s_both = jnp.concatenate([s_hi, s_lo], axis=1)
        out = mm(s_both, jnp.concatenate([v_hi, v_hi], axis=0), NN) + mm(s_hi, v_lo, NN)
        for bit in range(2):
            if m >> bit & 1:
                at = (m >> bit) - 1 << bit
                seen = states[at]
                for n in range(at + 1, at + 2**bit):
                    seen = jnp.exp(ends[n]) * seen + states[n]
                level = tile_bits + 1 + bit
                s_hi, s_lo = split(seen)
                made = mm(q_both, jnp.concatenate([s_hi, s_hi], axis=0), NN) + mm(q_hi, s_lo, NN)
                out = out + w[:, level : level + 1] * made
        out_ref[rows, :] = out
        if m < chunks - 1:
            end = c[CHUNK - 1 : CHUNK]
            states.append(outer_sum(k * jnp.exp(end - c), v))
            ends.append(end)


def near_part(queries, keys, values, sums, cols, weights, levels, first, heads, so_far=None, after=()):
    tok = queries.shape[0]
    per = CHUNK // levels
    one = pl.BlockSpec((tok, DH), lambda h: (0, first + h))
    more = [] if so_far is None else [so_far]
    return pl.pallas_call(
        functools.partial(near_kernel, first, levels),
        out_shape=(
            jax.ShapeDtypeStruct(queries.shape, F32),
            jax.ShapeDtypeStruct((8, CHUNK), F32),
        ),
        grid=(heads,),
        in_specs=[
            one,
            one,
            one,
            pl.BlockSpec((1, 1, tok), lambda h: (first + h, 0, 0)),
            pl.BlockSpec(cols.shape, lambda h: (0, 0)),
            pl.BlockSpec((tok, CHUNK), lambda h: (0, (first + h) // per)),
        ]
        + [ANY] * (len(more) + len(after)),
        out_specs=[one, pl.BlockSpec((8, CHUNK), lambda h: (0, 0))],
        input_output_aliases={6: 0} if more else {},
        compiler_params=params(),
        cost_estimate=cost(60 * tok * heads * DH * DH, 16 * tok * heads * DH),
        name="near",
    )(queries, keys, values, sums, cols, weights, *more, *after)


def add_levels(q_hi, q_lo, out, w, first_column, states):
    parts = []
    for state in states:
        hi, lo = split(state)
        parts.append(jnp.concatenate([hi, hi, lo], axis=0))
    made = mm(jnp.concatenate([q_hi, q_lo, q_hi], axis=1), jnp.concatenate(parts, axis=1), NN)
    for n in range(len(parts)):
        at = first_column + n
        out = out + w[:, at : at + 1] * made[:, n * DH : (n + 1) * DH]
    return out


def early_kernel(first, levels, count, upper_ref, q_ref, near_ref, w_ref, *refs):
    out_ref, before_ref = refs[-2:]
    step = q_ref.shape[1] // DH
    per = CHUNK // levels
    total = upper_ref.shape[0]
    head = first + pl.program_id(0) * step
    w = pltpu.roll(w_ref[...], (per - head % per) * levels, 1)
    for h in range(step):
        cols = pl.ds(h * DH, DH)
        q_hi, q_lo = split(q_ref[:, cols] * DH**-0.5)
        before = jnp.zeros((1, DH), F32)
        states = []
        for level in range(count):
            upper = upper_ref[level] == 1
            reach = jnp.where(upper, jnp.exp(before), 0.0)
            states.append(refs[level][h, :DH, :] * reach)
            before = before + jnp.where(upper, refs[level][h, DH : DH + 1, :], 0.0)
        out_ref[:, cols] = add_levels(q_hi, q_lo, near_ref[:, cols], w, h * levels + levels - total, states)
        before_ref[h] = jnp.broadcast_to(before, before_ref.shape[1:])


def early_levels(upper, queries, near, weights, levels, states, first, after=()):
    heads = states[0].shape[0]
    tok = queries.shape[0]
    per = CHUNK // levels
    step = 2
    wide = pl.BlockSpec((tok, step * DH), lambda i: (0, first // step + i))
    return pl.pallas_call(
        functools.partial(early_kernel, first, levels, len(states)),
        out_shape=(
            jax.ShapeDtypeStruct((tok, heads * DH), F32),
            jax.ShapeDtypeStruct((heads, 8, DH), F32),
        ),
        grid=(heads // step,),
        in_specs=[
            SMEM,
            wide,
            wide,
            pl.BlockSpec((tok, CHUNK), lambda i: (0, (first + i * step) // per)),
        ]
        + [pl.BlockSpec((step, ROWS, DH), lambda i: (i, 0, 0))] * len(states)
        + [ANY] * len(after),
        out_specs=[
            pl.BlockSpec((tok, step * DH), lambda i: (0, i)),
            pl.BlockSpec((step, 8, DH), lambda i: (i, 0, 0)),
        ],
        compiler_params=params(),
        cost_estimate=cost(8 * len(states) * tok * heads * DH * DH, 16 * tok * heads * DH),
        name="early",
    )(upper, queries, near, weights, *states, *after)


TILE = 256


def tile_copy(side, steps, part, j, w_ref, buffer_ref, sems, slot):
    depth = buffer_ref.shape[2]
    rows = pl.ds(pl.multiple_of((side * steps + j) * TILE, TILE), TILE)
    return pltpu.make_async_copy(
        w_ref.at[rows, pl.ds(part * depth, depth)], buffer_ref.at[slot], sems.at[slot]
    )


def project_tiles(side, steps, part, w_ref, buffer_ref, sems, slot, x_hi, x_lo, more_ref, out_ref):
    @pl.loop(0, steps)
    def _(j):
        tile_copy(side, steps, part, j, w_ref, buffer_ref, sems, slot + j).wait()
        w_hi, w_lo = split(buffer_ref[slot + j])
        cols = pl.ds(pl.multiple_of(j * TILE, TILE), TILE)
        made = mm(x_hi[...], w_hi, NT) + (mm(x_hi[...], w_lo, NT) + mm(x_lo[...], w_hi, NT))
        if more_ref is not None:
            made = made + more_ref[:, cols]
        out_ref[:, cols] = made


def finish_kernel(first, levels, skip, tiles, upper_ref, q_ref, near_ref, before_ref, w_ref, gain_ref, *refs):
    total = upper_ref.shape[0]
    states, refs = refs[: total - skip], refs[total - skip :]
    if tiles:
        sides_ref, weight_ref, more_ref, x_hi, x_lo, send_ref, q_buffer, q_sems, buffer_ref, sems = refs
    else:
        x_hi, x_lo, token_ref, q_buffer, q_sems = refs[-5:]
        token_ref[...] = jnp.zeros_like(token_ref)
    heads = states[0].shape[0]
    part = first // heads
    pair = 2

    def q_copy(n):
        cols = pl.ds(pl.multiple_of((first + n * pair) * DH, pair * DH), pair * DH)
        return pltpu.make_async_copy(q_ref.at[:, cols], q_buffer.at[n], q_sems.at[n])

    for n in range(heads // pair):
        q_copy(n).start()
    for j in range(tiles):
        tile_copy(sides_ref[0], tiles, part, j, weight_ref, buffer_ref, sems, j).start()

    per = CHUNK // levels

    @pl.loop(0, heads // pair)
    def _(n):
        q_copy(n).wait()
        group = pl.multiple_of((first + n * pair) // per * CHUNK, CHUNK)
        w = pltpu.roll(w_ref[:, pl.ds(group, CHUNK)], (per - (first + n * pair) % per) * levels, 1)
        for i in range(pair):
            h = n * pair + i
            cols = pl.ds(pl.multiple_of(h * DH, DH), DH)
            all_cols = pl.ds(pl.multiple_of((first + h) * DH, DH), DH)
            q_hi, q_lo = split(q_buffer[n, :, i * DH : (i + 1) * DH] * DH**-0.5)
            before = before_ref[h, 0:1, :]
            scaled = []
            for m, ref in enumerate(states):
                upper = upper_ref[skip + m] == 1
                scaled.append(ref[h, :DH, :] * jnp.where(upper, jnp.exp(before), 0.0))
                before = before + jnp.where(upper, ref[h, DH : DH + 1, :], 0.0)
            column = i * levels + levels - total + skip
            out = add_levels(q_hi, q_lo, near_ref[:, cols], w, column, scaled)
            squares = jnp.concatenate(split(out * out), axis=1)
            mean = mm(squares, jnp.full((2 * DH, DH), 1.0 / DH, BF16), NN)
            out = out * lax.rsqrt(mean + 1e-06) * gain_ref[:, all_cols]
            hi, lo = split(out)
            x_hi[:, cols] = hi
            x_lo[:, cols] = lo

    if tiles:
        project_tiles(
            sides_ref[0], tiles, part, weight_ref, buffer_ref, sems, 0, x_hi, x_lo, more_ref, send_ref
        )


def finish(upper, queries, near, before, weights, levels, gain, states, first, sides=None, weight=None, more=None, after=()):
    heads = states[0].shape[0]
    tok = queries.shape[0]
    depth = heads * DH
    skip = upper.shape[0] - len(states)
    half = jax.ShapeDtypeStruct((tok, depth), BF16)
    tiles = 0 if weight is None else more.shape[1] // TILE
    extra = [sides, weight, more] if tiles else []
    outs = [half, half, jax.ShapeDtypeStruct(more.shape if tiles else (8, CHUNK), F32)]
    return pl.pallas_call(
        functools.partial(finish_kernel, first, levels, skip, tiles),
        out_shape=outs,
        in_specs=[SMEM, ANY]
        + [VMEM] * (4 + len(states))
        + ([SMEM, ANY, VMEM] if tiles else [])
        + [ANY] * len(after),
        out_specs=[VMEM] * len(outs),
        scratch_shapes=[
            pltpu.VMEM((heads // 2, tok, 2 * DH), F32),
            pltpu.SemaphoreType.DMA((heads // 2,)),
        ]
        + ([pltpu.VMEM((tiles, TILE, depth), F32), pltpu.SemaphoreType.DMA((tiles,))] if tiles else []),
        compiler_params=params(44),
        cost_estimate=cost(8 * tok * depth * DH + 6 * tok * depth * tiles * TILE, 16 * tok * depth),
        name="finish",
    )(upper, queries, near, before, weights, gain, *states, *extra, *after)


def project_kernel(part, used, more, sides_ref, x_hi, x_lo, weight_ref, *refs):
    *out_refs, buffer_ref, sems = refs[-(len(used) + 2) :]
    steps = out_refs[0].shape[1] // TILE
    for n, side in enumerate(used):
        for j in range(steps):
            tile_copy(sides_ref[side], steps, part, j, weight_ref, buffer_ref, sems, n * steps + j).start()
    for n, side in enumerate(used):
        project_tiles(
            sides_ref[side],
            steps,
            part,
            weight_ref,
            buffer_ref,
            sems,
            n * steps,
            x_hi,
            x_lo,
            refs[0] if more else None,
            out_refs[n],
        )


def project(sides, used, x_hi, x_lo, weight, part, more=None, after=()):
    tok, depth = x_hi.shape
    width = weight.shape[0] // 2
    tiles = len(used) * width // TILE
    extra = [] if more is None else [more]
    return pl.pallas_call(
        functools.partial(project_kernel, part, used, bool(extra)),
        out_shape=[jax.ShapeDtypeStruct((tok, width), F32)] * len(used),
        in_specs=[SMEM, VMEM, VMEM, ANY] + [VMEM] * len(extra) + [ANY] * len(after),
        out_specs=[VMEM] * len(used),
        scratch_shapes=[pltpu.VMEM((tiles, TILE, depth), F32), pltpu.SemaphoreType.DMA((tiles,))],
        compiler_params=params(44),
        cost_estimate=cost(6 * tok * depth * width * len(used), 4 * (depth * width + 2 * tok * width)),
        name="project",
    )(sides, x_hi, x_lo, weight, *extra, *after)


def local(queries, keys, values, log_decay, level_weights, norm_gain, out_weight):
    head_count = log_decay.shape[0]
    levels = level_weights.shape[1]
    n_seq = lax.axis_size("seq")
    sides = lax.axis_size("head")
    seq_bits = n_seq.bit_length() - 1
    seq_index = lax.axis_index("seq")
    size = head_count // 2

    weight = lax.all_gather(out_weight.T, "seq", axis=0, tiled=True)
    upper = (seq_index >> jnp.arange(seq_bits, dtype=jnp.int32)) & 1
    gain = norm_gain.reshape(1, -1)

    def send(block, bit):
        def wanted(s):
            above = s >> bit
            return not (bit == seq_bits - 1 and above & 1) and not (bit == seq_bits - 2 and above == 3)

        flip = 3 << bit - 1 if bit % 2 else 1 << bit
        return lax.ppermute(block, "seq", [(s, s ^ flip) for s in range(n_seq) if wanted(s)])

    small = size // 2
    early = 4

    def near(n, so_far, *after):
        return near_part(
            queries, keys, values, sums, cols, weights, levels, n * small, small, so_far, after
        )

    def first_levels(group, states, *after):
        return early_levels(upper, queries, close, weights, levels, states, group * size, after)

    a, came_a, b, came_b = [], [], [], []

    def go(blocks, came, *after):
        bit = len(blocks) - 1
        blocks.append(merged(bit, upper, blocks[bit], came[bit], after))
        came.append(send(blocks[-1], bit + 1))

    a.append(own_state(keys, values, log_decay, 0, size))
    came_a.append(send(a[0], 0))
    own_b = own_state(keys, values, log_decay, 1, size, (a[0],))
    sums, cols, weights = prepare(log_decay, level_weights, (own_b,))
    after_a, own_b = merged(0, upper, a[0], came_a[0], (weights,), own_b)
    a.append(after_a)
    came_a.append(send(a[1], 1))
    b.append(own_b)
    came_b.append(send(b[0], 0))
    close, token = near(0, None, b[0])
    go(a, came_a, token)
    go(b, came_b, a[2])
    close, token = near(1, close, b[1])
    go(a, came_a, token)
    go(b, came_b, a[3])
    close, token = near(2, close, b[2])
    go(a, came_a, token)
    go(b, came_b, a[4])
    close, token = near(3, close, b[3])
    far_a, before_a = first_levels(0, came_a[:early], token)
    go(a, came_a, before_a)
    go(b, came_b, a[5])
    far_b, before_b = first_levels(1, came_b[:early], b[4])
    a_hi, a_lo, token = finish(
        upper, queries, far_a, before_a, weights, levels, gain, came_a[early:], 0, after=(before_b,)
    )
    go(b, came_b, token, weight[:8, :CHUNK])

    me = lax.axis_index("head").astype(jnp.int32)
    both = jnp.stack([sides - 1 - me, me])
    to_send, to_keep = project(both, (0, 1), a_hi, a_lo, weight, 0, after=(b[5],))
    b_hi, b_lo, to_send = finish(
        upper, queries, far_b, before_b, weights, levels, gain, came_b[early:], size, both, weight, to_send
    )
    came = lax.ppermute(to_send, "head", [(s, sides - 1 - s) for s in range(sides)])
    [to_keep] = project(both, (1,), b_hi, b_lo, weight, 1, to_keep)
    return to_keep + came


def solution(mesh):
    return jax.shard_map(
        local,
        mesh=mesh,
        in_specs=(
            P("seq", "head"),
            P("seq", "head"),
            P("seq", "head"),
            P("head", "seq"),
            P("head", None, "seq"),
            P("head"),
            P("head", "seq"),
        ),
        out_specs=P("seq", "head"),
        check_vma=False,
    )
```
